32 devices in a mesh: dp: 8 (over z, core), ctx: 4 (over y, x).
Axes of the slice: x: 2, y: 2, z: 4, core: 2. Of those that a mesh axis runs over, the one named last changes fastest.
Arguments:
- tokens: bfloat16 [16, 1024, 2048], P('dp', 'ctx'), may hold values from -6 to 6
- span_order: int32 [16, 8], P('dp'), may hold values from 0 to 7, as said below
- out_grad: bfloat16 [16, 1024, 2048], P('dp', 'ctx'), may hold values from -6 to 6
- first_gain: bfloat16 [2048], P(('dp', 'ctx')), may hold values from 0.5 to 1.5
- query_weight: bfloat16 [2048, 2048], P(('dp', 'ctx')), may hold values from -0.125 to 0.125
- key_matrix: bfloat16 [2048, 512], P(('dp', 'ctx')), may hold values from -0.125 to 0.125
- value_matrix: bfloat16 [2048, 512], P(('dp', 'ctx')), may hold values from -0.125 to 0.125
- merge_weight: bfloat16 [2048, 2048], P(('dp', 'ctx')), may hold values from -2 to 2
- second_gain: bfloat16 [2048], P(('dp', 'ctx')), may hold values from 0.5 to 1.5
- gate_weight: bfloat16 [2048, 8192], P(('dp', 'ctx')), may hold values from -0.125 to 0.125
- up_weight: bfloat16 [2048, 8192], P(('dp', 'ctx')), may hold values from -0.125 to 0.125
- down_weight: bfloat16 [2048, 8192], P(('dp', 'ctx')), may hold values from -0.0625 to 0.0625
Outputs:
- block_output: bfloat16 [16, 1024, 2048], P('dp', 'ctx')
- input_grad: float32 [16, 1024, 2048], P('dp', 'ctx')
- first_gain_grad: float32 [2048], P(('dp', 'ctx'))
- query_grad: float32 [2048, 2048], P(('dp', 'ctx'))
- key_grad: float32 [2048, 512], P(('dp', 'ctx'))
- value_grad: float32 [2048, 512], P(('dp', 'ctx'))
- merge_grad: float32 [2048, 2048], P(('dp', 'ctx'))
- second_gain_grad: float32 [2048], P(('dp', 'ctx'))
- gate_grad: float32 [2048, 8192], P(('dp', 'ctx'))
- up_grad: float32 [2048, 8192], P(('dp', 'ctx'))
- down_grad: float32 [2048, 8192], P(('dp', 'ctx'))
The draws below stay inside these ranges and needn't reach their ends.
Inputs may be any that keep to these rules, and one draw needn't show every extreme that they name: `span_order`: each row lists every span number 0 to 7 once; slots 2 c and 2 c + 1 hold spans j and 7 - j for some j, in either order.
All inputs are finite; a program needn't handle non-finite values.
Results may differ from the reference program's by a relative error of at most 0.014.
Values may be sent and summed in bfloat16 or wider, within the bound.
A program may use at most 768 MiB of HBM per device.

```python
import math
import jax
import jax.numpy as jnp
from jax import lax

MODEL_WIDTH = 2048
HQ = 32
KEY_VALUE_HEADS = 8
HEAD_SIZE = 64
FF = 8192
SEQ_LEN = 1024
SEQS = 16
N_CTX = 4


def draw_span_order(key, part):
    key = jax.random.fold_in(key, 11)

    def one_row(row_key):
        perm_key, flip_key = jax.random.split(row_key)
        low_half = jax.random.permutation(perm_key, N_CTX).astype(jnp.int32)
        flip_bits = jax.random.randint(flip_key, (N_CTX,), 0, 2)
        high_half = 2 * N_CTX - 1 - low_half
        leading = jnp.where(flip_bits == 1, high_half, low_half)
        trailing = jnp.where(flip_bits == 1, low_half, high_half)
        return jnp.stack([leading, trailing], axis=1).reshape(2 * N_CTX).astype(jnp.int32)
    return jax.vmap(one_row)(jax.random.split(key, SEQS))


def shard_levels(rng, extent, shards, smallest, top_value):
    level, own = 1.0, jax.random.fold_in(rng, 6)
    for axis_at, shards_of in shards:
        draws = jnp.exp(jax.random.uniform(jax.random.fold_in(own, axis_at), (shards_of,), jnp.float32, smallest / len(shards), top_value / len(shards)))
        level = level * jnp.repeat(draws, extent[axis_at] // shards_of).reshape([-1 if axis == axis_at else 1 for axis in range(len(extent))])
    return level


def centred(own_key, dims, width, limit, pieces=(), held_as=jnp.bfloat16):
    values = width * jax.random.normal(own_key, dims, jnp.float32)
    if pieces:
        values = values * shard_levels(own_key, dims, pieces, -0.22, 0.18)
    return jnp.clip(values, -limit, limit).astype(held_as)


def setup_inputs(seed: int = 0) -> dict:
    splits = jax.random.split(jax.random.key(seed), 13)
    return {
        "tokens": centred(splits[0], (SEQS, SEQ_LEN, MODEL_WIDTH), 1.0, 6.0, ((0, 8), (1, 4))),
        "span_order": draw_span_order(jax.random.fold_in(splits[12], 71), 0),
        "out_grad": centred(splits[2], (SEQS, SEQ_LEN, MODEL_WIDTH), 1.0, 6.0, ((0, 8), (1, 4))),
        "first_gain": jnp.clip(1.0 + 0.1 * jax.random.normal(splits[3], (MODEL_WIDTH,), jnp.float32), 0.5, 1.5).astype(jnp.bfloat16),
        "query_weight": centred(splits[4], (MODEL_WIDTH, HQ * HEAD_SIZE), MODEL_WIDTH ** -0.5, 0.125, ((0, 32),)),
        "key_matrix": centred(splits[5], (MODEL_WIDTH, KEY_VALUE_HEADS * HEAD_SIZE), MODEL_WIDTH ** -0.5, 0.125, ((0, 32),)),
        "value_matrix": centred(splits[6], (MODEL_WIDTH, KEY_VALUE_HEADS * HEAD_SIZE), MODEL_WIDTH ** -0.5, 0.125, ((0, 32),)),
        "merge_weight": centred(splits[7], (MODEL_WIDTH, HQ * HEAD_SIZE), (max(HQ * HEAD_SIZE // 256, 4)) ** -0.5, 2.0, ((0, 32),)),
        "second_gain": jnp.clip(1.0 + 0.1 * jax.random.normal(splits[8], (MODEL_WIDTH,), jnp.float32), 0.5, 1.5).astype(jnp.bfloat16),
        "gate_weight": centred(splits[9], (MODEL_WIDTH, FF), MODEL_WIDTH ** -0.5, 0.125, ((0, 32),)),
        "up_weight": centred(splits[10], (MODEL_WIDTH, FF), MODEL_WIDTH ** -0.5, 0.125, ((0, 32),)),
        "down_weight": centred(splits[11], (MODEL_WIDTH, FF), FF ** -0.5, 0.0625, ((0, 32),)),
    }


@jax.custom_vjp
def low(v):
    return lax.optimization_barrier(v.astype(jnp.bfloat16)).astype(jnp.float32)

@jax.custom_vjp
def low_back(v):
    return v

def low_keep(v):
    return (low(v), None)

def low_pass(kept, grad):
    return (grad,)

def back_keep(v):
    return (v, None)

def back_low(kept, grad):
    return (low(grad),)
low.defvjp(low_keep, low_pass)
low_back.defvjp(back_keep, back_low)
EPS = 1e-05
THETA = 500000.0
HIGHEST = lax.Precision.HIGHEST

def matmul(left, right):
    return jnp.dot(left, right, precision=HIGHEST, preferred_element_type=jnp.float32)

def rope_tables(positions):
    half_dim = HEAD_SIZE // 2
    frequency = jnp.exp(jnp.arange(half_dim, dtype=jnp.float32) * (-2.0 * math.log(THETA) / HEAD_SIZE))
    angles = positions.astype(jnp.float32)[:, None] * frequency[None, :]
    return (jnp.cos(angles)[:, None, :], jnp.sin(angles)[:, None, :])

def rotate(head_rows, cos_table, sin_table):
    half_dim = head_rows.shape[-1] // 2
    leading = head_rows[..., :half_dim]
    trailing = head_rows[..., half_dim:]
    return jnp.concatenate([leading * cos_table - trailing * sin_table, trailing * cos_table + leading * sin_table], axis=-1)

def rms_norm(values, gain_vec):
    inverse_rms = lax.rsqrt(lax.optimization_barrier(jnp.mean(values * values, axis=-1, keepdims=True)) + EPS)
    return values * inverse_rms * gain_vec

def attention(queries, keys_rot, values_in, allowed):
    seq_total = queries.shape[0]
    kv_heads = keys_rot.shape[1]
    query_groups = queries.reshape(seq_total, kv_heads, -1, HEAD_SIZE).transpose(1, 2, 0, 3)
    key_groups = keys_rot.transpose(1, 0, 2)
    value_groups = values_in.transpose(1, 0, 2)

    def head_block(operands):
        query_head, key_head, value_head = operands
        scores = jnp.einsum('gqd,kd->gqk', query_head, key_head, precision=HIGHEST) * HEAD_SIZE ** (-0.5)
        scores = low_back(scores)
        masked = jnp.where(allowed[None], scores, -1e+30)
        weights_soft = jax.nn.softmax(masked, axis=-1)
        return jnp.einsum('gqk,kd->gqd', low(weights_soft), value_head, precision=HIGHEST)
    attended = lax.map(jax.checkpoint(head_block), (query_groups, key_groups, value_groups))
    return attended.transpose(2, 0, 1, 3).reshape(seq_total, -1)

def layer(inputs, positions, first_gain, query_weight, key_matrix, value_matrix, merge_weight, second_gain, gate_weight, up_weight, down_weight):
    seq_total = inputs.shape[0]
    cos_table, sin_table = rope_tables(positions)
    allowed = positions[:, None] >= positions[None, :]
    attn_in = low(rms_norm(inputs, first_gain))
    query_pre = low_back(matmul(attn_in, query_weight))
    queries = low(rotate(query_pre.reshape(seq_total, -1, HEAD_SIZE), cos_table, sin_table))
    key_pre = low_back(matmul(attn_in, key_matrix))
    keys_rot = low(rotate(key_pre.reshape(seq_total, -1, HEAD_SIZE), cos_table, sin_table))
    values_in = low(low_back(matmul(attn_in, value_matrix))).reshape(seq_total, -1, HEAD_SIZE)
    attn_out = low(low_back(attention(queries, keys_rot, values_in, allowed)))
    branch_one = low_back(matmul(attn_out, merge_weight.T))
    hidden_one = inputs + branch_one
    feed_in = low(rms_norm(hidden_one, second_gain))
    gate_pre = low_back(matmul(feed_in, gate_weight))
    up_pre = low_back(matmul(feed_in, up_weight))
    activated = low(jax.nn.silu(gate_pre) * up_pre)
    branch_two = low_back(matmul(activated, down_weight.T))
    return hidden_one + branch_two

def reference(tokens, span_order, out_grad, first_gain, query_weight, key_matrix, value_matrix, merge_weight, second_gain, gate_weight, up_weight, down_weight):
    weights = jax.tree.map(lambda array_in: array_in.astype(jnp.float32), (first_gain, query_weight, key_matrix, value_matrix, merge_weight, second_gain, gate_weight, up_weight, down_weight))
    span_len = SEQ_LEN // (2 * N_CTX)
    offsets = jnp.arange(SEQ_LEN, dtype=jnp.int32) % span_len
    slot_ids = jnp.arange(SEQ_LEN, dtype=jnp.int32) // span_len

    def per_sequence(running, operands):
        inputs, ordering_row, cotangent = operands
        positions = (ordering_row[slot_ids] * span_len + offsets).astype(jnp.int32)

        def forward(inputs_in, *params):
            return layer(inputs_in, positions, *params)
        result, pullback = jax.vjp(forward, inputs, *weights)
        updates = pullback(cotangent)
        running = tuple((before + update for before, update in zip(running, updates[1:])))
        return (running, (result.astype(jnp.bfloat16), updates[0]))
    initial = tuple((jnp.zeros_like(weight_arr) for weight_arr in weights))
    total_counts, (blocks, input_grads) = lax.scan(per_sequence, initial, (tokens.astype(jnp.float32), span_order, out_grad.astype(jnp.float32)))
    return (blocks, input_grads, total_counts[0], total_counts[1], total_counts[2], total_counts[3], total_counts[4], total_counts[5], total_counts[6], total_counts[7], total_counts[8])
```

```python
import functools
import math

import jax
import jax.numpy as jnp
from jax import lax
from jax.experimental import pallas as pl
from jax.experimental.pallas import tpu as pltpu
from jax.sharding import PartitionSpec as P

HEAD_SIZE = 64
LANES = 128
EPS = 1e-05
THETA = 500000.0
QUERY_BLOCK = 256
F32 = jnp.float32
BF16 = jnp.bfloat16

NN = (((1,), (0,)), ((), ()))
NT = (((1,), (1,)), ((), ()))
TN = (((0,), (0,)), ((), ()))


def dot(left, right, dims=NN, out=F32):
    return lax.dot_general(left, right, dims, preferred_element_type=F32).astype(out)


def swap(block, bits):
    size = lax.axis_size("ctx")
    return lax.ppermute(block, "ctx", [(i, i ^ bits) for i in range(size)])


def square():
    return lax.axis_size("ctx") == 4


def gather_rows(own):
    if not square():
        return lax.all_gather(own, "ctx", axis=0, tiled=True)
    half = own.shape[0] // 2
    from_one, from_two = swap(own, 1), swap(own, 2)
    across_low = swap(from_one[:half], 2)
    across_high = swap(from_two[half:], 1)
    return jnp.concatenate([own, from_one, from_two, across_low, across_high], axis=0)


def scatter_rows(parts):
    if not square():
        return lax.psum_scatter(parts, "ctx", scatter_dimension=0, tiled=True).astype(F32)
    rows = parts.shape[0] // 4
    half = rows // 2
    block = parts.reshape(4, rows, -1)
    low = swap(block[3, :half], 1)
    high = swap(block[3, half:], 2)
    for_one = jnp.concatenate(
        [block[1, :half], (block[1, half:].astype(F32) + high.astype(F32)).astype(BF16)], axis=0
    )
    for_two = jnp.concatenate(
        [(block[2, :half].astype(F32) + low.astype(F32)).astype(BF16), block[2, half:]], axis=0
    )
    return (
        block[0].astype(F32) + swap(for_one, 1).astype(F32) + swap(for_two, 2).astype(F32)
    )


def exchange(block_for):
    size = lax.axis_size("ctx")
    rank = lax.axis_index("ctx")
    if not square():
        stacked = jnp.stack([block_for(t) for t in range(size)])
        return lax.all_to_all(stacked, "ctx", 0, 0)
    received = [block_for(rank)] + [swap(block_for(rank ^ m), m) for m in (1, 2, 3)]
    out = jnp.zeros((4,) + received[0].shape, received[0].dtype)
    for member, value in enumerate(received):
        out = lax.dynamic_update_index_in_dim(out, value, rank ^ member, 0)
    return out


def gather_columns(block_for):
    mine = exchange(block_for)
    mine = mine.reshape(-1, mine.shape[-1])
    return lax.all_gather(mine, "dp", axis=0, tiled=True)


def scatter_columns(grads):
    size = lax.axis_size("ctx")
    summed = lax.psum_scatter(grads, "dp", scatter_dimension=0, tiled=True)
    rows = summed.shape[0] // size
    return exchange(lambda t: lax.dynamic_slice_in_dim(summed, t * rows, rows, axis=0))


def swap_halves(rows):
    lane = lax.broadcasted_iota(jnp.int32, rows.shape, 1)
    return jnp.where(
        lane % HEAD_SIZE < HEAD_SIZE // 2,
        pltpu.roll(rows, LANES - HEAD_SIZE // 2, 1),
        pltpu.roll(rows, HEAD_SIZE // 2, 1),
    )


def both_halves(rows, half):
    lane = lax.broadcasted_iota(jnp.int32, rows.shape, 1)
    kept = jnp.where(lane // HEAD_SIZE == half, rows.astype(F32), 0.0)
    return (kept + pltpu.roll(kept, HEAD_SIZE, 1)).astype(BF16)


def two_heads(rows):
    lane = lax.broadcasted_iota(jnp.int32, rows.shape, 1)
    wide = rows.astype(F32)
    first = jnp.where(lane < HEAD_SIZE, wide, 0.0)
    second = jnp.where(lane < HEAD_SIZE, 0.0, wide)
    return jnp.concatenate([first, second], axis=0).astype(BF16)


def visible(size):
    key = lax.broadcasted_iota(jnp.int32, (size, 2 * size), 0)
    query = lax.broadcasted_iota(jnp.int32, (size, 2 * size), 1) % size
    return key <= query


def attention_forward_kernel(
    slot_ref, q_ref, k_ref, v_ref, cos_ref, sin_ref,
    out_ref, queries_ref, keys_ref, values_ref, total_ref, key_both, value_turned,
    *, span, pairs_of_head, pairs_of_block
):
    pair = pl.program_id(0)
    length = q_ref.shape[0]
    spans = length // span
    block = QUERY_BLOCK

    def place(index):
        return pl.ds(pl.multiple_of(slot_ref[index] * span, span), span)

    def turned(source, index):
        here = slice(index * span, (index + 1) * span)
        rows = source[place(index), :]
        return rows * cos_ref[here, :] + swap_halves(rows) * sin_ref[here, :]

    for index in range(spans):
        here = slice(index * span, (index + 1) * span)
        queries_ref[here, :] = turned(q_ref, index).astype(BF16)

    @pl.when(pair % pairs_of_block == 0)
    def _():
        for index in range(spans):
            here = slice(index * span, (index + 1) * span)
            keys_ref[here, :] = turned(k_ref, index).astype(BF16)
            values_ref[here, :] = v_ref[place(index), :].astype(BF16)

    @pl.when(pair % pairs_of_head == 0)
    def _():
        half = (pair // pairs_of_head) % 2
        key_both[...] = both_halves(keys_ref[...], half)
        value_both = both_halves(values_ref[...], half)
        value_turned[...] = value_both.astype(F32).T[:HEAD_SIZE].astype(BF16)

    mask = visible(block)
    for index in range(length // block):
        low, high = index * block, (index + 1) * block
        wide = two_heads(queries_ref[low:high, :] * jnp.asarray(HEAD_SIZE**-0.5, BF16))
        diagonal = jnp.where(mask, dot(key_both[low:high, :], wide, NT), -1e30)
        top = jnp.max(diagonal, axis=0, keepdims=True)
        if index:
            before = dot(key_both[:low, :], wide, NT)
            top = jnp.maximum(top, jnp.max(before, axis=0, keepdims=True))
        near = jnp.exp(diagonal - top)
        total = jnp.sum(near, axis=0, keepdims=True)
        attended = dot(value_turned[:, low:high], near.astype(BF16))
        if index:
            far = jnp.exp(before - top)
            total = total + jnp.sum(far, axis=0, keepdims=True)
            attended = attended + dot(value_turned[:, :low], far.astype(BF16))
        total_ref[0, index : index + 1, :] = top + jnp.log(total)
        attended = attended / total
        rows = jnp.concatenate([attended[:, :block], attended[:, block:]], axis=0).T.astype(BF16)
        for part in range(block // span):
            out_ref[place(index * (block // span) + part), :] = rows[
                part * span : (part + 1) * span
            ]


def attention_backward_kernel(
    slot_ref, queries_ref, keys_ref, values_ref, total_ref, grad_ref, cos_ref, sin_ref,
    grad_q_ref, grad_k_ref, grad_v_ref, key_both, value_both, key_turned, key_sum, value_sum,
    *, span, pairs_of_head
):
    pair = pl.program_id(0)
    length = queries_ref.shape[0]
    spans = length // span
    block = QUERY_BLOCK
    each = block // span
    half = (pair // pairs_of_head) % 2

    def place(index):
        return pl.ds(pl.multiple_of(slot_ref[index] * span, span), span)

    def turned_back(rows, index):
        here = slice(index * span, (index + 1) * span)
        return rows * cos_ref[here, :] - swap_halves(rows) * sin_ref[here, :]

    @pl.when(pair % pairs_of_head == 0)
    def _():
        key_both[...] = both_halves(keys_ref[...], half)
        value_both[...] = both_halves(values_ref[...], half)
        key_turned[...] = key_both[...].astype(F32).T[:HEAD_SIZE].astype(BF16)
        key_sum[...] = jnp.zeros_like(key_sum)
        value_sum[...] = jnp.zeros_like(value_sum)

    mask = visible(block)
    for index in range(length // block):
        low, high = index * block, (index + 1) * block
        wide = two_heads(queries_ref[low:high, :] * jnp.asarray(HEAD_SIZE**-0.5, BF16))
        grad = two_heads(
            jnp.concatenate(
                [grad_ref[place(index * each + part), :] for part in range(each)], axis=0
            )
        )
        total = total_ref[0, index : index + 1, :]
        ranges = [(low, high)] + ([(0, low)] if index else [])
        probs, grad_probs, row_dot = [], [], 0.0
        for start, stop in ranges:
            scores = dot(key_both[start:stop, :], wide, NT)
            if start == low:
                scores = jnp.where(mask, scores, -1e30)
            prob = jnp.exp(scores - total)
            grad_prob = dot(value_both[start:stop, :], grad, NT)
            row_dot = row_dot + jnp.sum(prob * grad_prob, axis=0, keepdims=True)
            probs.append(prob)
            grad_probs.append(grad_prob)
        turned = 0.0
        for (start, stop), prob, grad_prob in zip(ranges, probs, grad_probs):
            grad_score = (prob * (grad_prob - row_dot)).astype(BF16)
            value_sum[start:stop, :] += dot(prob.astype(BF16), grad)
            key_sum[start:stop, :] += dot(grad_score, wide)
            turned = turned + dot(key_turned[:, start:stop], grad_score)
        turned = turned * HEAD_SIZE**-0.5
        rows = jnp.concatenate([turned[:, :block], turned[:, block:]], axis=0).T
        for part in range(each):
            at = index * each + part
            grad_q_ref[place(at), :] = turned_back(
                rows[part * span : (part + 1) * span], at
            ).astype(BF16)

    @pl.when(pair % pairs_of_head == pairs_of_head - 1)
    def _():
        for index in range(spans):
            here = slice(index * span, (index + 1) * span)
            key_rows, value_rows = key_sum[here, :], value_sum[here, :]
            key_rows = turned_back(key_rows + pltpu.roll(key_rows, HEAD_SIZE, 1), index)
            value_rows = value_rows + pltpu.roll(value_rows, HEAD_SIZE, 1)
            lane = lax.broadcasted_iota(jnp.int32, key_rows.shape, 1)
            for target, rows in ((grad_k_ref, key_rows), (grad_v_ref, value_rows)):
                old = target[place(index), :].astype(F32)
                keep = (lane < HEAD_SIZE) & (half == 1)
                target[place(index), :] = jnp.where(keep, old, rows).astype(BF16)


def attention_sizes(query_width, group_size):
    pairs = query_width // LANES
    pairs_of_head = group_size // 2
    return pairs, pairs_of_head, 2 * pairs_of_head


def attention_forward(qkv, slots, cos_lanes, sin_lanes, query_width, key_width, group_size):
    length = qkv.shape[0]
    pairs, pairs_of_head, pairs_of_block = attention_sizes(query_width, group_size)
    key_at, value_at = query_width // LANES, (query_width + key_width) // LANES
    tile = (length, LANES)
    by_pair = pl.BlockSpec(tile, lambda p, s: (0, p))
    by_block = pl.BlockSpec(tile, lambda p, s: (0, p // pairs_of_block))
    whole = pl.BlockSpec(tile, lambda p, s: (0, 0))
    blocks = length // QUERY_BLOCK
    work = 2 * query_width * length * length
    return pl.pallas_call(
        functools.partial(
            attention_forward_kernel,
            span=length // slots.shape[0],
            pairs_of_head=pairs_of_head,
            pairs_of_block=pairs_of_block,
        ),
        grid_spec=pltpu.PrefetchScalarGridSpec(
            num_scalar_prefetch=1,
            grid=(pairs,),
            in_specs=[
                by_pair,
                pl.BlockSpec(tile, lambda p, s: (0, key_at + p // pairs_of_block)),
                pl.BlockSpec(tile, lambda p, s: (0, value_at + p // pairs_of_block)),
                whole,
                whole,
            ],
            out_specs=[
                by_pair,
                by_pair,
                by_block,
                by_block,
                pl.BlockSpec((1, blocks, 2 * QUERY_BLOCK), lambda p, s: (p, 0, 0)),
            ],
            scratch_shapes=[pltpu.VMEM(tile, BF16), pltpu.VMEM((HEAD_SIZE, length), BF16)],
        ),
        out_shape=[
            jax.ShapeDtypeStruct((length, query_width), BF16),
            jax.ShapeDtypeStruct((length, query_width), BF16),
            jax.ShapeDtypeStruct((length, key_width), BF16),
            jax.ShapeDtypeStruct((length, key_width), BF16),
            jax.ShapeDtypeStruct((pairs, blocks, 2 * QUERY_BLOCK), F32),
        ],
        compiler_params=pltpu.CompilerParams(
            dimension_semantics=("arbitrary",), vmem_limit_bytes=48 << 20
        ),
        cost_estimate=pl.CostEstimate(
            flops=8 * work, bytes_accessed=8 << 20, transcendentals=work // 128
        ),
        name="attention_forward",
    )(slots, qkv, qkv, qkv, cos_lanes, sin_lanes)


def attention_backward(kept, grad, slots, cos_lanes, sin_lanes, group_size):
    queries, keys, values, totals = kept
    length, query_width = queries.shape
    key_width = keys.shape[1]
    pairs, pairs_of_head, pairs_of_block = attention_sizes(query_width, group_size)
    tile = (length, LANES)
    by_pair = pl.BlockSpec(tile, lambda p, s: (0, p))
    by_block = pl.BlockSpec(tile, lambda p, s: (0, p // pairs_of_block))
    whole = pl.BlockSpec(tile, lambda p, s: (0, 0))
    blocks = length // QUERY_BLOCK
    work = 2 * query_width * length * length
    return pl.pallas_call(
        functools.partial(
            attention_backward_kernel, span=length // slots.shape[0], pairs_of_head=pairs_of_head
        ),
        grid_spec=pltpu.PrefetchScalarGridSpec(
            num_scalar_prefetch=1,
            grid=(pairs,),
            in_specs=[
                by_pair,
                by_block,
                by_block,
                pl.BlockSpec((1, blocks, 2 * QUERY_BLOCK), lambda p, s: (p, 0, 0)),
                by_pair,
                whole,
                whole,
            ],
            out_specs=[by_pair, by_block, by_block],
            scratch_shapes=[
                pltpu.VMEM(tile, BF16),
                pltpu.VMEM(tile, BF16),
                pltpu.VMEM((HEAD_SIZE, length), BF16),
                pltpu.VMEM(tile, F32),
                pltpu.VMEM(tile, F32),
            ],
        ),
        out_shape=[
            jax.ShapeDtypeStruct((length, query_width), BF16),
            jax.ShapeDtypeStruct((length, key_width), BF16),
            jax.ShapeDtypeStruct((length, key_width), BF16),
        ],
        compiler_params=pltpu.CompilerParams(
            dimension_semantics=("arbitrary",), vmem_limit_bytes=48 << 20
        ),
        cost_estimate=pl.CostEstimate(
            flops=20 * work, bytes_accessed=8 << 20, transcendentals=work // 128
        ),
        name="attention_backward",
    )(slots, queries, keys, values, totals, grad, cos_lanes, sin_lanes)


def feed_kernel(feed_ref, down_in_ref, pair_ref, down_ref, activated_ref, grads_ref):
    tile = down_ref.shape[1]
    both = dot(feed_ref[...], pair_ref[...])
    grad_act = dot(down_in_ref[...], down_ref[...])
    gate, up = both[:, :tile], both[:, tile:]
    sig = jax.nn.sigmoid(gate)
    silu = gate * sig
    activated_ref[...] = (silu * up).astype(BF16)
    grads_ref[:, :tile] = (grad_act * up * sig * (1.0 + gate * (1.0 - sig))).astype(BF16)
    grads_ref[:, tile:] = (grad_act * silu).astype(BF16)


def feed_middle(feed_in, down_in, weights, width, tile):
    rows, depth = feed_in.shape
    tiles = width // tile
    work = rows * depth * width
    return pl.pallas_call(
        feed_kernel,
        grid=(tiles,),
        in_specs=[
            pl.BlockSpec((rows, depth), lambda j: (0, 0), pipeline_mode=pl.Buffered(1)),
            pl.BlockSpec((rows, depth), lambda j: (0, 0), pipeline_mode=pl.Buffered(1)),
            pl.BlockSpec((depth, 2 * tile), lambda j: (0, j)),
            pl.BlockSpec((depth, tile), lambda j: (0, 2 * tiles + j)),
        ],
        out_specs=[
            pl.BlockSpec((rows, tile), lambda j: (0, j)),
            pl.BlockSpec((rows, 2 * tile), lambda j: (0, j)),
        ],
        out_shape=[
            jax.ShapeDtypeStruct((rows, width), BF16),
            jax.ShapeDtypeStruct((rows, 2 * width), BF16),
        ],
        compiler_params=pltpu.CompilerParams(
            dimension_semantics=("arbitrary",), vmem_limit_bytes=56 << 20
        ),
        cost_estimate=pl.CostEstimate(
            flops=6 * work,
            bytes_accessed=2 * (2 * rows * depth + 3 * depth * width + 3 * rows * width),
            transcendentals=rows * width,
        ),
        name="feed_middle",
    )(feed_in, down_in, weights, weights)


def norm_forward(values):
    inverse_rms = lax.rsqrt(jnp.mean(values * values, axis=-1, keepdims=True) + EPS)
    return (values * inverse_rms, inverse_rms)


def norm_backward(grad_normed, normed, inverse_rms, gain):
    grad_hat = grad_normed * gain
    grad_input = inverse_rms * (
        grad_hat - normed * jnp.mean(grad_hat * normed, axis=-1, keepdims=True)
    )
    return (grad_input, jnp.sum(grad_normed * normed, axis=0))


def rope_lanes(length):
    half = HEAD_SIZE // 2
    frequency = jnp.exp(
        jnp.arange(half, dtype=F32) * (-2.0 * math.log(THETA) / HEAD_SIZE)
    )
    angles = jnp.arange(length, dtype=jnp.int32).astype(F32)[:, None] * frequency[None, :]
    cosine, sine = jnp.cos(angles), jnp.sin(angles)
    return (
        jnp.concatenate([cosine] * 4, axis=1),
        jnp.concatenate([-sine, sine, -sine, sine], axis=1),
    )


def pad_columns(array, width):
    return jnp.pad(array, ((0, 0), (0, width - array.shape[1])))


def body(
    tokens, span_order, out_grad, first_gain, query_weight, key_matrix, value_matrix,
    merge_weight, second_gain, gate_weight, up_weight, down_weight,
):
    seqs, own_rows, depth = tokens.shape
    ctx = lax.axis_size("ctx")
    rank = lax.axis_index("ctx")
    length = own_rows * ctx
    spans = span_order.shape[1]
    weight_rows = gate_weight.shape[0]
    group_size = query_weight.shape[1] // key_matrix.shape[1]
    query_width = query_weight.shape[1] // ctx
    own_key_width = key_matrix.shape[1] // ctx
    key_width = -(-own_key_width // LANES) * LANES
    feed_width = gate_weight.shape[1] // ctx
    chunks = 2
    chunk = feed_width // chunks
    tile = min(512, chunk)

    def columns(weight, t, width, at=0):
        return lax.dynamic_slice_in_dim(weight, t * (weight.shape[1] // ctx) + at, width, axis=1)

    gain_columns = pad_columns(jnp.stack([first_gain, second_gain], axis=1), LANES)

    def projections_for(t):
        return jnp.concatenate(
            [
                columns(query_weight, t, query_width),
                pad_columns(columns(key_matrix, t, own_key_width), key_width),
                pad_columns(columns(value_matrix, t, own_key_width), key_width),
                gain_columns,
            ],
            axis=1,
        )

    def feed_for(part):
        def of(t):
            pieces = []
            for start in range(part * chunk, (part + 1) * chunk, tile):
                pieces += [
                    columns(gate_weight, t, tile, start),
                    columns(up_weight, t, tile, start),
                ]
            pieces.append(columns(down_weight, t, chunk, part * chunk))
            return jnp.concatenate(pieces, axis=1)

        return of

    projections = gather_columns(projections_for)
    merge = gather_columns(lambda t: columns(merge_weight, t, query_width))
    feeds = [gather_columns(feed_for(part)) for part in range(chunks)]

    qkv_width = query_width + 2 * key_width
    qkv_weight = projections[:, :qkv_width]
    gains = projections[:, qkv_width : qkv_width + 2].astype(F32)
    gain_one, gain_two = gains[:, 0], gains[:, 1]

    slots = jnp.argsort(span_order, axis=1).astype(jnp.int32)
    if square():
        slots = ((slots // 2) ^ rank) * 2 + slots % 2
    cos_lanes, sin_lanes = rope_lanes(length)

    inputs = [tokens[s].astype(F32) for s in range(seqs)]
    normed_one, inverse_one, attn_in = [], [], []
    for s in range(seqs):
        normed, inverse = norm_forward(inputs[s])
        normed_one.append(normed)
        inverse_one.append(inverse)
        attn_in.append(gather_rows((normed * gain_one).astype(BF16)))
    down_in = [gather_rows(out_grad[s]) for s in range(seqs)]
    attn_out, kept, hidden_one = [], [], []
    for s in range(seqs):
        qkv = dot(attn_in[s], qkv_weight)
        attended, *rest = attention_forward(
            qkv, slots[s], cos_lanes, sin_lanes, query_width, key_width, group_size
        )
        attn_out.append(attended)
        kept.append(rest)
        hidden_one.append(inputs[s] + scatter_rows(dot(attended, merge, NT, BF16)))

    normed_two, inverse_two, feed_in = [], [], []
    for s in range(seqs):
        normed, inverse = norm_forward(hidden_one[s])
        normed_two.append(normed)
        inverse_two.append(inverse)
        feed_in.append(gather_rows((normed * gain_two).astype(BF16)))
    middle = [
        [feed_middle(feed_in[s], down_in[s], feeds[part], chunk, tile) for part in range(chunks)]
        for s in range(seqs)
    ]
    blocks, grad_hidden, merge_in, gain_two_sum = [], [], [], 0.0
    for s in range(seqs):
        grad_feed_in = sum(
            dot(middle[s][part][1], feeds[part][:, : 2 * chunk], NT) for part in range(chunks)
        )
        grad_middle, gain_part = norm_backward(
            scatter_rows(grad_feed_in.astype(BF16)), normed_two[s], inverse_two[s], gain_two
        )
        gain_two_sum = gain_two_sum + gain_part
        grad_hidden.append(out_grad[s].astype(F32) + grad_middle)
        merge_in.append(gather_rows(grad_hidden[s].astype(BF16)))
    feed_tokens = jnp.concatenate(feed_in, axis=0)
    down_tokens = jnp.concatenate(down_in, axis=0)
    feed_sums = []
    for part in range(chunks):
        activated = jnp.concatenate([middle[s][part][0] for s in range(seqs)], axis=0)
        grads = jnp.concatenate([middle[s][part][1] for s in range(seqs)], axis=0)
        grads = jnp.concatenate(
            [dot(feed_tokens, grads, TN, BF16), dot(down_tokens, activated, TN, BF16)], axis=1
        )
        feed_sums.append(scatter_columns(grads))
    for s in range(seqs):
        branch = sum(
            dot(middle[s][part][0], feeds[part][:, 2 * chunk :], NT) for part in range(chunks)
        )
        blocks.append((hidden_one[s] + scatter_rows(branch.astype(BF16))).astype(BF16))

    grad_qkv, input_grad, gain_one_sum = [], [], 0.0
    for s in range(seqs):
        grad_attn = dot(merge_in[s], merge, NN, BF16)
        parts = attention_backward(
            kept[s], grad_attn, slots[s], cos_lanes, sin_lanes, group_size
        )
        grad_qkv.append(jnp.concatenate(parts, axis=1))
        grad_lower, gain_part = norm_backward(
            scatter_rows(dot(grad_qkv[s], qkv_weight, NT, BF16)),
            normed_one[s],
            inverse_one[s],
            gain_one,
        )
        gain_one_sum = gain_one_sum + gain_part
        input_grad.append(grad_hidden[s] + grad_lower)
    attention_grads = jnp.concatenate(
        [
            dot(jnp.concatenate(attn_in, axis=0), jnp.concatenate(grad_qkv, axis=0), TN, BF16),
            dot(jnp.concatenate(merge_in, axis=0), jnp.concatenate(attn_out, axis=0), TN, BF16),
            pad_columns(jnp.stack([gain_one_sum, gain_two_sum], axis=1).astype(BF16), LANES),
        ],
        axis=1,
    )
    attention_sums = scatter_columns(attention_grads)

    def spread(pieces):
        return pieces.astype(F32).transpose(1, 0, 2).reshape(pieces.shape[1], -1)

    def of_feed(kind):
        pieces = []
        for part in range(chunks):
            for at in range(chunk // tile):
                start = 2 * chunk + at * tile if kind == 2 else (2 * at + kind) * tile
                pieces.append(feed_sums[part][:, :, start : start + tile])
        return spread(jnp.concatenate(pieces, axis=2))

    key_at, value_at = query_width, query_width + key_width
    merge_at, gain_at = qkv_width, qkv_width + query_width
    gain_totals = jnp.sum(attention_sums[:, :, gain_at : gain_at + 2].astype(F32), axis=0)
    return (
        jnp.stack(blocks),
        jnp.stack(input_grad),
        gain_totals[:, 0],
        spread(attention_sums[:, :, :query_width]),
        spread(attention_sums[:, :, key_at : key_at + own_key_width]),
        spread(attention_sums[:, :, value_at : value_at + own_key_width]),
        spread(attention_sums[:, :, merge_at : merge_at + query_width]),
        gain_totals[:, 1],
        of_feed(0),
        of_feed(1),
        of_feed(2),
    )


def solution(mesh):
    rows = P(("dp", "ctx"), None)
    vector = P(("dp", "ctx"))
    acts = P("dp", "ctx", None)
    in_specs = (
        acts, P("dp", None), acts, vector, rows, rows, rows, rows, vector, rows, rows, rows,
    )
    out_specs = (acts, acts, vector, rows, rows, rows, rows, vector, rows, rows, rows)
    return jax.shard_map(body, mesh=mesh, in_specs=in_specs, out_specs=out_specs, check_vma=False)
```

```python
import functools
import math

import jax
import jax.numpy as jnp
from jax import lax
from jax.experimental import pallas as pl
from jax.experimental.pallas import tpu as pltpu
from jax.sharding import PartitionSpec as P

HEAD_SIZE = 64
LANES = 128
EPS = 1e-05
THETA = 500000.0
QUERY_BLOCK = 256
F32 = jnp.float32
BF16 = jnp.bfloat16

NN = (((1,), (0,)), ((), ()))
NT = (((1,), (1,)), ((), ()))
TN = (((0,), (0,)), ((), ()))


def dot(left, right, dims=NN, out=F32):
    return lax.dot_general(left, right, dims, preferred_element_type=F32).astype(out)


class Chain:
    def __init__(self):
        self.last = ()

    def after(self, values):
        values = tuple(values)
        if not self.last:
            return values
        return lax.optimization_barrier(values + self.last)[: len(values)]

    def run(self, function, *args):
        leaves, tree = jax.tree.flatten(args)
        out = function(*jax.tree.unflatten(tree, self.after(leaves)))
        self.last = tuple(jax.tree.leaves(out))
        return out

    def wait(self, *arrays):
        self.last = self.last + arrays


    def send(self, *sends):
        blocks = self.after(block for block, _ in sends)
        return [
            lax.ppermute(block, "ctx", [(i, i ^ bits) for i in range(4)])
            for block, (_, bits) in zip(blocks, sends)
        ]

    def gather_near(self, own):
        return self.send((own, 1), (own, 2)) if square() else []

    def gather_far(self, near):
        if not square():
            return []
        self.wait(*near)
        half = near[0].shape[0] // 2
        one, two = self.after(near)
        return self.send((one[:half], 2), (two[half:], 1))

    def gathered(self, own, near, far):
        if not square():
            return lax.all_gather(own, "ctx", axis=0, tiled=True)
        self.wait(*far)
        return jnp.concatenate([own, *near, *far], axis=0)

    def scatter_near(self, parts):
        if not square():
            return []
        across = 3 * (parts.shape[0] // 4)
        half = parts.shape[0] // 8
        return self.send((parts[across : across + half], 1), (parts[across + half :], 2))

    def scatter_far(self, parts, near):
        if not square():
            return []
        rows = parts.shape[0] // 4
        half = rows // 2

        def add(parts, low, high):
            one, two = parts[rows : 2 * rows], parts[2 * rows : 3 * rows]
            one_high = (one[half:].astype(F32) + high.astype(F32)).astype(BF16)
            two_low = (two[:half].astype(F32) + low.astype(F32)).astype(BF16)
            return (
                jnp.concatenate([one[:half], one_high], axis=0),
                jnp.concatenate([two_low, two[half:]], axis=0),
            )

        self.wait(*near)
        one, two = self.run(add, parts, *near)
        return self.send((one, 1), (two, 2))

    def scattered(self, parts, far):
        if not square():
            return lax.psum_scatter(parts, "ctx", scatter_dimension=0, tiled=True).astype(F32)
        self.wait(*far)
        own = parts[: parts.shape[0] // 4]
        return own.astype(F32) + far[0].astype(F32) + far[1].astype(F32)

    def exchange(self, block_for):
        size = lax.axis_size("ctx")
        rank = lax.axis_index("ctx")
        if not square():
            stacked = jnp.stack([block_for(t) for t in range(size)])
            return [lax.all_to_all(stacked, "ctx", 0, 0)]
        return [block_for(rank)] + self.send(*[(block_for(rank ^ m), m) for m in (1, 2, 3)])

    def exchanged(self, received):
        if not square():
            return received[0]
        rank = lax.axis_index("ctx")
        self.wait(*received[1:])

        def lay(*received):
            out = jnp.zeros((4,) + received[0].shape, received[0].dtype)
            for member, value in enumerate(received):
                out = lax.dynamic_update_index_in_dim(out, value, rank ^ member, 0)
            return out

        return self.run(lay, *received)

    def all_rows(self, received):
        mine = self.exchanged(received)
        return lax.all_gather(
            mine.reshape(-1, mine.shape[-1]), "dp", axis=0, tiled=True
        )

    def own_rows(self, summed):
        rows = summed.shape[0] // lax.axis_size("ctx")
        self.wait(summed)
        return self.exchange(lambda t: lax.dynamic_slice_in_dim(summed, t * rows, rows, axis=0))


def square():
    return lax.axis_size("ctx") == 4


def sum_over_dp(grads):
    return lax.psum_scatter(grads, "dp", scatter_dimension=0, tiled=True)


def swap_halves(rows):
    lane = lax.broadcasted_iota(jnp.int32, rows.shape, 1)
    return jnp.where(
        lane % HEAD_SIZE < HEAD_SIZE // 2,
        pltpu.roll(rows, LANES - HEAD_SIZE // 2, 1),
        pltpu.roll(rows, HEAD_SIZE // 2, 1),
    )


def both_halves(rows, half):
    lane = lax.broadcasted_iota(jnp.int32, rows.shape, 1)
    kept = jnp.where(lane // HEAD_SIZE == half, rows.astype(F32), 0.0)
    return (kept + pltpu.roll(kept, HEAD_SIZE, 1)).astype(BF16)


def two_heads(rows):
    lane = lax.broadcasted_iota(jnp.int32, rows.shape, 1)
    wide = rows.astype(F32)
    first = jnp.where(lane < HEAD_SIZE, wide, 0.0)
    second = jnp.where(lane < HEAD_SIZE, 0.0, wide)
    return jnp.concatenate([first, second], axis=0).astype(BF16)


def visible(size):
    key = lax.broadcasted_iota(jnp.int32, (size, 2 * size), 0)
    query = lax.broadcasted_iota(jnp.int32, (size, 2 * size), 1) % size
    return key <= query


def attention_forward_kernel(
    slot_ref, q_ref, k_ref, v_ref, cos_ref, sin_ref,
    out_ref, queries_ref, keys_ref, values_ref, total_ref, key_both, value_turned,
    *, span, pairs_of_head, pairs_of_block
):
    pair = pl.program_id(0)
    length = q_ref.shape[0]
    spans = length // span
    block = QUERY_BLOCK

    def place(index):
        return pl.ds(pl.multiple_of(slot_ref[index] * span, span), span)

    def turned(source, index):
        here = slice(index * span, (index + 1) * span)
        rows = source[place(index), :]
        return rows * cos_ref[here, :] + swap_halves(rows) * sin_ref[here, :]

    for index in range(spans):
        here = slice(index * span, (index + 1) * span)
        queries_ref[here, :] = turned(q_ref, index).astype(BF16)

    @pl.when(pair % pairs_of_block == 0)
    def _():
        for index in range(spans):
            here = slice(index * span, (index + 1) * span)
            keys_ref[here, :] = turned(k_ref, index).astype(BF16)
            values_ref[here, :] = v_ref[place(index), :].astype(BF16)

    @pl.when(pair % pairs_of_head == 0)
    def _():
        half = (pair // pairs_of_head) % 2
        key_both[...] = both_halves(keys_ref[...], half)
        value_both = both_halves(values_ref[...], half)
        value_turned[...] = value_both.astype(F32).T[:HEAD_SIZE].astype(BF16)

    mask = visible(block)
    for index in range(length // block):
        low, high = index * block, (index + 1) * block
        wide = two_heads(queries_ref[low:high, :] * jnp.asarray(HEAD_SIZE**-0.5, BF16))
        diagonal = jnp.where(mask, dot(key_both[low:high, :], wide, NT), -1e30)
        top = jnp.max(diagonal, axis=0, keepdims=True)
        if index:
            before = dot(key_both[:low, :], wide, NT)
            top = jnp.maximum(top, jnp.max(before, axis=0, keepdims=True))
        near = jnp.exp(diagonal - top)
        total = jnp.sum(near, axis=0, keepdims=True)
        attended = dot(value_turned[:, low:high], near.astype(BF16))
        if index:
            far = jnp.exp(before - top)
            total = total + jnp.sum(far, axis=0, keepdims=True)
            attended = attended + dot(value_turned[:, :low], far.astype(BF16))
        total_ref[0, index : index + 1, :] = top + jnp.log(total)
        attended = attended / total
        rows = jnp.concatenate([attended[:, :block], attended[:, block:]], axis=0).T.astype(BF16)
        for part in range(block // span):
            out_ref[place(index * (block // span) + part), :] = rows[
                part * span : (part + 1) * span
            ]


def attention_backward_kernel(
    slot_ref, queries_ref, keys_ref, values_ref, total_ref, grad_ref, cos_ref, sin_ref,
    grad_q_ref, grad_k_ref, grad_v_ref, key_both, value_both, key_turned, key_sum, value_sum,
    *, span, pairs_of_head
):
    pair = pl.program_id(0)
    length = queries_ref.shape[0]
    spans = length // span
    block = QUERY_BLOCK
    each = block // span
    half = (pair // pairs_of_head) % 2

    def place(index):
        return pl.ds(pl.multiple_of(slot_ref[index] * span, span), span)

    def turned_back(rows, index):
        here = slice(index * span, (index + 1) * span)
        return rows * cos_ref[here, :] - swap_halves(rows) * sin_ref[here, :]

    @pl.when(pair % pairs_of_head == 0)
    def _():
        key_both[...] = both_halves(keys_ref[...], half)
        value_both[...] = both_halves(values_ref[...], half)
        key_turned[...] = key_both[...].astype(F32).T[:HEAD_SIZE].astype(BF16)
        key_sum[...] = jnp.zeros_like(key_sum)
        value_sum[...] = jnp.zeros_like(value_sum)

    mask = visible(block)
    for index in range(length // block):
        low, high = index * block, (index + 1) * block
        wide = two_heads(queries_ref[low:high, :] * jnp.asarray(HEAD_SIZE**-0.5, BF16))
        grad = two_heads(
            jnp.concatenate(
                [grad_ref[place(index * each + part), :] for part in range(each)], axis=0
            )
        )
        total = total_ref[0, index : index + 1, :]
        ranges = [(low, high)] + ([(0, low)] if index else [])
        probs, grad_probs, row_dot = [], [], 0.0
        for start, stop in ranges:
            scores = dot(key_both[start:stop, :], wide, NT)
            if start == low:
                scores = jnp.where(mask, scores, -1e30)
            prob = jnp.exp(scores - total)
            grad_prob = dot(value_both[start:stop, :], grad, NT)
            row_dot = row_dot + jnp.sum(prob * grad_prob, axis=0, keepdims=True)
            probs.append(prob)
            grad_probs.append(grad_prob)
        turned = 0.0
        for (start, stop), prob, grad_prob in zip(ranges, probs, grad_probs):
            grad_score = (prob * (grad_prob - row_dot)).astype(BF16)
            value_sum[start:stop, :] += dot(prob.astype(BF16), grad)
            key_sum[start:stop, :] += dot(grad_score, wide)
            turned = turned + dot(key_turned[:, start:stop], grad_score)
        turned = turned * HEAD_SIZE**-0.5
        rows = jnp.concatenate([turned[:, :block], turned[:, block:]], axis=0).T
        for part in range(each):
            at = index * each + part
            grad_q_ref[place(at), :] = turned_back(
                rows[part * span : (part + 1) * span], at
            ).astype(BF16)

    @pl.when(pair % pairs_of_head == pairs_of_head - 1)
    def _():
        for index in range(spans):
            here = slice(index * span, (index + 1) * span)
            key_rows, value_rows = key_sum[here, :], value_sum[here, :]
            key_rows = turned_back(key_rows + pltpu.roll(key_rows, HEAD_SIZE, 1), index)
            value_rows = value_rows + pltpu.roll(value_rows, HEAD_SIZE, 1)
            lane = lax.broadcasted_iota(jnp.int32, key_rows.shape, 1)
            for target, rows in ((grad_k_ref, key_rows), (grad_v_ref, value_rows)):
                old = target[place(index), :].astype(F32)
                keep = (lane < HEAD_SIZE) & (half == 1)
                target[place(index), :] = jnp.where(keep, old, rows).astype(BF16)


def attention_sizes(query_width, group_size):
    pairs = query_width // LANES
    pairs_of_head = group_size // 2
    return pairs, pairs_of_head, 2 * pairs_of_head


def attention_forward(qkv, slots, cos_lanes, sin_lanes, query_width, key_width, group_size):
    length = qkv.shape[0]
    pairs, pairs_of_head, pairs_of_block = attention_sizes(query_width, group_size)
    key_at, value_at = query_width // LANES, (query_width + key_width) // LANES
    tile = (length, LANES)
    by_pair = pl.BlockSpec(tile, lambda p, s: (0, p))
    by_block = pl.BlockSpec(tile, lambda p, s: (0, p // pairs_of_block))
    whole = pl.BlockSpec(tile, lambda p, s: (0, 0))
    blocks = length // QUERY_BLOCK
    work = 2 * query_width * length * length
    return pl.pallas_call(
        functools.partial(
            attention_forward_kernel,
            span=length // slots.shape[0],
            pairs_of_head=pairs_of_head,
            pairs_of_block=pairs_of_block,
        ),
        grid_spec=pltpu.PrefetchScalarGridSpec(
            num_scalar_prefetch=1,
            grid=(pairs,),
            in_specs=[
                by_pair,
                pl.BlockSpec(tile, lambda p, s: (0, key_at + p // pairs_of_block)),
                pl.BlockSpec(tile, lambda p, s: (0, value_at + p // pairs_of_block)),
                whole,
                whole,
            ],
            out_specs=[
                by_pair,
                by_pair,
                by_block,
                by_block,
                pl.BlockSpec((1, blocks, 2 * QUERY_BLOCK), lambda p, s: (p, 0, 0)),
            ],
            scratch_shapes=[pltpu.VMEM(tile, BF16), pltpu.VMEM((HEAD_SIZE, length), BF16)],
        ),
        out_shape=[
            jax.ShapeDtypeStruct((length, query_width), BF16),
            jax.ShapeDtypeStruct((length, query_width), BF16),
            jax.ShapeDtypeStruct((length, key_width), BF16),
            jax.ShapeDtypeStruct((length, key_width), BF16),
            jax.ShapeDtypeStruct((pairs, blocks, 2 * QUERY_BLOCK), F32),
        ],
        compiler_params=pltpu.CompilerParams(
            dimension_semantics=("arbitrary",), vmem_limit_bytes=48 << 20
        ),
        cost_estimate=pl.CostEstimate(
            flops=8 * work, bytes_accessed=8 << 20, transcendentals=work // 128
        ),
        name="attention_forward",
    )(slots, qkv, qkv, qkv, cos_lanes, sin_lanes)


def attention_backward(kept, grad, slots, cos_lanes, sin_lanes, group_size):
    queries, keys, values, totals = kept
    length, query_width = queries.shape
    key_width = keys.shape[1]
    pairs, pairs_of_head, pairs_of_block = attention_sizes(query_width, group_size)
    tile = (length, LANES)
    by_pair = pl.BlockSpec(tile, lambda p, s: (0, p))
    by_block = pl.BlockSpec(tile, lambda p, s: (0, p // pairs_of_block))
    whole = pl.BlockSpec(tile, lambda p, s: (0, 0))
    blocks = length // QUERY_BLOCK
    work = 2 * query_width * length * length
    return pl.pallas_call(
        functools.partial(
            attention_backward_kernel, span=length // slots.shape[0], pairs_of_head=pairs_of_head
        ),
        grid_spec=pltpu.PrefetchScalarGridSpec(
            num_scalar_prefetch=1,
            grid=(pairs,),
            in_specs=[
                by_pair,
                by_block,
                by_block,
                pl.BlockSpec((1, blocks, 2 * QUERY_BLOCK), lambda p, s: (p, 0, 0)),
                by_pair,
                whole,
                whole,
            ],
            out_specs=[by_pair, by_block, by_block],
            scratch_shapes=[
                pltpu.VMEM(tile, BF16),
                pltpu.VMEM(tile, BF16),
                pltpu.VMEM((HEAD_SIZE, length), BF16),
                pltpu.VMEM(tile, F32),
                pltpu.VMEM(tile, F32),
            ],
        ),
        out_shape=[
            jax.ShapeDtypeStruct((length, query_width), BF16),
            jax.ShapeDtypeStruct((length, key_width), BF16),
            jax.ShapeDtypeStruct((length, key_width), BF16),
        ],
        compiler_params=pltpu.CompilerParams(
            dimension_semantics=("arbitrary",), vmem_limit_bytes=48 << 20
        ),
        cost_estimate=pl.CostEstimate(
            flops=20 * work, bytes_accessed=8 << 20, transcendentals=work // 128
        ),
        name="attention_backward",
    )(slots, queries, keys, values, totals, grad, cos_lanes, sin_lanes)


def feed_kernel(feed_ref, down_in_ref, pair_ref, down_ref, activated_ref, grads_ref):
    tile = down_ref.shape[1]
    step = min(256, feed_ref.shape[0])
    for start in range(0, feed_ref.shape[0], step):
        here = slice(start, start + step)
        both = dot(feed_ref[here, :], pair_ref[...])
        grad_act = dot(down_in_ref[here, :], down_ref[...])
        gate, up = both[:, :tile], both[:, tile:]
        sig = jax.nn.sigmoid(gate)
        silu = gate * sig
        activated_ref[here, :] = (silu * up).astype(BF16)
        grads_ref[here, :tile] = (grad_act * up * (sig + silu * (1.0 - sig))).astype(BF16)
        grads_ref[here, tile:] = (grad_act * silu).astype(BF16)


def feed_middle(feed_in, down_in, weights, width, tile):
    rows, depth = feed_in.shape
    tiles = width // tile
    work = rows * depth * width
    return pl.pallas_call(
        feed_kernel,
        grid=(tiles,),
        in_specs=[
            pl.BlockSpec((rows, depth), lambda j: (0, 0), pipeline_mode=pl.Buffered(1)),
            pl.BlockSpec((rows, depth), lambda j: (0, 0), pipeline_mode=pl.Buffered(1)),
            pl.BlockSpec((depth, 2 * tile), lambda j: (0, j)),
            pl.BlockSpec((depth, tile), lambda j: (0, 2 * tiles + j)),
        ],
        out_specs=[
            pl.BlockSpec((rows, tile), lambda j: (0, j)),
            pl.BlockSpec((rows, 2 * tile), lambda j: (0, j)),
        ],
        out_shape=[
            jax.ShapeDtypeStruct((rows, width), BF16),
            jax.ShapeDtypeStruct((rows, 2 * width), BF16),
        ],
        compiler_params=pltpu.CompilerParams(
            dimension_semantics=("arbitrary",), vmem_limit_bytes=56 << 20
        ),
        cost_estimate=pl.CostEstimate(
            flops=6 * work,
            bytes_accessed=2 * (2 * rows * depth + 3 * depth * width + 3 * rows * width),
            transcendentals=rows * width,
        ),
        name="feed_middle",
    )(feed_in, down_in, weights, weights)


def spread_kernel(*refs):
    count = (len(refs) - 1) // 2
    total = sum(dot(refs[i][...], refs[count + i][...], NT) for i in range(count))
    refs[-1][...] = total.astype(BF16)


def feed_spread(lefts, weights, places, tile):
    rows = lefts[0].shape[0]
    depth = weights[0].shape[0]
    widths = [left.shape[1] for left in lefts]
    work = rows * depth * sum(widths)

    step = min(512, rows)

    def weight_spec(width, place):
        return pl.BlockSpec((tile, width), lambda i, j: (j, place))

    return pl.pallas_call(
        spread_kernel,
        grid=(rows // step, depth // tile),
        in_specs=[pl.BlockSpec((step, width), lambda i, j: (i, 0)) for width in widths]
        + [weight_spec(width, place) for width, place in zip(widths, places)],
        out_specs=pl.BlockSpec((step, tile), lambda i, j: (i, j)),
        out_shape=jax.ShapeDtypeStruct((rows, depth), BF16),
        compiler_params=pltpu.CompilerParams(
            dimension_semantics=("arbitrary", "arbitrary"), vmem_limit_bytes=56 << 20
        ),
        cost_estimate=pl.CostEstimate(
            flops=2 * work,
            bytes_accessed=2 * ((rows + depth) * sum(widths) + rows * depth),
            transcendentals=0,
        ),
        name="feed_spread",
    )(*lefts, *weights)


def lay_kernel(place_ref, *refs, plan, inputs):
    outs = refs[inputs:]
    for source, member, start, width, target, at in plan:
        each = outs[target].shape[1] // 4
        where = pl.ds(pl.multiple_of(place_ref[member] * each + at, LANES), width)
        outs[target][:, where] = refs[source][:, start : start + width].astype(F32)


def lay_out(received, pieces, widths):
    blocks = [block for group in received for block in group]
    rows = blocks[0].shape[0]
    plan = [
        (4 * group + member, member, start, width, target, at)
        for group, start, width, target, at in pieces
        for member in range(4)
    ]
    return pl.pallas_call(
        functools.partial(lay_kernel, plan=plan, inputs=len(blocks)),
        grid_spec=pltpu.PrefetchScalarGridSpec(
            num_scalar_prefetch=1,
            grid=(1,),
            in_specs=[pl.BlockSpec(block.shape, lambda i, p: (0, 0)) for block in blocks],
            out_specs=[pl.BlockSpec((rows, 4 * width), lambda i, p: (0, 0)) for width in widths],
        ),
        out_shape=[jax.ShapeDtypeStruct((rows, 4 * width), F32) for width in widths],
        compiler_params=pltpu.CompilerParams(vmem_limit_bytes=48 << 20),
        name="lay_out",
    )(lax.axis_index("ctx") ^ jnp.arange(4, dtype=jnp.int32), *blocks)


def norm_forward(values):
    inverse_rms = lax.rsqrt(jnp.mean(values * values, axis=-1, keepdims=True) + EPS)
    return (values * inverse_rms, inverse_rms)


def norm_backward(grad_normed, normed, inverse_rms, gain):
    grad_hat = grad_normed * gain
    grad_input = inverse_rms * (
        grad_hat - normed * jnp.mean(grad_hat * normed, axis=-1, keepdims=True)
    )
    return (grad_input, jnp.sum(grad_normed * normed, axis=0))


def rope_lanes(length):
    half = HEAD_SIZE // 2
    frequency = jnp.exp(
        jnp.arange(half, dtype=F32) * (-2.0 * math.log(THETA) / HEAD_SIZE)
    )
    angles = jnp.arange(length, dtype=jnp.int32).astype(F32)[:, None] * frequency[None, :]
    cosine, sine = jnp.cos(angles), jnp.sin(angles)
    return (
        jnp.concatenate([cosine] * 4, axis=1),
        jnp.concatenate([-sine, sine, -sine, sine], axis=1),
    )


def pad_columns(array, width):
    return jnp.pad(array, ((0, 0), (0, width - array.shape[1])))


def body(
    tokens, span_order, out_grad, first_gain, query_weight, key_matrix, value_matrix,
    merge_weight, second_gain, gate_weight, up_weight, down_weight,
):
    seqs, own_rows, depth = tokens.shape
    ctx = lax.axis_size("ctx")
    rank = lax.axis_index("ctx")
    length = own_rows * ctx
    spans = span_order.shape[1]
    weight_rows = gate_weight.shape[0]
    group_size = query_weight.shape[1] // key_matrix.shape[1]
    query_width = query_weight.shape[1] // ctx
    own_key_width = key_matrix.shape[1] // ctx
    key_width = -(-own_key_width // LANES) * LANES
    feed_width = gate_weight.shape[1] // ctx
    tile = min(512, feed_width)
    tiles = feed_width // tile
    first = max(1, 3 * tiles // 4)
    chunks = [first * tile] + ([(tiles - first) * tile] if tiles > first else [])
    starts = [0, chunks[0]][: len(chunks)]
    chain = Chain()

    def columns(weight, t, width, at=0):
        return lax.dynamic_slice_in_dim(weight, t * (weight.shape[1] // ctx) + at, width, axis=1)

    gain_columns = pad_columns(jnp.stack([first_gain, second_gain], axis=1), LANES)

    def projections_for(t):
        return jnp.concatenate(
            [
                columns(query_weight, t, query_width),
                pad_columns(columns(key_matrix, t, own_key_width), key_width),
                pad_columns(columns(value_matrix, t, own_key_width), key_width),
                gain_columns,
            ],
            axis=1,
        )

    def feed_for(part):
        def of(t):
            pieces = []
            for start in range(starts[part], starts[part] + chunks[part], tile):
                pieces += [
                    columns(gate_weight, t, tile, start),
                    columns(up_weight, t, tile, start),
                ]
            pieces.append(columns(down_weight, t, chunks[part], starts[part]))
            return jnp.concatenate(pieces, axis=1)

        return of

    assert seqs == 2 and len(chunks) <= 2
    many = len(chunks) > 1
    last_part = len(chunks) - 1
    qkv_width = query_width + 2 * key_width

    slots = jnp.argsort(span_order, axis=1).astype(jnp.int32)
    if square():
        slots = ((slots // 2) ^ rank) * 2 + slots % 2
    cos_lanes, sin_lanes = rope_lanes(length)

    def project(rows, weight, gain):
        normed, _ = norm_forward(rows.astype(F32))
        rows = (normed * gain).astype(BF16)
        return rows, dot(rows, weight)

    def attend(qkv, slots):
        return attention_forward(
            qkv, slots, cos_lanes, sin_lanes, query_width, key_width, group_size
        )

    def merge_back(rows, weight):
        return dot(rows, weight, NT, BF16)

    def feed_norm(hidden, gain):
        normed, _ = norm_forward(hidden)
        return hidden, (normed * gain).astype(BF16)

    def middle_of(feed_in, down_in, weights, part):
        return feed_middle(feed_in, down_in, weights, chunks[part], tile)

    def feed_back(grads, weights):
        return feed_spread(grads, weights, [0] * len(grads), tile)

    def feed_out(activated, weights):
        return feed_spread(activated, weights, [2] * len(activated), tile)

    def token_grads(left, right):
        return dot(jnp.concatenate(left, axis=0), jnp.concatenate(right, axis=0), TN, BF16)

    def last_grads(feed_in, grads, down_in, activated):
        activated = [jnp.concatenate(parts, axis=1) for parts in activated]
        down = token_grads(down_in, activated)
        if not many:
            return down
        return jnp.concatenate([token_grads(feed_in, grads), down], axis=1)

    def feed_norm_back(hidden, summed, cot, gain):
        normed, inverse = norm_forward(hidden)
        grad_middle, gain_part = norm_backward(summed, normed, inverse, gain)
        grad_hidden = cot.astype(F32) + grad_middle
        return grad_hidden, grad_hidden.astype(BF16), gain_part

    def attend_back(merge_in, weight, kept, slots):
        grad_attn = dot(merge_in, weight, NN, BF16)
        parts = attention_backward(kept, grad_attn, slots, cos_lanes, sin_lanes, group_size)
        return jnp.concatenate(parts, axis=1)

    def project_back(grads, weight):
        return dot(grads, weight, NT, BF16)

    def gain_part_of(rows, lower):
        normed, _ = norm_forward(rows.astype(F32))
        return jnp.sum(normed * lower.astype(F32), axis=0)

    def attention_grads_of(attn_in, grad_qkv, merge_in, attn_out, rows, lower, gain_two_parts):
        gain_one_sum = sum(gain_part_of(r, l) for r, l in zip(rows, lower))
        gains = jnp.stack([gain_one_sum, sum(gain_two_parts)], axis=1)
        return jnp.concatenate(
            [
                token_grads(attn_in, grad_qkv),
                token_grads(merge_in, attn_out),
                pad_columns(gains.astype(BF16), LANES),
            ],
            axis=1,
        )

    def project_norm_back(rows, summed, grad_hidden, gain):
        normed, inverse = norm_forward(rows.astype(F32))
        grad_lower, _ = norm_backward(summed, normed, inverse, gain)
        return grad_hidden + grad_lower

    moved = chain.exchange(projections_for)
    a_near = chain.gather_near(tokens[0])
    projections = chain.all_rows(moved)
    moved = chain.exchange(lambda t: columns(merge_weight, t, query_width))
    merge = chain.all_rows(moved)
    a_far = chain.gather_far(a_near)
    moved = chain.exchange(feed_for(0))
    rows_a = chain.gathered(tokens[0], a_near, a_far)
    b_near = chain.gather_near(tokens[1])

    qkv_weight = projections[:, :qkv_width]
    gains = projections[:, qkv_width : qkv_width + 2].astype(F32)
    gain_one, gain_two = gains[:, 0], gains[:, 1]
    attn_in_a, qkv = chain.run(project, rows_a, qkv_weight, gain_one)
    feeds = [chain.all_rows(moved)]
    attn_out_a, *kept_a = chain.run(attend, qkv, slots[0])
    branch_a = chain.run(merge_back, attn_out_a, merge)
    near_a = chain.scatter_near(branch_a)
    b_far = chain.gather_far(b_near)
    far_a = chain.scatter_far(branch_a, near_a)
    rows_b = chain.gathered(tokens[1], b_near, b_far)
    cot_a_near = chain.gather_near(out_grad[0])
    attn_in_b, qkv = chain.run(project, rows_b, qkv_weight, gain_one)
    hidden_a, feed_a = chain.run(
        feed_norm, tokens[0].astype(F32) + chain.scattered(branch_a, far_a), gain_two
    )
    feed_a_near = chain.gather_near(feed_a)
    attn_out_b, *kept_b = chain.run(attend, qkv, slots[1])
    cot_a_far = chain.gather_far(cot_a_near)
    branch_b = chain.run(merge_back, attn_out_b, merge)
    near_b = chain.scatter_near(branch_b)
    feed_a_far = chain.gather_far(feed_a_near)
    down_in_a = chain.gathered(out_grad[0], cot_a_near, cot_a_far)
    if many:
        moved = chain.exchange(feed_for(1))
    far_b = chain.scatter_far(branch_b, near_b)
    feed_in_a = chain.gathered(feed_a, feed_a_near, feed_a_far)
    cot_b_near = chain.gather_near(out_grad[1])
    if many:
        feeds.append(chain.all_rows(moved))
    hidden_b, feed_b = chain.run(
        feed_norm, tokens[1].astype(F32) + chain.scattered(branch_b, far_b), gain_two
    )
    feed_b_near = chain.gather_near(feed_b)
    middle_a = [chain.run(lambda f, d, w: middle_of(f, d, w, 0), feed_in_a, down_in_a, feeds[0])]
    cot_b_far = chain.gather_far(cot_b_near)
    feed_b_far = chain.gather_far(feed_b_near)
    down_in_b = chain.gathered(out_grad[1], cot_b_near, cot_b_far)
    feed_in_b = chain.gathered(feed_b, feed_b_near, feed_b_far)
    if many:
        middle_a.append(
            chain.run(lambda f, d, w: middle_of(f, d, w, 1), feed_in_a, down_in_a, feeds[1])
        )
    back_a = chain.run(feed_back, [m[1] for m in middle_a], feeds)
    near_a = chain.scatter_near(back_a)
    middle_b = [chain.run(lambda f, d, w: middle_of(f, d, w, 0), feed_in_b, down_in_b, feeds[0])]
    far_a = chain.scatter_far(back_a, near_a)
    grads_first = chain.run(
        token_grads, [feed_in_a, feed_in_b], [middle_a[0][1], middle_b[0][1]]
    )
    sums_first = sum_over_dp(grads_first)
    grad_hidden_a, merge_a, gain_two_a = chain.run(
        feed_norm_back, hidden_a, chain.scattered(back_a, far_a), out_grad[0], gain_two
    )
    merge_a_near = chain.gather_near(merge_a)
    if many:
        middle_b.append(
            chain.run(lambda f, d, w: middle_of(f, d, w, 1), feed_in_b, down_in_b, feeds[1])
        )
    back_b = chain.run(feed_back, [m[1] for m in middle_b], feeds)
    near_b = chain.scatter_near(back_b)
    merge_a_far = chain.gather_far(merge_a_near)
    out_a = chain.run(feed_out, [m[0] for m in middle_a], feeds)
    out_a_near = chain.scatter_near(out_a)
    far_b = chain.scatter_far(back_b, near_b)
    merge_in_a = chain.gathered(merge_a, merge_a_near, merge_a_far)
    grads_last = chain.run(
        last_grads,
        [feed_in_a, feed_in_b],
        [middle_a[last_part][1], middle_b[last_part][1]],
        [down_in_a, down_in_b],
        [[m[0] for m in middle_a], [m[0] for m in middle_b]],
    )
    out_a_far = chain.scatter_far(out_a, out_a_near)
    grad_hidden_b, merge_b, gain_two_b = chain.run(
        feed_norm_back, hidden_b, chain.scattered(back_b, far_b), out_grad[1], gain_two
    )
    merge_b_near = chain.gather_near(merge_b)
    grad_qkv_a = chain.run(attend_back, merge_in_a, merge, kept_a, slots[0])
    chain.wait(sums_first)
    sums_last = sum_over_dp(chain.run(lambda g: g, grads_last))
    merge_b_far = chain.gather_far(merge_b_near)
    lower_a = chain.run(project_back, grad_qkv_a, qkv_weight)
    lower_a_near = chain.scatter_near(lower_a)
    out_b = chain.run(feed_out, [m[0] for m in middle_b], feeds)
    lower_a_far = chain.scatter_far(lower_a, lower_a_near)
    merge_in_b = chain.gathered(merge_b, merge_b_near, merge_b_far)
    out_b_near = chain.scatter_near(out_b)
    grad_qkv_b = chain.run(attend_back, merge_in_b, merge, kept_b, slots[1])
    lower_b = chain.run(project_back, grad_qkv_b, qkv_weight)
    lower_b_near = chain.scatter_near(lower_b)
    out_b_far = chain.scatter_far(out_b, out_b_near)
    attention_grads = chain.run(
        attention_grads_of,
        [attn_in_a, attn_in_b],
        [grad_qkv_a, grad_qkv_b],
        [merge_in_a, merge_in_b],
        [attn_out_a, attn_out_b],
        [rows_a, rows_b],
        [lower_a, lower_b],
        [gain_two_a, gain_two_b],
    )
    lower_b_far = chain.scatter_far(lower_b, lower_b_near)
    moved_first = chain.own_rows(sums_first)
    input_grad_a = chain.run(
        project_norm_back, tokens[0], chain.scattered(lower_a, lower_a_far), grad_hidden_a, gain_one
    )
    block_a = chain.run(lambda h, o: (h + o).astype(BF16), hidden_a, chain.scattered(out_a, out_a_far))
    block_b = chain.run(lambda h, o: (h + o).astype(BF16), hidden_b, chain.scattered(out_b, out_b_far))
    input_grad_b = chain.run(
        project_norm_back, tokens[1], chain.scattered(lower_b, lower_b_far), grad_hidden_b, gain_one
    )
    chain.wait(sums_last)
    attention_sums = sum_over_dp(chain.run(lambda g: g, attention_grads))
    moved_last = chain.own_rows(sums_last)
    chain.wait(*moved_last[1:])
    blocks = [block_a, block_b]
    input_grad = [input_grad_a, input_grad_b]

    key_at, value_at = query_width, query_width + key_width
    merge_at, gain_at = qkv_width, qkv_width + query_width
    feed_pieces = [
        (part, (2 * at + kind) * tile, tile, kind, starts[part] + at * tile)
        for part, width in enumerate(chunks)
        for at in range(width // tile)
        for kind in range(2)
    ] + [(len(chunks) - 1, 2 * chunks[1] if many else 0, feed_width, 2, 0)]
    attention_pieces = [
        (0, 0, query_width, 0, 0),
        (0, key_at, own_key_width, 1, 0),
        (0, value_at, own_key_width, 2, 0),
        (0, merge_at, query_width, 3, 0),
    ]

    def results(received, pieces, widths):
        if square():
            return lay_out(received, pieces, widths)
        columns_of = [[] for _ in widths]
        for group, start, width, target, at in sorted(pieces, key=lambda piece: piece[4]):
            columns_of[target].append(received[group][0][:, :, start : start + width])
        return [
            jnp.concatenate(parts, axis=2)
            .astype(F32)
            .transpose(1, 0, 2)
            .reshape(weight_rows, -1)
            for parts in columns_of
        ]

    gate_total, up_total, down_total = chain.run(
        lambda *received: results(received, feed_pieces, [feed_width] * 3),
        *([moved_first, moved_last] if many else [moved_last]),
    )
    moved = chain.own_rows(attention_sums)
    chain.wait(*moved[1:])
    query_total, key_total, value_total, merge_total = chain.run(
        lambda received: results(
            [received], attention_pieces, [query_width, own_key_width, own_key_width, query_width]
        ),
        moved,
    )
    gain_totals = sum(block[..., gain_at : gain_at + 2].astype(F32) for block in moved)
    if not square():
        gain_totals = jnp.sum(gain_totals, axis=0)
    return (
        jnp.stack(blocks),
        jnp.stack(input_grad),
        gain_totals[:, 0],
        query_total,
        key_total,
        value_total,
        merge_total,
        gain_totals[:, 1],
        gate_total,
        up_total,
        down_total,
    )


def solution(mesh):
    rows = P(("dp", "ctx"), None)
    vector = P(("dp", "ctx"))
    acts = P("dp", "ctx", None)
    in_specs = (
        acts, P("dp", None), acts, vector, rows, rows, rows, rows, vector, rows, rows, rows,
    )
    out_specs = (acts, acts, vector, rows, rows, rows, rows, vector, rows, rows, rows)
    return jax.shard_map(body, mesh=mesh, in_specs=in_specs, out_specs=out_specs, check_vma=False)
```

```python
import functools
import math

import jax
import jax.numpy as jnp
from jax import lax
from jax.experimental import pallas as pl
from jax.experimental.pallas import tpu as pltpu
from jax.sharding import PartitionSpec as P

HEAD_SIZE = 64
LANES = 128
EPS = 1e-05
THETA = 500000.0
QUERY_BLOCK = 256
F32 = jnp.float32
BF16 = jnp.bfloat16

NN = (((1,), (0,)), ((), ()))
NT = (((1,), (1,)), ((), ()))
TN = (((0,), (0,)), ((), ()))


def dot(left, right, dims=NN, out=F32):
    return lax.dot_general(left, right, dims, preferred_element_type=F32).astype(out)


class Chain:
    def __init__(self):
        self.last = ()

    def after(self, values):
        values = tuple(values)
        if not self.last:
            return values
        return lax.optimization_barrier(values + self.last)[: len(values)]

    def run(self, function, *args):
        leaves, tree = jax.tree.flatten(args)
        out = function(*jax.tree.unflatten(tree, self.after(leaves)))
        self.last = tuple(jax.tree.leaves(out))
        return out

    def wait(self, *arrays):
        self.last = self.last + arrays


    def send(self, *sends):
        blocks = self.after(block for block, _ in sends)
        return [
            lax.ppermute(block, "ctx", [(i, i ^ bits) for i in range(4)])
            for block, (_, bits) in zip(blocks, sends)
        ]

    def gather_near(self, own):
        return self.send((own, 1), (own, 2)) if square() else []

    def gather_far(self, near):
        if not square():
            return []
        self.wait(*near)
        half = near[0].shape[0] // 2
        one, two = self.after(near)
        return self.send((one[:half], 2), (two[half:], 1))

    def scatter_near(self, parts):
        return self.send((parts[1], 1), (parts[2], 2)) if square() else []

    def scatter_far(self, parts, near):
        if not square():
            return []

        def add(own, one, two):
            half = one.shape[0] // 2
            for_one = own[2 * half : 3 * half].astype(F32) + two[half:].astype(F32)
            for_two = own[3 * half :].astype(F32) + one[half:].astype(F32)
            return for_one.astype(BF16), for_two.astype(BF16)

        self.wait(*near)
        for_one, for_two = self.run(add, parts[0], *near)
        return self.send((for_one, 1), (for_two, 2))

    def exchange(self, block_for):
        size = lax.axis_size("ctx")
        rank = lax.axis_index("ctx")
        if not square():
            stacked = jnp.stack([block_for(t) for t in range(size)])
            return [lax.all_to_all(stacked, "ctx", 0, 0)]
        return [block_for(rank)] + self.send(*[(block_for(rank ^ m), m) for m in (1, 2, 3)])

    def exchanged(self, received):
        if not square():
            return received[0]
        rank = lax.axis_index("ctx")
        self.wait(*received[1:])

        def lay(*received):
            out = jnp.zeros((4,) + received[0].shape, received[0].dtype)
            for member, value in enumerate(received):
                out = lax.dynamic_update_index_in_dim(out, value, rank ^ member, 0)
            return out

        return self.run(lay, *received)

    def all_rows(self, received):
        mine = self.exchanged(received)
        return lax.all_gather(
            mine.reshape(-1, mine.shape[-1]), "dp", axis=0, tiled=True
        )

    def own_rows(self, summed):
        rows = summed.shape[0] // lax.axis_size("ctx")
        self.wait(summed)
        return self.exchange(lambda t: lax.dynamic_slice_in_dim(summed, t * rows, rows, axis=0))


def square():
    return lax.axis_size("ctx") == 4


HALVES = ((0, 0), (0, 1), (1, 1), (2, 0), (1, 0), (3, 0), (2, 1), (3, 1))


def gathered(own, near, far):
    if not square():
        return lax.all_gather(own, "ctx", axis=0, tiled=True)
    half = own.shape[0] // 2
    one, two = near
    low, high = far
    return jnp.concatenate(
        [own, one[half:], two[:half], one[:half], low, two[half:], high], axis=0
    )


def scattered(parts, near, far):
    if not square():
        return lax.psum_scatter(parts[0], "ctx", scatter_dimension=0, tiled=True).astype(F32)
    half = near[0].shape[0] // 2
    low = parts[0][:half].astype(F32) + near[0][:half].astype(F32) + far[1].astype(F32)
    high = parts[0][half : 2 * half].astype(F32) + near[1][:half].astype(F32) + far[0].astype(F32)
    return jnp.concatenate([low, high], axis=0)


def sum_over_dp(grads):
    return lax.psum_scatter(grads, "dp", scatter_dimension=0, tiled=True)


def swap_halves(rows):
    lane = lax.broadcasted_iota(jnp.int32, rows.shape, 1)
    return jnp.where(
        lane % HEAD_SIZE < HEAD_SIZE // 2,
        pltpu.roll(rows, LANES - HEAD_SIZE // 2, 1),
        pltpu.roll(rows, HEAD_SIZE // 2, 1),
    )


def both_halves(rows, half):
    lane = lax.broadcasted_iota(jnp.int32, rows.shape, 1)
    kept = jnp.where(lane // HEAD_SIZE == half, rows.astype(F32), 0.0)
    return (kept + pltpu.roll(kept, HEAD_SIZE, 1)).astype(BF16)


def two_heads(rows):
    lane = lax.broadcasted_iota(jnp.int32, rows.shape, 1)
    wide = rows.astype(F32)
    first = jnp.where(lane < HEAD_SIZE, wide, 0.0)
    second = jnp.where(lane < HEAD_SIZE, 0.0, wide)
    return jnp.concatenate([first, second], axis=0).astype(BF16)


def visible(size):
    key = lax.broadcasted_iota(jnp.int32, (size, 2 * size), 0)
    query = lax.broadcasted_iota(jnp.int32, (size, 2 * size), 1) % size
    return key <= query


def attention_forward_kernel(
    slot_ref, q_ref, k_ref, v_ref, cos_ref, sin_ref,
    out_ref, queries_ref, keys_ref, values_ref, total_ref, key_both, value_turned,
    *, span, pairs_of_head, pairs_of_block
):
    pair = pl.program_id(0)
    length = q_ref.shape[0]
    spans = length // span
    block = QUERY_BLOCK

    def place(index):
        return pl.ds(pl.multiple_of(slot_ref[index] * span, span), span)

    def turned(source, index):
        here = slice(index * span, (index + 1) * span)
        rows = source[place(index), :]
        return rows * cos_ref[here, :] + swap_halves(rows) * sin_ref[here, :]

    for index in range(spans):
        here = slice(index * span, (index + 1) * span)
        queries_ref[here, :] = turned(q_ref, index).astype(BF16)

    @pl.when(pair % pairs_of_block == 0)
    def _():
        for index in range(spans):
            here = slice(index * span, (index + 1) * span)
            keys_ref[here, :] = turned(k_ref, index).astype(BF16)
            values_ref[here, :] = v_ref[place(index), :].astype(BF16)

    @pl.when(pair % pairs_of_head == 0)
    def _():
        half = (pair // pairs_of_head) % 2
        key_both[...] = both_halves(keys_ref[...], half)
        value_both = both_halves(values_ref[...], half)
        value_turned[...] = value_both.astype(F32).T[:HEAD_SIZE].astype(BF16)

    mask = visible(block)
    for index in range(length // block):
        low, high = index * block, (index + 1) * block
        wide = two_heads(queries_ref[low:high, :] * jnp.asarray(HEAD_SIZE**-0.5, BF16))
        diagonal = jnp.where(mask, dot(key_both[low:high, :], wide, NT), -1e30)
        top = jnp.max(diagonal, axis=0, keepdims=True)
        if index:
            before = dot(key_both[:low, :], wide, NT)
            top = jnp.maximum(top, jnp.max(before, axis=0, keepdims=True))
        near = jnp.exp(diagonal - top)
        total = jnp.sum(near, axis=0, keepdims=True)
        attended = dot(value_turned[:, low:high], near.astype(BF16))
        if index:
            far = jnp.exp(before - top)
            total = total + jnp.sum(far, axis=0, keepdims=True)
            attended = attended + dot(value_turned[:, :low], far.astype(BF16))
        total_ref[0, index : index + 1, :] = top + jnp.log(total)
        attended = attended / total
        rows = jnp.concatenate([attended[:, :block], attended[:, block:]], axis=0).T.astype(BF16)
        for part in range(block // span):
            out_ref[place(index * (block // span) + part), :] = rows[
                part * span : (part + 1) * span
            ]


def attention_backward_kernel(
    slot_ref, queries_ref, keys_ref, values_ref, total_ref, grad_ref, cos_ref, sin_ref,
    grad_q_ref, grad_k_ref, grad_v_ref, key_both, value_both, key_turned, key_sum, value_sum,
    *, span, pairs_of_head
):
    pair = pl.program_id(0)
    length = queries_ref.shape[0]
    spans = length // span
    block = QUERY_BLOCK
    each = block // span
    half = (pair // pairs_of_head) % 2

    def place(index):
        return pl.ds(pl.multiple_of(slot_ref[index] * span, span), span)

    def turned_back(rows, index):
        here = slice(index * span, (index + 1) * span)
        return rows * cos_ref[here, :] - swap_halves(rows) * sin_ref[here, :]

    @pl.when(pair % pairs_of_head == 0)
    def _():
        key_both[...] = both_halves(keys_ref[...], half)
        value_both[...] = both_halves(values_ref[...], half)
        key_turned[...] = key_both[...].astype(F32).T[:HEAD_SIZE].astype(BF16)
        key_sum[...] = jnp.zeros_like(key_sum)
        value_sum[...] = jnp.zeros_like(value_sum)

    mask = visible(block)
    for index in range(length // block):
        low, high = index * block, (index + 1) * block
        wide = two_heads(queries_ref[low:high, :] * jnp.asarray(HEAD_SIZE**-0.5, BF16))
        grad = two_heads(
            jnp.concatenate(
                [grad_ref[place(index * each + part), :] for part in range(each)], axis=0
            )
        )
        total = total_ref[0, index : index + 1, :]
        ranges = [(low, high)] + ([(0, low)] if index else [])
        probs, grad_probs, row_dot = [], [], 0.0
        for start, stop in ranges:
            scores = dot(key_both[start:stop, :], wide, NT)
            if start == low:
                scores = jnp.where(mask, scores, -1e30)
            prob = jnp.exp(scores - total)
            grad_prob = dot(value_both[start:stop, :], grad, NT)
            row_dot = row_dot + jnp.sum(prob * grad_prob, axis=0, keepdims=True)
            probs.append(prob)
            grad_probs.append(grad_prob)
        turned = 0.0
        for (start, stop), prob, grad_prob in zip(ranges, probs, grad_probs):
            grad_score = (prob * (grad_prob - row_dot)).astype(BF16)
            value_sum[start:stop, :] += dot(prob.astype(BF16), grad)
            key_sum[start:stop, :] += dot(grad_score, wide)
            turned = turned + dot(key_turned[:, start:stop], grad_score)
        turned = turned * HEAD_SIZE**-0.5
        rows = jnp.concatenate([turned[:, :block], turned[:, block:]], axis=0).T
        for part in range(each):
            at = index * each + part
            grad_q_ref[place(at), :] = turned_back(
                rows[part * span : (part + 1) * span], at
            ).astype(BF16)

    @pl.when(pair % pairs_of_head == pairs_of_head - 1)
    def _():
        for index in range(spans):
            here = slice(index * span, (index + 1) * span)
            key_rows, value_rows = key_sum[here, :], value_sum[here, :]
            key_rows = turned_back(key_rows + pltpu.roll(key_rows, HEAD_SIZE, 1), index)
            value_rows = value_rows + pltpu.roll(value_rows, HEAD_SIZE, 1)
            lane = lax.broadcasted_iota(jnp.int32, key_rows.shape, 1)
            for target, rows in ((grad_k_ref, key_rows), (grad_v_ref, value_rows)):
                old = target[place(index), :].astype(F32)
                keep = (lane < HEAD_SIZE) & (half == 1)
                target[place(index), :] = jnp.where(keep, old, rows).astype(BF16)


def attention_sizes(query_width, group_size):
    pairs = query_width // LANES
    pairs_of_head = group_size // 2
    return pairs, pairs_of_head, 2 * pairs_of_head


def attention_forward(qkv, slots, cos_lanes, sin_lanes, query_width, key_width, group_size):
    length = qkv.shape[0]
    pairs, pairs_of_head, pairs_of_block = attention_sizes(query_width, group_size)
    key_at, value_at = query_width // LANES, (query_width + key_width) // LANES
    tile = (length, LANES)
    by_pair = pl.BlockSpec(tile, lambda p, s: (0, p))
    by_block = pl.BlockSpec(tile, lambda p, s: (0, p // pairs_of_block))
    whole = pl.BlockSpec(tile, lambda p, s: (0, 0))
    blocks = length // QUERY_BLOCK
    work = 2 * query_width * length * length
    return pl.pallas_call(
        functools.partial(
            attention_forward_kernel,
            span=length // slots.shape[0],
            pairs_of_head=pairs_of_head,
            pairs_of_block=pairs_of_block,
        ),
        grid_spec=pltpu.PrefetchScalarGridSpec(
            num_scalar_prefetch=1,
            grid=(pairs,),
            in_specs=[
                by_pair,
                pl.BlockSpec(tile, lambda p, s: (0, key_at + p // pairs_of_block)),
                pl.BlockSpec(tile, lambda p, s: (0, value_at + p // pairs_of_block)),
                whole,
                whole,
            ],
            out_specs=[
                by_pair,
                by_pair,
                by_block,
                by_block,
                pl.BlockSpec((1, blocks, 2 * QUERY_BLOCK), lambda p, s: (p, 0, 0)),
            ],
            scratch_shapes=[pltpu.VMEM(tile, BF16), pltpu.VMEM((HEAD_SIZE, length), BF16)],
        ),
        out_shape=[
            jax.ShapeDtypeStruct((length, query_width), BF16),
            jax.ShapeDtypeStruct((length, query_width), BF16),
            jax.ShapeDtypeStruct((length, key_width), BF16),
            jax.ShapeDtypeStruct((length, key_width), BF16),
            jax.ShapeDtypeStruct((pairs, blocks, 2 * QUERY_BLOCK), F32),
        ],
        compiler_params=pltpu.CompilerParams(
            dimension_semantics=("arbitrary",), vmem_limit_bytes=48 << 20
        ),
        cost_estimate=pl.CostEstimate(
            flops=8 * work, bytes_accessed=8 << 20, transcendentals=work // 128
        ),
        name="attention_forward",
    )(slots, qkv, qkv, qkv, cos_lanes, sin_lanes)


def attention_backward(kept, grad, slots, cos_lanes, sin_lanes, group_size):
    queries, keys, values, totals = kept
    length, query_width = queries.shape
    key_width = keys.shape[1]
    pairs, pairs_of_head, pairs_of_block = attention_sizes(query_width, group_size)
    tile = (length, LANES)
    by_pair = pl.BlockSpec(tile, lambda p, s: (0, p))
    by_block = pl.BlockSpec(tile, lambda p, s: (0, p // pairs_of_block))
    whole = pl.BlockSpec(tile, lambda p, s: (0, 0))
    blocks = length // QUERY_BLOCK
    work = 2 * query_width * length * length
    return pl.pallas_call(
        functools.partial(
            attention_backward_kernel, span=length // slots.shape[0], pairs_of_head=pairs_of_head
        ),
        grid_spec=pltpu.PrefetchScalarGridSpec(
            num_scalar_prefetch=1,
            grid=(pairs,),
            in_specs=[
                by_pair,
                by_block,
                by_block,
                pl.BlockSpec((1, blocks, 2 * QUERY_BLOCK), lambda p, s: (p, 0, 0)),
                by_pair,
                whole,
                whole,
            ],
            out_specs=[by_pair, by_block, by_block],
            scratch_shapes=[
                pltpu.VMEM(tile, BF16),
                pltpu.VMEM(tile, BF16),
                pltpu.VMEM((HEAD_SIZE, length), BF16),
                pltpu.VMEM(tile, F32),
                pltpu.VMEM(tile, F32),
            ],
        ),
        out_shape=[
            jax.ShapeDtypeStruct((length, query_width), BF16),
            jax.ShapeDtypeStruct((length, key_width), BF16),
            jax.ShapeDtypeStruct((length, key_width), BF16),
        ],
        compiler_params=pltpu.CompilerParams(
            dimension_semantics=("arbitrary",), vmem_limit_bytes=48 << 20
        ),
        cost_estimate=pl.CostEstimate(
            flops=20 * work, bytes_accessed=8 << 20, transcendentals=work // 128
        ),
        name="attention_backward",
    )(slots, queries, keys, values, totals, grad, cos_lanes, sin_lanes)


def feed_kernel(feed_ref, down_in_ref, pair_ref, down_ref, activated_ref, grads_ref):
    tile = down_ref.shape[1]
    step = min(256, feed_ref.shape[0])
    for start in range(0, feed_ref.shape[0], step):
        here = slice(start, start + step)
        both = dot(feed_ref[here, :], pair_ref[...])
        grad_act = dot(down_in_ref[here, :], down_ref[...])
        gate, up = both[:, :tile], both[:, tile:]
        sig = jax.nn.sigmoid(gate)
        silu = gate * sig
        activated_ref[here, :] = (silu * up).astype(BF16)
        grads_ref[here, :tile] = (grad_act * up * (sig + silu * (1.0 - sig))).astype(BF16)
        grads_ref[here, tile:] = (grad_act * silu).astype(BF16)


def feed_middle(feed_in, down_in, weights, width, tile):
    rows, depth = feed_in.shape
    tiles = width // tile
    work = rows * depth * width
    return pl.pallas_call(
        feed_kernel,
        grid=(tiles,),
        in_specs=[
            pl.BlockSpec((rows, depth), lambda j: (0, 0), pipeline_mode=pl.Buffered(1)),
            pl.BlockSpec((rows, depth), lambda j: (0, 0), pipeline_mode=pl.Buffered(1)),
            pl.BlockSpec((depth, 2 * tile), lambda j: (0, j)),
            pl.BlockSpec((depth, tile), lambda j: (0, 2 * tiles + j)),
        ],
        out_specs=[
            pl.BlockSpec((rows, tile), lambda j: (0, j)),
            pl.BlockSpec((rows, 2 * tile), lambda j: (0, j)),
        ],
        out_shape=[
            jax.ShapeDtypeStruct((rows, width), BF16),
            jax.ShapeDtypeStruct((rows, 2 * width), BF16),
        ],
        compiler_params=pltpu.CompilerParams(
            dimension_semantics=("arbitrary",), vmem_limit_bytes=56 << 20
        ),
        cost_estimate=pl.CostEstimate(
            flops=6 * work,
            bytes_accessed=2 * (2 * rows * depth + 3 * depth * width + 3 * rows * width),
            transcendentals=rows * width,
        ),
        name="feed_middle",
    )(feed_in, down_in, weights, weights)


def spread_kernel(*refs, count):
    total = sum(dot(refs[i][...], refs[count + i][...], NT) for i in range(count))
    total = total.astype(BF16)
    start = 0
    for out in refs[2 * count :]:
        out[...] = total[start : start + out.shape[0]]
        start += out.shape[0]


def spread_rows(lefts, weights, places, tile):
    rows = lefts[0].shape[0]
    depth = weights[0].shape[0]
    widths = [left.shape[1] for left in lefts]
    work = rows * depth * sum(widths)
    outs = [rows // 2, rows // 4, rows // 4] if square() else [rows]

    def weight_spec(width, place):
        return pl.BlockSpec((tile, width), lambda j: (j, place))

    return pl.pallas_call(
        functools.partial(spread_kernel, count=len(lefts)),
        grid=(depth // tile,),
        in_specs=[
            pl.BlockSpec((rows, width), lambda j: (0, 0), pipeline_mode=pl.Buffered(1))
            for width in widths
        ]
        + [weight_spec(width, place) for width, place in zip(widths, places)],
        out_specs=[pl.BlockSpec((each, tile), lambda j: (0, j)) for each in outs],
        out_shape=[jax.ShapeDtypeStruct((each, depth), BF16) for each in outs],
        compiler_params=pltpu.CompilerParams(
            dimension_semantics=("arbitrary",), vmem_limit_bytes=56 << 20
        ),
        cost_estimate=pl.CostEstimate(
            flops=2 * work,
            bytes_accessed=2 * ((rows + depth) * sum(widths) + rows * depth),
            transcendentals=0,
        ),
        name="spread_rows",
    )(*lefts, *weights)


def token_kernel(*refs, seqs, pair_tiles):
    feeds, downs, pairs, acts = (refs[at * seqs : (at + 1) * seqs] for at in range(4))
    column = pl.program_id(0)

    @pl.when(column < pair_tiles)
    def _():
        total = sum(dot(left[...], right[...], TN) for left, right in zip(feeds, pairs))
        refs[-1][...] = total.astype(BF16)

    @pl.when(column >= pair_tiles)
    def _():
        total = sum(dot(left[...], right[...], TN) for left, right in zip(downs, acts))
        refs[-1][...] = total.astype(BF16)


def feed_grads(feeds, downs, pairs, acts, tile):
    seqs = len(feeds)
    rows, depth = feeds[0].shape
    pair_tiles, act_tiles = pairs[0].shape[1] // tile, acts[0].shape[1] // tile
    step = min(512, depth)
    columns = (pair_tiles + act_tiles) * tile
    left_pair = pl.BlockSpec((rows, step), lambda j, i: (0, jnp.where(j < pair_tiles, i, 0)))
    left_act = pl.BlockSpec((rows, step), lambda j, i: (0, jnp.where(j < pair_tiles, 0, i)))
    pair = pl.BlockSpec((rows, tile), lambda j, i: (0, jnp.minimum(j, pair_tiles - 1)))
    act = pl.BlockSpec((rows, tile), lambda j, i: (0, jnp.maximum(j - pair_tiles, 0)))
    work = seqs * rows * depth * columns
    return pl.pallas_call(
        functools.partial(token_kernel, seqs=seqs, pair_tiles=pair_tiles),
        grid=(pair_tiles + act_tiles, depth // step),
        in_specs=[left_pair] * seqs + [left_act] * seqs + [pair] * seqs + [act] * seqs,
        out_specs=pl.BlockSpec((step, tile), lambda j, i: (i, j)),
        out_shape=jax.ShapeDtypeStruct((depth, columns), BF16),
        compiler_params=pltpu.CompilerParams(
            dimension_semantics=("arbitrary", "arbitrary"), vmem_limit_bytes=56 << 20
        ),
        cost_estimate=pl.CostEstimate(
            flops=2 * work,
            bytes_accessed=2 * (2 * seqs * rows * depth + (seqs * rows + depth) * columns),
            transcendentals=0,
        ),
        name="feed_grads",
    )(*feeds, *downs, *pairs, *acts)


def lay_kernel(place_ref, *refs, plan, inputs):
    outs = refs[inputs:]
    for source, member, start, width, target, at in plan:
        each = outs[target].shape[1] // 4
        where = pl.ds(pl.multiple_of(place_ref[member] * each + at, LANES), width)
        outs[target][:, where] = refs[source][:, start : start + width].astype(F32)


def lay_out(received, pieces, widths):
    blocks = [block for group in received for block in group]
    rows = blocks[0].shape[0]
    plan = [
        (4 * group + member, member, start, width, target, at)
        for group, start, width, target, at in pieces
        for member in range(4)
    ]
    return pl.pallas_call(
        functools.partial(lay_kernel, plan=plan, inputs=len(blocks)),
        grid_spec=pltpu.PrefetchScalarGridSpec(
            num_scalar_prefetch=1,
            grid=(1,),
            in_specs=[pl.BlockSpec(block.shape, lambda i, p: (0, 0)) for block in blocks],
            out_specs=[pl.BlockSpec((rows, 4 * width), lambda i, p: (0, 0)) for width in widths],
        ),
        out_shape=[jax.ShapeDtypeStruct((rows, 4 * width), F32) for width in widths],
        compiler_params=pltpu.CompilerParams(vmem_limit_bytes=48 << 20),
        name="lay_out",
    )(lax.axis_index("ctx") ^ jnp.arange(4, dtype=jnp.int32), *blocks)


def norm_forward(values):
    inverse_rms = lax.rsqrt(jnp.mean(values * values, axis=-1, keepdims=True) + EPS)
    return (values * inverse_rms, inverse_rms)


def norm_backward(grad_normed, normed, inverse_rms, gain):
    grad_hat = grad_normed * gain
    grad_input = inverse_rms * (
        grad_hat - normed * jnp.mean(grad_hat * normed, axis=-1, keepdims=True)
    )
    return (grad_input, jnp.sum(grad_normed * normed, axis=0))


def rope_lanes(length):
    half = HEAD_SIZE // 2
    frequency = jnp.exp(
        jnp.arange(half, dtype=F32) * (-2.0 * math.log(THETA) / HEAD_SIZE)
    )
    angles = jnp.arange(length, dtype=jnp.int32).astype(F32)[:, None] * frequency[None, :]
    cosine, sine = jnp.cos(angles), jnp.sin(angles)
    return (
        jnp.concatenate([cosine] * 4, axis=1),
        jnp.concatenate([-sine, sine, -sine, sine], axis=1),
    )


def pad_columns(array, width):
    return jnp.pad(array, ((0, 0), (0, width - array.shape[1])))


def body(
    tokens, span_order, out_grad, first_gain, query_weight, key_matrix, value_matrix,
    merge_weight, second_gain, gate_weight, up_weight, down_weight,
):
    seqs, own_rows, depth = tokens.shape
    ctx = lax.axis_size("ctx")
    rank = lax.axis_index("ctx")
    length = own_rows * ctx
    spans = span_order.shape[1]
    weight_rows = gate_weight.shape[0]
    group_size = query_weight.shape[1] // key_matrix.shape[1]
    query_width = query_weight.shape[1] // ctx
    own_key_width = key_matrix.shape[1] // ctx
    key_width = -(-own_key_width // LANES) * LANES
    feed_width = gate_weight.shape[1] // ctx
    tile = min(512, feed_width)
    tiles = feed_width // tile
    first = max(1, 3 * tiles // 4)
    chunks = [first * tile] + ([(tiles - first) * tile] if tiles > first else [])
    starts = [0, chunks[0]][: len(chunks)]
    chain = Chain()

    def columns(weight, t, width, at=0):
        return lax.dynamic_slice_in_dim(weight, t * (weight.shape[1] // ctx) + at, width, axis=1)

    gain_columns = pad_columns(jnp.stack([first_gain, second_gain], axis=1), LANES)

    def projections_for(t):
        return jnp.concatenate(
            [
                columns(query_weight, t, query_width),
                pad_columns(columns(key_matrix, t, own_key_width), key_width),
                pad_columns(columns(value_matrix, t, own_key_width), key_width),
                gain_columns,
            ],
            axis=1,
        )

    def feed_for(part):
        def of(t):
            pieces = []
            for start in range(starts[part], starts[part] + chunks[part], tile):
                pieces += [
                    columns(gate_weight, t, tile, start),
                    columns(up_weight, t, tile, start),
                ]
            pieces.append(columns(down_weight, t, chunks[part], starts[part]))
            return jnp.concatenate(pieces, axis=1)

        return of

    assert seqs == 2 and len(chunks) <= 2
    many = len(chunks) > 1
    qkv_width = query_width + 2 * key_width

    slots = jnp.argsort(span_order, axis=1).astype(jnp.int32)
    if square():
        places = [HALVES.index((member, half)) for member in range(4) for half in range(2)]
        slots = jnp.array(places, jnp.int32)[((slots // 2) ^ rank) * 2 + slots % 2]
    cos_lanes, sin_lanes = rope_lanes(length)

    def project(own, near, far, weight, gain):
        rows = gathered(own, near, far)
        normed, _ = norm_forward(rows.astype(F32))
        attn_in = (normed * gain).astype(BF16)
        return rows, attn_in, dot(attn_in, weight)

    def attend(qkv, slots):
        return attention_forward(
            qkv, slots, cos_lanes, sin_lanes, query_width, key_width, group_size
        )

    def merge_back(rows, weight):
        return spread_rows([rows], [weight], [0], tile)

    def feed_norm(rows, branch, near, far, gain):
        hidden = rows.astype(F32) + scattered(branch, near, far)
        normed, _ = norm_forward(hidden)
        return hidden, (normed * gain).astype(BF16)

    def middle_of(feed_in, down_in, weights, part):
        return feed_middle(feed_in, down_in, weights, chunks[part], tile)

    def feed_back(grads, weights):
        return spread_rows(grads, weights, [0] * len(grads), tile)

    def feed_out(activated, weights):
        return spread_rows(activated, weights, [2] * len(activated), tile)

    def token_grads(left, right):
        return dot(jnp.concatenate(left, axis=0), jnp.concatenate(right, axis=0), TN, BF16)

    def feed_grads_of(feed_in, down_in, middle, part):
        return feed_grads(
            feed_in, down_in, [m[1] for m in middle], [m[0] for m in middle], chunks[part]
        )

    def feed_norm_back(hidden, parts, near, far, cot, gain):
        normed, inverse = norm_forward(hidden)
        grad_middle, gain_part = norm_backward(
            scattered(parts, near, far), normed, inverse, gain
        )
        grad_hidden = cot.astype(F32) + grad_middle
        return grad_hidden, grad_hidden.astype(BF16), gain_part

    def attend_back(own, near, far, weight, kept, slots):
        merge_in = gathered(own, near, far)
        grad_attn = dot(merge_in, weight, NN, BF16)
        parts = attention_backward(kept, grad_attn, slots, cos_lanes, sin_lanes, group_size)
        return merge_in, jnp.concatenate(parts, axis=1)

    def project_back(grads, weight):
        return spread_rows([grads], [weight], [0], tile)

    def gain_part_of(rows, lower):
        normed, _ = norm_forward(rows.astype(F32))
        total, start = 0.0, 0
        for part in lower:
            here = slice(start, start + part.shape[0])
            total = total + jnp.sum(normed[here] * part.astype(F32), axis=0)
            start += part.shape[0]
        return total

    def attention_grads_of(attn_in, grad_qkv, merge_in, attn_out, rows, lower, gain_two_parts):
        gain_one_sum = sum(gain_part_of(r, l) for r, l in zip(rows, lower))
        gains = jnp.stack([gain_one_sum, sum(gain_two_parts)], axis=1)
        return jnp.concatenate(
            [
                token_grads(attn_in, grad_qkv),
                token_grads(merge_in, attn_out),
                pad_columns(gains.astype(BF16), LANES),
            ],
            axis=1,
        )

    def project_norm_back(rows, parts, near, far, grad_hidden, gain):
        normed, inverse = norm_forward(rows.astype(F32))
        grad_lower, _ = norm_backward(scattered(parts, near, far), normed, inverse, gain)
        return grad_hidden + grad_lower

    def block_of(hidden, parts, near, far):
        return (hidden + scattered(parts, near, far)).astype(BF16)

    def only(*values):
        return values

    moved = chain.exchange(projections_for)
    a_near = chain.gather_near(tokens[0])
    projections = chain.all_rows(moved)
    moved = chain.exchange(lambda t: columns(merge_weight, t, query_width))
    merge = chain.all_rows(moved)
    a_far = chain.gather_far(a_near)
    moved = chain.exchange(feed_for(0))
    chain.wait(*a_far)
    b_near = chain.gather_near(tokens[1])
    gains = projections[:, qkv_width : qkv_width + 2].astype(F32)
    gain_one, gain_two = gains[:, 0], gains[:, 1]
    rows_a, attn_in_a, qkv = chain.run(
        project, tokens[0], a_near, a_far, projections[:, :qkv_width], gain_one
    )
    feeds = [chain.all_rows(moved)]
    attn_out_a, *kept_a = chain.run(attend, qkv, slots[0])
    b_far = chain.gather_far(b_near)
    branch_a = chain.run(merge_back, attn_out_a, merge)
    near_a = chain.scatter_near(branch_a)
    chain.wait(*b_far)
    rows_b, attn_in_b, qkv = chain.run(
        project, tokens[1], b_near, b_far, projections[:, :qkv_width], gain_one
    )
    far_a = chain.scatter_far(branch_a, near_a)
    cot_a_near = chain.gather_near(out_grad[0])
    attn_out_b, *kept_b = chain.run(attend, qkv, slots[1])
    chain.wait(*far_a)
    hidden_a, feed_a = chain.run(feed_norm, tokens[0], branch_a, near_a, far_a, gain_two)
    feed_a_near = chain.gather_near(feed_a)
    branch_b = chain.run(merge_back, attn_out_b, merge)
    chain.wait(*cot_a_near)
    if many:
        moved = chain.exchange(feed_for(1))
    cot_a_far = chain.gather_far(cot_a_near)
    near_b = chain.scatter_near(branch_b)
    feed_a_far = chain.gather_far(feed_a_near)
    chain.wait(*cot_a_far)
    down_in_a = chain.run(gathered, out_grad[0], cot_a_near, cot_a_far)
    if many:
        feeds.append(chain.all_rows(moved))
    far_b = chain.scatter_far(branch_b, near_b)
    chain.wait(*feed_a_far)
    cot_b_near = chain.gather_near(out_grad[1])
    feed_in_a = chain.run(gathered, feed_a, feed_a_near, feed_a_far)
    middle_a = [chain.run(lambda f, d, w: middle_of(f, d, w, 0), feed_in_a, down_in_a, feeds[0])]
    chain.wait(*far_b)
    hidden_b, feed_b = chain.run(feed_norm, tokens[1], branch_b, near_b, far_b, gain_two)
    feed_b_near = chain.gather_near(feed_b)
    cot_b_far = chain.gather_far(cot_b_near)
    if many:
        middle_a.append(
            chain.run(lambda f, d, w: middle_of(f, d, w, 1), feed_in_a, down_in_a, feeds[1])
        )
    feed_b_far = chain.gather_far(feed_b_near)
    back_a = chain.run(feed_back, [m[1] for m in middle_a], feeds)
    near_a = chain.scatter_near(back_a)
    chain.wait(*cot_b_far, *feed_b_far)
    down_in_b = chain.run(gathered, out_grad[1], cot_b_near, cot_b_far)
    feed_in_b = chain.run(gathered, feed_b, feed_b_near, feed_b_far)
    middle_b = [chain.run(lambda f, d, w: middle_of(f, d, w, 0), feed_in_b, down_in_b, feeds[0])]
    far_a = chain.scatter_far(back_a, near_a)
    grads_first = chain.run(
        lambda f, d, m: feed_grads_of(f, d, m, 0),
        [feed_in_a, feed_in_b], [down_in_a, down_in_b], [middle_a[0], middle_b[0]],
    )
    chain.wait(*far_a)
    sums = [sum_over_dp(*chain.run(only, grads_first))]
    grad_hidden_a, merge_a, gain_two_a = chain.run(
        feed_norm_back, hidden_a, back_a, near_a, far_a, out_grad[0], gain_two
    )
    merge_a_near = chain.gather_near(merge_a)
    if many:
        middle_b.append(
            chain.run(lambda f, d, w: middle_of(f, d, w, 1), feed_in_b, down_in_b, feeds[1])
        )
    merge_a_far = chain.gather_far(merge_a_near)
    back_b = chain.run(feed_back, [m[1] for m in middle_b], feeds)
    near_b = chain.scatter_near(back_b)
    chain.wait(*merge_a_far)
    merge_in_a, grad_qkv_a = chain.run(
        attend_back, merge_a, merge_a_near, merge_a_far, merge, kept_a, slots[0]
    )
    far_b = chain.scatter_far(back_b, near_b)
    lower_a = chain.run(project_back, grad_qkv_a, projections)
    lower_a_near = chain.scatter_near(lower_a)
    out_a = chain.run(feed_out, [m[0] for m in middle_a], feeds)
    chain.wait(*far_b)
    grad_hidden_b, merge_b, gain_two_b = chain.run(
        feed_norm_back, hidden_b, back_b, near_b, far_b, out_grad[1], gain_two
    )
    merge_b_near = chain.gather_near(merge_b)
    lower_a_far = chain.scatter_far(lower_a, lower_a_near)
    if many:
        grads_last = chain.run(
            lambda f, d, m: feed_grads_of(f, d, m, 1),
            [feed_in_a, feed_in_b], [down_in_a, down_in_b], [middle_a[1], middle_b[1]],
        )
    merge_b_far = chain.gather_far(merge_b_near)
    out_a_near = chain.scatter_near(out_a)
    chain.wait(*lower_a_far)
    input_grad_a = chain.run(
        project_norm_back, tokens[0], lower_a, lower_a_near, lower_a_far, grad_hidden_a, gain_one
    )
    out_b = chain.run(feed_out, [m[0] for m in middle_b], feeds)
    chain.wait(*merge_b_far)
    if many:
        chain.wait(sums[0])
        sums.append(sum_over_dp(*chain.run(only, grads_last)))
    out_a_far = chain.scatter_far(out_a, out_a_near)
    out_b_near = chain.scatter_near(out_b)
    merge_in_b, grad_qkv_b = chain.run(
        attend_back, merge_b, merge_b_near, merge_b_far, merge, kept_b, slots[1]
    )
    lower_b = chain.run(project_back, grad_qkv_b, projections)
    lower_b_near = chain.scatter_near(lower_b)
    chain.wait(*out_a_far)
    block_a = chain.run(block_of, hidden_a, out_a, out_a_near, out_a_far)
    out_b_far = chain.scatter_far(out_b, out_b_near)
    attention_grads = chain.run(
        attention_grads_of,
        [attn_in_a, attn_in_b],
        [grad_qkv_a, grad_qkv_b],
        [merge_in_a, merge_in_b],
        [attn_out_a, attn_out_b],
        [rows_a, rows_b],
        [lower_a, lower_b],
        [gain_two_a, gain_two_b],
    )
    chain.wait(sums[-1])
    attention_sums = sum_over_dp(*chain.run(only, attention_grads))
    lower_b_far = chain.scatter_far(lower_b, lower_b_near)
    moved_feed = [chain.own_rows(sums[0])]
    chain.wait(*out_b_far)
    block_b = chain.run(block_of, hidden_b, out_b, out_b_near, out_b_far)
    chain.wait(*lower_b_far)
    input_grad_b = chain.run(
        project_norm_back, tokens[1], lower_b, lower_b_near, lower_b_far, grad_hidden_b, gain_one
    )
    chain.wait(*moved_feed[0][1:])
    moved_feed += [chain.own_rows(part) for part in sums[1:]]
    chain.wait(*moved_feed[-1][1:])
    blocks = [block_a, block_b]
    input_grad = [input_grad_a, input_grad_b]

    key_at, value_at = query_width, query_width + key_width
    merge_at, gain_at = qkv_width, qkv_width + query_width
    feed_pieces = [
        (part, 2 * width + at * tile if kind == 2 else (2 * at + kind) * tile, tile, kind,
         starts[part] + at * tile)
        for part, width in enumerate(chunks)
        for at in range(width // tile)
        for kind in range(3)
    ]
    attention_pieces = [
        (0, 0, query_width, 0, 0),
        (0, key_at, own_key_width, 1, 0),
        (0, value_at, own_key_width, 2, 0),
        (0, merge_at, query_width, 3, 0),
    ]

    def results(received, pieces, widths):
        if square():
            return lay_out(received, pieces, widths)
        columns_of = [[] for _ in widths]
        for group, start, width, target, at in sorted(pieces, key=lambda piece: piece[4]):
            columns_of[target].append(received[group][0][:, :, start : start + width])
        return [
            jnp.concatenate(parts, axis=2)
            .astype(F32)
            .transpose(1, 0, 2)
            .reshape(weight_rows, -1)
            for parts in columns_of
        ]

    gate_total, up_total, down_total = chain.run(
        lambda *received: results(received, feed_pieces, [feed_width] * 3),
        *moved_feed,
    )
    moved = chain.own_rows(attention_sums)
    chain.wait(*moved[1:])
    query_total, key_total, value_total, merge_total = chain.run(
        lambda received: results(
            [received], attention_pieces, [query_width, own_key_width, own_key_width, query_width]
        ),
        moved,
    )
    gain_totals = sum(block[..., gain_at : gain_at + 2].astype(F32) for block in moved)
    if not square():
        gain_totals = jnp.sum(gain_totals, axis=0)
    return (
        jnp.stack(blocks),
        jnp.stack(input_grad),
        gain_totals[:, 0],
        query_total,
        key_total,
        value_total,
        merge_total,
        gain_totals[:, 1],
        gate_total,
        up_total,
        down_total,
    )


def solution(mesh):
    rows = P(("dp", "ctx"), None)
    vector = P(("dp", "ctx"))
    acts = P("dp", "ctx", None)
    in_specs = (
        acts, P("dp", None), acts, vector, rows, rows, rows, rows, vector, rows, rows, rows,
    )
    out_specs = (acts, acts, vector, rows, rows, rows, rows, vector, rows, rows, rows)
    return jax.shard_map(body, mesh=mesh, in_specs=in_specs, out_specs=out_specs, check_vma=False)
```

```python
import functools
import math

import jax
import jax.numpy as jnp
from jax import lax
from jax.experimental import pallas as pl
from jax.experimental.pallas import tpu as pltpu
from jax.sharding import PartitionSpec as P

HEAD_SIZE = 64
LANES = 128
EPS = 1e-05
THETA = 500000.0
QUERY_BLOCK = 256
F32 = jnp.float32
BF16 = jnp.bfloat16

NN = (((1,), (0,)), ((), ()))
NT = (((1,), (1,)), ((), ()))
TN = (((0,), (0,)), ((), ()))


def dot(left, right, dims=NN, out=F32):
    return lax.dot_general(left, right, dims, preferred_element_type=F32).astype(out)


class Chain:
    def __init__(self):
        self.last = ()

    def after(self, values):
        values = tuple(values)
        if not self.last:
            return values
        return lax.optimization_barrier(values + self.last)[: len(values)]

    def run(self, function, *args):
        leaves, tree = jax.tree.flatten(args)
        out = function(*jax.tree.unflatten(tree, self.after(leaves)))
        self.last = tuple(jax.tree.leaves(out))
        return out

    def wait(self, *arrays):
        self.last = self.last + arrays


    def send(self, *sends):
        blocks = self.after(block for block, _ in sends)
        return [
            lax.ppermute(block, "ctx", [(i, i ^ bits) for i in range(4)])
            for block, (_, bits) in zip(blocks, sends)
        ]

    def gather_near(self, own):
        return self.send((own, 1), (own, 2)) if square() else []

    def gather_far(self, near):
        if not square():
            return []
        self.wait(*near)
        half = near[0].shape[0] // 2
        one, two = self.after(near)
        return self.send((one[:half], 2), (two[half:], 1))

    def scatter_near(self, parts):
        return self.send((parts[1], 1), (parts[2], 2)) if square() else []

    def scatter_far(self, parts, near):
        if not square():
            return []

        def add(own, one, two):
            half = one.shape[0] // 2
            for_one = own[2 * half : 3 * half].astype(F32) + two[half:].astype(F32)
            for_two = own[3 * half :].astype(F32) + one[half:].astype(F32)
            return for_one.astype(BF16), for_two.astype(BF16)

        self.wait(*near)
        for_one, for_two = self.run(add, parts[0], *near)
        return self.send((for_one, 1), (for_two, 2))

    def exchange(self, block_for):
        size = lax.axis_size("ctx")
        rank = lax.axis_index("ctx")
        if not square():
            stacked = jnp.stack([block_for(t) for t in range(size)])
            return [lax.all_to_all(stacked, "ctx", 0, 0)]
        return [block_for(rank)] + self.send(*[(block_for(rank ^ m), m) for m in (1, 2, 3)])

    def exchanged(self, received):
        if not square():
            return received[0]
        rank = lax.axis_index("ctx")
        self.wait(*received[1:])

        def lay(*received):
            out = jnp.zeros((4,) + received[0].shape, received[0].dtype)
            for member, value in enumerate(received):
                out = lax.dynamic_update_index_in_dim(out, value, rank ^ member, 0)
            return out

        return self.run(lay, *received)

    def all_rows(self, received):
        mine = self.exchanged(received)
        return lax.all_gather(
            mine.reshape(-1, mine.shape[-1]), "dp", axis=0, tiled=True
        )

    def own_rows(self, summed):
        rows = summed.shape[0] // lax.axis_size("ctx")
        self.wait(summed)
        return self.exchange(lambda t: lax.dynamic_slice_in_dim(summed, t * rows, rows, axis=0))


def square():
    return lax.axis_size("ctx") == 4


HALVES = ((0, 0), (0, 1), (1, 1), (2, 0), (1, 0), (3, 0), (2, 1), (3, 1))


def pieces_of(own, near, far):
    rows = own.shape[0]
    if not square():
        whole = gathered(own, near, far)
        return [whole], [(0, 0, whole.shape[0], 0)]
    half = rows // 2
    sources = [own, *near, *far]
    plan = []
    for at, (member, part) in enumerate(HALVES):
        if member == 3:
            plan.append((3 + part, 0, half, at * half))
        else:
            plan.append((member, part * half, half, at * half))
    return sources, plan


def gathered(own, near, far):
    if not square():
        return lax.all_gather(own, "ctx", axis=0, tiled=True)
    half = own.shape[0] // 2
    one, two = near
    low, high = far
    return jnp.concatenate(
        [own, one[half:], two[:half], one[:half], low, two[half:], high], axis=0
    )


def scattered(parts, near, far):
    if not square():
        return lax.psum_scatter(parts[0], "ctx", scatter_dimension=0, tiled=True).astype(F32)
    half = near[0].shape[0] // 2
    low = parts[0][:half].astype(F32) + near[0][:half].astype(F32) + far[1].astype(F32)
    high = parts[0][half : 2 * half].astype(F32) + near[1][:half].astype(F32) + far[0].astype(F32)
    return jnp.concatenate([low, high], axis=0)


def sum_over_dp(grads):
    return lax.psum_scatter(grads, "dp", scatter_dimension=0, tiled=True)


def swap_halves(rows):
    lane = lax.broadcasted_iota(jnp.int32, rows.shape, 1)
    return jnp.where(
        lane % HEAD_SIZE < HEAD_SIZE // 2,
        pltpu.roll(rows, LANES - HEAD_SIZE // 2, 1),
        pltpu.roll(rows, HEAD_SIZE // 2, 1),
    )


def both_halves(rows, half):
    lane = lax.broadcasted_iota(jnp.int32, rows.shape, 1)
    kept = jnp.where(lane // HEAD_SIZE == half, rows.astype(F32), 0.0)
    return (kept + pltpu.roll(kept, HEAD_SIZE, 1)).astype(BF16)


def two_heads(rows):
    lane = lax.broadcasted_iota(jnp.int32, rows.shape, 1)
    wide = rows.astype(F32)
    first = jnp.where(lane < HEAD_SIZE, wide, 0.0)
    second = jnp.where(lane < HEAD_SIZE, 0.0, wide)
    return jnp.concatenate([first, second], axis=0).astype(BF16)


def visible(size):
    key = lax.broadcasted_iota(jnp.int32, (size, 2 * size), 0)
    query = lax.broadcasted_iota(jnp.int32, (size, 2 * size), 1) % size
    return key <= query


def attention_forward_kernel(
    slot_ref, q_ref, k_ref, v_ref, cos_ref, sin_ref,
    out_ref, queries_ref, keys_ref, values_ref, total_ref, key_both, value_turned,
    *, span, pairs_of_head, pairs_of_block
):
    pair = pl.program_id(0)
    length = q_ref.shape[0]
    spans = length // span
    block = QUERY_BLOCK

    def place(index):
        return pl.ds(pl.multiple_of(slot_ref[index] * span, span), span)

    def turned(source, index):
        here = slice(index * span, (index + 1) * span)
        rows = source[place(index), :]
        return rows * cos_ref[here, :] + swap_halves(rows) * sin_ref[here, :]

    for index in range(spans):
        here = slice(index * span, (index + 1) * span)
        queries_ref[here, :] = turned(q_ref, index).astype(BF16)

    @pl.when(pair % pairs_of_block == 0)
    def _():
        for index in range(spans):
            here = slice(index * span, (index + 1) * span)
            keys_ref[here, :] = turned(k_ref, index).astype(BF16)
            values_ref[here, :] = v_ref[place(index), :].astype(BF16)

    @pl.when(pair % pairs_of_head == 0)
    def _():
        half = (pair // pairs_of_head) % 2
        key_both[...] = both_halves(keys_ref[...], half)
        value_both = both_halves(values_ref[...], half)
        value_turned[...] = value_both.astype(F32).T[:HEAD_SIZE].astype(BF16)

    mask = visible(block)
    for index in range(length // block):
        low, high = index * block, (index + 1) * block
        wide = two_heads(queries_ref[low:high, :] * jnp.asarray(HEAD_SIZE**-0.5, BF16))
        diagonal = jnp.where(mask, dot(key_both[low:high, :], wide, NT), -1e30)
        top = jnp.max(diagonal, axis=0, keepdims=True)
        if index:
            before = dot(key_both[:low, :], wide, NT)
            top = jnp.maximum(top, jnp.max(before, axis=0, keepdims=True))
        near = jnp.exp(diagonal - top)
        total = jnp.sum(near, axis=0, keepdims=True)
        attended = dot(value_turned[:, low:high], near.astype(BF16))
        if index:
            far = jnp.exp(before - top)
            total = total + jnp.sum(far, axis=0, keepdims=True)
            attended = attended + dot(value_turned[:, :low], far.astype(BF16))
        total_ref[0, index : index + 1, :] = top + jnp.log(total)
        attended = attended / total
        rows = jnp.concatenate([attended[:, :block], attended[:, block:]], axis=0).T.astype(BF16)
        for part in range(block // span):
            out_ref[place(index * (block // span) + part), :] = rows[
                part * span : (part + 1) * span
            ]


def attention_backward_kernel(
    slot_ref, queries_ref, keys_ref, values_ref, total_ref, grad_ref, cos_ref, sin_ref,
    grad_q_ref, grad_k_ref, grad_v_ref, key_both, value_both, key_turned, key_sum, value_sum,
    *, span, pairs_of_head
):
    pair = pl.program_id(0)
    length = queries_ref.shape[0]
    spans = length // span
    block = QUERY_BLOCK
    each = block // span
    half = (pair // pairs_of_head) % 2

    def place(index):
        return pl.ds(pl.multiple_of(slot_ref[index] * span, span), span)

    def turned_back(rows, index):
        here = slice(index * span, (index + 1) * span)
        return rows * cos_ref[here, :] - swap_halves(rows) * sin_ref[here, :]

    @pl.when(pair % pairs_of_head == 0)
    def _():
        key_both[...] = both_halves(keys_ref[...], half)
        value_both[...] = both_halves(values_ref[...], half)
        key_turned[...] = key_both[...].astype(F32).T[:HEAD_SIZE].astype(BF16)
        key_sum[...] = jnp.zeros_like(key_sum)
        value_sum[...] = jnp.zeros_like(value_sum)

    mask = visible(block)
    for index in range(length // block):
        low, high = index * block, (index + 1) * block
        wide = two_heads(queries_ref[low:high, :] * jnp.asarray(HEAD_SIZE**-0.5, BF16))
        grad = two_heads(
            jnp.concatenate(
                [grad_ref[place(index * each + part), :] for part in range(each)], axis=0
            )
        )
        total = total_ref[0, index : index + 1, :]
        ranges = [(low, high)] + ([(0, low)] if index else [])
        probs, grad_probs, row_dot = [], [], 0.0
        for start, stop in ranges:
            scores = dot(key_both[start:stop, :], wide, NT)
            if start == low:
                scores = jnp.where(mask, scores, -1e30)
            prob = jnp.exp(scores - total)
            grad_prob = dot(value_both[start:stop, :], grad, NT)
            row_dot = row_dot + jnp.sum(prob * grad_prob, axis=0, keepdims=True)
            probs.append(prob)
            grad_probs.append(grad_prob)
        turned = 0.0
        for (start, stop), prob, grad_prob in zip(ranges, probs, grad_probs):
            grad_score = (prob * (grad_prob - row_dot)).astype(BF16)
            value_sum[start:stop, :] += dot(prob.astype(BF16), grad)
            key_sum[start:stop, :] += dot(grad_score, wide)
            turned = turned + dot(key_turned[:, start:stop], grad_score)
        turned = turned * HEAD_SIZE**-0.5
        rows = jnp.concatenate([turned[:, :block], turned[:, block:]], axis=0).T
        for part in range(each):
            at = index * each + part
            grad_q_ref[place(at), :] = turned_back(
                rows[part * span : (part + 1) * span], at
            ).astype(BF16)

    @pl.when(pair % pairs_of_head == pairs_of_head - 1)
    def _():
        for index in range(spans):
            here = slice(index * span, (index + 1) * span)
            key_rows, value_rows = key_sum[here, :], value_sum[here, :]
            key_rows = turned_back(key_rows + pltpu.roll(key_rows, HEAD_SIZE, 1), index)
            value_rows = value_rows + pltpu.roll(value_rows, HEAD_SIZE, 1)
            lane = lax.broadcasted_iota(jnp.int32, key_rows.shape, 1)
            for target, rows in ((grad_k_ref, key_rows), (grad_v_ref, value_rows)):
                old = target[place(index), :].astype(F32)
                keep = (lane < HEAD_SIZE) & (half == 1)
                target[place(index), :] = jnp.where(keep, old, rows).astype(BF16)


def attention_sizes(query_width, group_size):
    pairs = query_width // LANES
    pairs_of_head = group_size // 2
    return pairs, pairs_of_head, 2 * pairs_of_head


def attention_forward(qkv, slots, cos_lanes, sin_lanes, query_width, key_width, group_size):
    length = qkv.shape[0]
    pairs, pairs_of_head, pairs_of_block = attention_sizes(query_width, group_size)
    key_at, value_at = query_width // LANES, (query_width + key_width) // LANES
    tile = (length, LANES)
    by_pair = pl.BlockSpec(tile, lambda p, s: (0, p))
    by_block = pl.BlockSpec(tile, lambda p, s: (0, p // pairs_of_block))
    whole = pl.BlockSpec(tile, lambda p, s: (0, 0))
    blocks = length // QUERY_BLOCK
    work = 2 * query_width * length * length
    return pl.pallas_call(
        functools.partial(
            attention_forward_kernel,
            span=length // slots.shape[0],
            pairs_of_head=pairs_of_head,
            pairs_of_block=pairs_of_block,
        ),
        grid_spec=pltpu.PrefetchScalarGridSpec(
            num_scalar_prefetch=1,
            grid=(pairs,),
            in_specs=[
                by_pair,
                pl.BlockSpec(tile, lambda p, s: (0, key_at + p // pairs_of_block)),
                pl.BlockSpec(tile, lambda p, s: (0, value_at + p // pairs_of_block)),
                whole,
                whole,
            ],
            out_specs=[
                by_pair,
                by_pair,
                by_block,
                by_block,
                pl.BlockSpec((1, blocks, 2 * QUERY_BLOCK), lambda p, s: (p, 0, 0)),
            ],
            scratch_shapes=[pltpu.VMEM(tile, BF16), pltpu.VMEM((HEAD_SIZE, length), BF16)],
        ),
        out_shape=[
            jax.ShapeDtypeStruct((length, query_width), BF16),
            jax.ShapeDtypeStruct((length, query_width), BF16),
            jax.ShapeDtypeStruct((length, key_width), BF16),
            jax.ShapeDtypeStruct((length, key_width), BF16),
            jax.ShapeDtypeStruct((pairs, blocks, 2 * QUERY_BLOCK), F32),
        ],
        compiler_params=pltpu.CompilerParams(
            dimension_semantics=("arbitrary",), vmem_limit_bytes=48 << 20
        ),
        cost_estimate=pl.CostEstimate(
            flops=8 * work, bytes_accessed=8 << 20, transcendentals=work // 128
        ),
        name="attention_forward",
    )(slots, qkv, qkv, qkv, cos_lanes, sin_lanes)


def attention_backward(kept, grad, slots, cos_lanes, sin_lanes, group_size):
    queries, keys, values, totals = kept
    length, query_width = queries.shape
    key_width = keys.shape[1]
    pairs, pairs_of_head, pairs_of_block = attention_sizes(query_width, group_size)
    tile = (length, LANES)
    by_pair = pl.BlockSpec(tile, lambda p, s: (0, p))
    by_block = pl.BlockSpec(tile, lambda p, s: (0, p // pairs_of_block))
    whole = pl.BlockSpec(tile, lambda p, s: (0, 0))
    blocks = length // QUERY_BLOCK
    work = 2 * query_width * length * length
    return pl.pallas_call(
        functools.partial(
            attention_backward_kernel, span=length // slots.shape[0], pairs_of_head=pairs_of_head
        ),
        grid_spec=pltpu.PrefetchScalarGridSpec(
            num_scalar_prefetch=1,
            grid=(pairs,),
            in_specs=[
                by_pair,
                by_block,
                by_block,
                pl.BlockSpec((1, blocks, 2 * QUERY_BLOCK), lambda p, s: (p, 0, 0)),
                by_pair,
                whole,
                whole,
            ],
            out_specs=[by_pair, by_block, by_block],
            scratch_shapes=[
                pltpu.VMEM(tile, BF16),
                pltpu.VMEM(tile, BF16),
                pltpu.VMEM((HEAD_SIZE, length), BF16),
                pltpu.VMEM(tile, F32),
                pltpu.VMEM(tile, F32),
            ],
        ),
        out_shape=[
            jax.ShapeDtypeStruct((length, query_width), BF16),
            jax.ShapeDtypeStruct((length, key_width), BF16),
            jax.ShapeDtypeStruct((length, key_width), BF16),
        ],
        compiler_params=pltpu.CompilerParams(
            dimension_semantics=("arbitrary",), vmem_limit_bytes=48 << 20
        ),
        cost_estimate=pl.CostEstimate(
            flops=20 * work, bytes_accessed=8 << 20, transcendentals=work // 128
        ),
        name="attention_backward",
    )(slots, queries, keys, values, totals, grad, cos_lanes, sin_lanes)


def put_together(sources, plan, target, whole_ref, sems):
    copies = [
        pltpu.make_async_copy(
            sources[source].at[pl.ds(row, rows)], target.at[pl.ds(to, rows)], sems.at[at]
        )
        for at, (source, row, rows, to) in enumerate(plan)
    ]
    return copies, pltpu.make_async_copy(target, whole_ref, sems.at[len(plan)])


def gather_in(calls):
    for copies, _ in calls:
        for copy in copies:
            copy.start()
    for copies, out in calls:
        for copy in copies:
            copy.wait()
        out.start()


def feed_tile(feed_ref, down_in_ref, pair_ref, down_ref, activated_ref, grads_ref):
    tile = down_ref.shape[1]
    both = dot(feed_ref[...], pair_ref[...])
    grad_act = dot(down_in_ref[...], down_ref[...])
    gate, up = both[:, :tile], both[:, tile:]
    sig = jax.nn.sigmoid(gate)
    silu = gate * sig
    activated_ref[...] = (silu * up).astype(BF16)
    grads_ref[:, :tile] = (grad_act * up * (sig + silu * (1.0 - sig))).astype(BF16)
    grads_ref[:, tile:] = (grad_act * silu).astype(BF16)


def feed_kernel(*refs, plan, count):
    step = pl.program_id(0)
    feeds, downs, refs = refs[:count], refs[count : 2 * count], refs[2 * count :]
    pair_ref, down_ref, activated_ref, grads_ref, feed_out, down_out = refs[:6]
    feed_all, down_all, feed_sems, down_sems = refs[6:]
    calls = [
        put_together(feeds, plan, feed_all, feed_out, feed_sems),
        put_together(downs, plan, down_all, down_out, down_sems),
    ]

    @pl.when(step == 0)
    def _():
        gather_in(calls)

    feed_tile(feed_all, down_all, pair_ref, down_ref, activated_ref, grads_ref)

    @pl.when(step == pl.num_programs(0) - 1)
    def _():
        for _, out in calls:
            out.wait()


def feed_specs(rows, depth, width, tile):
    tiles = width // tile
    weights = [
        pl.BlockSpec((depth, 2 * tile), lambda j: (0, j)),
        pl.BlockSpec((depth, tile), lambda j: (0, 2 * tiles + j)),
    ]
    outs = [
        pl.BlockSpec((rows, tile), lambda j: (0, j)),
        pl.BlockSpec((rows, 2 * tile), lambda j: (0, j)),
    ]
    shapes = [
        jax.ShapeDtypeStruct((rows, width), BF16),
        jax.ShapeDtypeStruct((rows, 2 * width), BF16),
    ]
    work = rows * depth * width
    settings = {
        "compiler_params": pltpu.CompilerParams(
            dimension_semantics=("arbitrary",), vmem_limit_bytes=56 << 20
        ),
        "cost_estimate": pl.CostEstimate(
            flops=6 * work,
            bytes_accessed=2 * (2 * rows * depth + 3 * depth * width + 3 * rows * width),
            transcendentals=rows * width,
        ),
    }
    return weights, outs, shapes, settings


def feed_first(feed, down, weights, width, tile):
    feeds, plan = pieces_of(*feed)
    downs, _ = pieces_of(*down)
    rows, depth = sum(entry[2] for entry in plan), weights.shape[0]
    weight_specs, outs, shapes, settings = feed_specs(rows, depth, width, tile)
    anywhere = pl.BlockSpec(memory_space=pl.ANY)
    whole = jax.ShapeDtypeStruct((rows, depth), BF16)
    return pl.pallas_call(
        functools.partial(feed_kernel, plan=plan, count=len(feeds)),
        grid=(width // tile,),
        in_specs=[anywhere] * (2 * len(feeds)) + weight_specs,
        out_specs=outs + [anywhere] * 2,
        out_shape=shapes + [whole] * 2,
        scratch_shapes=[
            pltpu.VMEM((rows, depth), BF16),
            pltpu.VMEM((rows, depth), BF16),
            pltpu.SemaphoreType.DMA((len(plan) + 1,)),
            pltpu.SemaphoreType.DMA((len(plan) + 1,)),
        ],
        name="feed_first",
        **settings,
    )(*feeds, *downs, weights, weights)


def feed_middle(feed_in, down_in, weights, width, tile):
    rows, depth = feed_in.shape
    weight_specs, outs, shapes, settings = feed_specs(rows, depth, width, tile)
    resident = pl.BlockSpec((rows, depth), lambda j: (0, 0), pipeline_mode=pl.Buffered(1))
    return pl.pallas_call(
        feed_tile,
        grid=(width // tile,),
        in_specs=[resident] * 2 + weight_specs,
        out_specs=outs,
        out_shape=shapes,
        name="feed_middle",
        **settings,
    )(feed_in, down_in, weights, weights)


def rows_kernel(*refs, plan, count):
    sources, (weight_ref, out_ref, whole_ref, target, sems) = refs[:count], refs[count:]
    call = put_together(sources, plan, target, whole_ref, sems)
    gather_in([call])
    out_ref[...] = dot(target[...], weight_ref[...]).astype(BF16)
    call[1].wait()


def rows_times(own, near, far, weight):
    sources, plan = pieces_of(own, near, far)
    rows, depth = sum(entry[2] for entry in plan), weight.shape[0]
    anywhere = pl.BlockSpec(memory_space=pl.ANY)
    return pl.pallas_call(
        functools.partial(rows_kernel, plan=plan, count=len(sources)),
        in_specs=[anywhere] * len(sources) + [pl.BlockSpec(memory_space=pltpu.VMEM)],
        out_specs=[pl.BlockSpec(memory_space=pltpu.VMEM), anywhere],
        out_shape=[
            jax.ShapeDtypeStruct((rows, weight.shape[1]), BF16),
            jax.ShapeDtypeStruct((rows, depth), BF16),
        ],
        scratch_shapes=[
            pltpu.VMEM((rows, depth), BF16),
            pltpu.SemaphoreType.DMA((len(plan) + 1,)),
        ],
        compiler_params=pltpu.CompilerParams(vmem_limit_bytes=48 << 20),
        cost_estimate=pl.CostEstimate(
            flops=2 * rows * depth * weight.shape[1],
            bytes_accessed=2 * (2 * rows * depth + (rows + depth) * weight.shape[1]),
            transcendentals=0,
        ),
        name="rows_times",
    )(*sources, weight)


def spread_kernel(*refs, count, begun):
    total = sum(dot(refs[i][...], refs[count + i][...], NT) for i in range(count))
    if begun:
        total = total + refs[2 * count][...]
    start = 0
    for out in refs[2 * count + begun :]:
        out[...] = total[start : start + out.shape[0]].astype(out.dtype)
        start += out.shape[0]


def spread_rows(lefts, weights, places, tile, begun=None, whole=False):
    rows = lefts[0].shape[0]
    depth = weights[0].shape[0]
    widths = [left.shape[1] for left in lefts]
    work = rows * depth * sum(widths)
    outs = [rows // 2, rows // 4, rows // 4] if square() and not whole else [rows]
    begun = [] if begun is None else [begun]

    def weight_spec(width, place):
        return pl.BlockSpec((tile, width), lambda j: (j, place))

    return pl.pallas_call(
        functools.partial(spread_kernel, count=len(lefts), begun=len(begun)),
        grid=(depth // tile,),
        in_specs=[
            pl.BlockSpec((rows, width), lambda j: (0, 0), pipeline_mode=pl.Buffered(1))
            for width in widths
        ]
        + [weight_spec(width, place) for width, place in zip(widths, places)]
        + [pl.BlockSpec((rows, tile), lambda j: (0, j)) for _ in begun],
        out_specs=[pl.BlockSpec((each, tile), lambda j: (0, j)) for each in outs],
        out_shape=[jax.ShapeDtypeStruct((each, depth), F32 if whole else BF16) for each in outs],
        compiler_params=pltpu.CompilerParams(
            dimension_semantics=("arbitrary",), vmem_limit_bytes=56 << 20
        ),
        cost_estimate=pl.CostEstimate(
            flops=2 * work,
            bytes_accessed=2 * ((rows + depth) * sum(widths) + rows * depth),
            transcendentals=0,
        ),
        name="spread_rows",
    )(*lefts, *weights, *begun)


def token_kernel(*refs, seqs, pair_tiles):
    feeds, downs, pairs, acts = (refs[at * seqs : (at + 1) * seqs] for at in range(4))
    column = pl.program_id(0)

    @pl.when(column < pair_tiles)
    def _():
        total = sum(dot(left[...], right[...], TN) for left, right in zip(feeds, pairs))
        refs[-1][...] = total.astype(BF16)

    @pl.when(column >= pair_tiles)
    def _():
        total = sum(dot(left[...], right[...], TN) for left, right in zip(downs, acts))
        refs[-1][...] = total.astype(BF16)


def feed_grads(feeds, downs, pairs, acts, tile):
    seqs = len(feeds)
    rows, depth = feeds[0].shape
    pair_tiles, act_tiles = pairs[0].shape[1] // tile, acts[0].shape[1] // tile
    step = min(512, depth)
    columns = (pair_tiles + act_tiles) * tile
    left_pair = pl.BlockSpec((rows, step), lambda j, i: (0, jnp.where(j < pair_tiles, i, 0)))
    left_act = pl.BlockSpec((rows, step), lambda j, i: (0, jnp.where(j < pair_tiles, 0, i)))
    pair = pl.BlockSpec((rows, tile), lambda j, i: (0, jnp.minimum(j, pair_tiles - 1)))
    act = pl.BlockSpec((rows, tile), lambda j, i: (0, jnp.maximum(j - pair_tiles, 0)))
    work = seqs * rows * depth * columns
    return pl.pallas_call(
        functools.partial(token_kernel, seqs=seqs, pair_tiles=pair_tiles),
        grid=(pair_tiles + act_tiles, depth // step),
        in_specs=[left_pair] * seqs + [left_act] * seqs + [pair] * seqs + [act] * seqs,
        out_specs=pl.BlockSpec((step, tile), lambda j, i: (i, j)),
        out_shape=jax.ShapeDtypeStruct((depth, columns), BF16),
        compiler_params=pltpu.CompilerParams(
            dimension_semantics=("arbitrary", "arbitrary"), vmem_limit_bytes=56 << 20
        ),
        cost_estimate=pl.CostEstimate(
            flops=2 * work,
            bytes_accessed=2 * (2 * seqs * rows * depth + (seqs * rows + depth) * columns),
            transcendentals=0,
        ),
        name="feed_grads",
    )(*feeds, *downs, *pairs, *acts)


def two_grads_kernel(*refs, seqs):
    lefts, rights, others, more = (refs[at * seqs : (at + 1) * seqs] for at in range(4))
    gains_ref, out_ref = refs[4 * seqs :]
    width = rights[0].shape[1]
    end = width + more[0].shape[1]
    first = sum(dot(left[...], right[...], TN) for left, right in zip(lefts, rights))
    out_ref[:, :width] = first.astype(BF16)
    second = sum(dot(left[...], right[...], TN) for left, right in zip(others, more))
    out_ref[:, width:end] = second.astype(BF16)
    out_ref[:, end:] = gains_ref[...]


def two_grads(lefts, rights, others, more, gains):
    seqs = len(lefts)
    rows, depth = lefts[0].shape
    widths = [rights[0].shape[1], more[0].shape[1], gains.shape[1]]
    step = min(512, depth)
    work = seqs * rows * depth * (widths[0] + widths[1])

    def resident(array):
        return pl.BlockSpec(array.shape, lambda i: (0, 0), pipeline_mode=pl.Buffered(1))

    left = pl.BlockSpec((rows, step), lambda i: (0, i))
    return pl.pallas_call(
        functools.partial(two_grads_kernel, seqs=seqs),
        grid=(depth // step,),
        in_specs=[left] * seqs
        + [resident(array) for array in rights]
        + [left] * seqs
        + [resident(array) for array in more]
        + [pl.BlockSpec((step, widths[2]), lambda i: (i, 0))],
        out_specs=pl.BlockSpec((step, sum(widths)), lambda i: (i, 0)),
        out_shape=jax.ShapeDtypeStruct((depth, sum(widths)), BF16),
        compiler_params=pltpu.CompilerParams(
            dimension_semantics=("arbitrary",), vmem_limit_bytes=56 << 20
        ),
        cost_estimate=pl.CostEstimate(
            flops=2 * work,
            bytes_accessed=2 * (2 * seqs * rows * depth + (seqs * rows + depth) * sum(widths)),
            transcendentals=0,
        ),
        name="two_grads",
    )(*lefts, *rights, *others, *more, gains)


def lay_kernel(place_ref, *refs, plan, inputs):
    outs = refs[inputs:]
    for source, member, start, width, target, at in plan:
        each = outs[target].shape[1] // 4
        where = pl.ds(pl.multiple_of(place_ref[member] * each + at, LANES), width)
        outs[target][:, where] = refs[source][:, start : start + width].astype(F32)


def lay_out(received, pieces, widths):
    blocks = [block for group in received for block in group]
    rows = blocks[0].shape[0]
    plan = [
        (4 * group + member, member, start, width, target, at)
        for group, start, width, target, at in pieces
        for member in range(4)
    ]
    return pl.pallas_call(
        functools.partial(lay_kernel, plan=plan, inputs=len(blocks)),
        grid_spec=pltpu.PrefetchScalarGridSpec(
            num_scalar_prefetch=1,
            grid=(1,),
            in_specs=[pl.BlockSpec(block.shape, lambda i, p: (0, 0)) for block in blocks],
            out_specs=[pl.BlockSpec((rows, 4 * width), lambda i, p: (0, 0)) for width in widths],
        ),
        out_shape=[jax.ShapeDtypeStruct((rows, 4 * width), F32) for width in widths],
        compiler_params=pltpu.CompilerParams(vmem_limit_bytes=48 << 20),
        name="lay_out",
    )(lax.axis_index("ctx") ^ jnp.arange(4, dtype=jnp.int32), *blocks)


def norm_forward(values):
    inverse_rms = lax.rsqrt(jnp.mean(values * values, axis=-1, keepdims=True) + EPS)
    return (values * inverse_rms, inverse_rms)


def norm_backward(grad_normed, normed, inverse_rms, gain):
    grad_hat = grad_normed * gain
    grad_input = inverse_rms * (
        grad_hat - normed * jnp.mean(grad_hat * normed, axis=-1, keepdims=True)
    )
    return (grad_input, jnp.sum(grad_normed * normed, axis=0))


def rope_lanes(length):
    half = HEAD_SIZE // 2
    frequency = jnp.exp(
        jnp.arange(half, dtype=F32) * (-2.0 * math.log(THETA) / HEAD_SIZE)
    )
    angles = jnp.arange(length, dtype=jnp.int32).astype(F32)[:, None] * frequency[None, :]
    cosine, sine = jnp.cos(angles), jnp.sin(angles)
    return (
        jnp.concatenate([cosine] * 4, axis=1),
        jnp.concatenate([-sine, sine, -sine, sine], axis=1),
    )


def pad_columns(array, width):
    return jnp.pad(array, ((0, 0), (0, width - array.shape[1])))


def body(
    tokens, span_order, out_grad, first_gain, query_weight, key_matrix, value_matrix,
    merge_weight, second_gain, gate_weight, up_weight, down_weight,
):
    seqs, own_rows, depth = tokens.shape
    ctx = lax.axis_size("ctx")
    rank = lax.axis_index("ctx")
    length = own_rows * ctx
    spans = span_order.shape[1]
    weight_rows = gate_weight.shape[0]
    group_size = query_weight.shape[1] // key_matrix.shape[1]
    query_width = query_weight.shape[1] // ctx
    own_key_width = key_matrix.shape[1] // ctx
    key_width = -(-own_key_width // LANES) * LANES
    feed_width = gate_weight.shape[1] // ctx
    tile = min(512, feed_width)
    tiles = feed_width // tile
    first = max(1, 3 * tiles // 4)
    chunks = [first * tile] + ([(tiles - first) * tile] if tiles > first else [])
    starts = [0, chunks[0]][: len(chunks)]
    chain = Chain()

    def columns(weight, t, width, at=0):
        return lax.dynamic_slice_in_dim(weight, t * (weight.shape[1] // ctx) + at, width, axis=1)

    gain_columns = pad_columns(jnp.stack([first_gain, second_gain], axis=1), LANES)

    def projections_for(t):
        return jnp.concatenate(
            [
                columns(query_weight, t, query_width),
                pad_columns(columns(key_matrix, t, own_key_width), key_width),
                pad_columns(columns(value_matrix, t, own_key_width), key_width),
                gain_columns,
            ],
            axis=1,
        )

    def feed_for(part):
        def of(t):
            pieces = []
            for start in range(starts[part], starts[part] + chunks[part], tile):
                pieces += [
                    columns(gate_weight, t, tile, start),
                    columns(up_weight, t, tile, start),
                ]
            pieces.append(columns(down_weight, t, chunks[part], starts[part]))
            return jnp.concatenate(pieces, axis=1)

        return of

    assert seqs == 2 and len(chunks) <= 2
    many = len(chunks) > 1
    qkv_width = query_width + 2 * key_width

    slots = jnp.argsort(span_order, axis=1).astype(jnp.int32)
    if square():
        places = [HALVES.index((member, half)) for member in range(4) for half in range(2)]
        slots = jnp.array(places, jnp.int32)[((slots // 2) ^ rank) * 2 + slots % 2]
    cos_lanes, sin_lanes = rope_lanes(length)

    def project(own, near, far, weight, gain):
        rows = gathered(own, near, far)
        normed, _ = norm_forward(rows.astype(F32))
        attn_in = (normed * gain).astype(BF16)
        return rows, attn_in, dot(attn_in, weight)

    def attend(qkv, slots):
        return attention_forward(
            qkv, slots, cos_lanes, sin_lanes, query_width, key_width, group_size
        )

    def merge_back(rows, weight):
        return spread_rows([rows], [weight], [0], tile)

    def feed_norm(rows, branch, near, far, gain):
        hidden = rows.astype(F32) + scattered(branch, near, far)
        normed, _ = norm_forward(hidden)
        return hidden, (normed * gain).astype(BF16)

    def middle_first(feed, down, weights):
        return feed_first(feed, down, weights, chunks[0], tile)

    def middle_last(feed_in, down_in, weights):
        return feed_middle(feed_in, down_in, weights, chunks[1], tile)

    def feed_back(grads, weights, begun=None, whole=False):
        return spread_rows(grads, weights, [0] * len(grads), tile, begun, whole)

    def feed_out(activated, weights, begun=None, whole=False):
        return spread_rows(activated, weights, [2] * len(activated), tile, begun, whole)

    def feed_grads_of(feed_in, down_in, middle, part):
        return feed_grads(
            feed_in, down_in, [m[1] for m in middle], [m[0] for m in middle], chunks[part]
        )

    def feed_norm_back(hidden, parts, near, far, cot, gain):
        normed, inverse = norm_forward(hidden)
        grad_middle, gain_part = norm_backward(
            scattered(parts, near, far), normed, inverse, gain
        )
        grad_hidden = cot.astype(F32) + grad_middle
        return grad_hidden, grad_hidden.astype(BF16), gain_part

    def attend_back(own, near, far, weight, kept, slots):
        grad_attn, merge_in = rows_times(own, near, far, weight)
        parts = attention_backward(kept, grad_attn, slots, cos_lanes, sin_lanes, group_size)
        return merge_in, jnp.concatenate(parts, axis=1)

    def project_back(grads, weight):
        return spread_rows([grads], [weight], [0], tile)

    def gain_part_of(rows, lower):
        normed, _ = norm_forward(rows.astype(F32))
        total, start = 0.0, 0
        for part in lower:
            here = slice(start, start + part.shape[0])
            total = total + jnp.sum(normed[here] * part.astype(F32), axis=0)
            start += part.shape[0]
        return total

    def attention_grads_of(attn_in, grad_qkv, merge_in, attn_out, rows, lower, gain_two_parts):
        gain_one_sum = sum(gain_part_of(r, l) for r, l in zip(rows, lower))
        gains = jnp.stack([gain_one_sum, sum(gain_two_parts)], axis=1)
        gains = pad_columns(gains.astype(BF16), LANES)
        return two_grads(attn_in, grad_qkv, merge_in, attn_out, gains)

    def project_norm_back(rows, parts, near, far, grad_hidden, gain):
        normed, inverse = norm_forward(rows.astype(F32))
        grad_lower, _ = norm_backward(scattered(parts, near, far), normed, inverse, gain)
        return grad_hidden + grad_lower

    def block_of(hidden, parts, near, far):
        return (hidden + scattered(parts, near, far)).astype(BF16)

    def only(*values):
        return values

    moved = chain.exchange(projections_for)
    a_near = chain.gather_near(tokens[0])
    projections = chain.all_rows(moved)
    moved = chain.exchange(lambda t: columns(merge_weight, t, query_width))
    merge = chain.all_rows(moved)
    a_far = chain.gather_far(a_near)
    moved = chain.exchange(feed_for(0))
    chain.wait(*a_far)
    b_near = chain.gather_near(tokens[1])
    gains = projections[:, qkv_width : qkv_width + 2].astype(F32)
    gain_one, gain_two = gains[:, 0], gains[:, 1]
    rows_a, attn_in_a, qkv = chain.run(
        project, tokens[0], a_near, a_far, projections[:, :qkv_width], gain_one
    )
    feeds = [chain.all_rows(moved)]
    attn_out_a, *kept_a = chain.run(attend, qkv, slots[0])
    b_far = chain.gather_far(b_near)
    branch_a = chain.run(merge_back, attn_out_a, merge)
    near_a = chain.scatter_near(branch_a)
    chain.wait(*b_far)
    rows_b, attn_in_b, qkv = chain.run(
        project, tokens[1], b_near, b_far, projections[:, :qkv_width], gain_one
    )
    far_a = chain.scatter_far(branch_a, near_a)
    cot_a_near = chain.gather_near(out_grad[0])
    attn_out_b, *kept_b = chain.run(attend, qkv, slots[1])
    chain.wait(*far_a)
    hidden_a, feed_a = chain.run(feed_norm, tokens[0], branch_a, near_a, far_a, gain_two)
    feed_a_near = chain.gather_near(feed_a)
    branch_b = chain.run(merge_back, attn_out_b, merge)
    cot_a_far = chain.gather_far(cot_a_near)
    feed_a_far = chain.gather_far(feed_a_near)
    if many:
        moved = chain.exchange(feed_for(1))
    chain.wait(*cot_a_far)
    chain.wait(*feed_a_far)
    near_b = chain.scatter_near(branch_b)
    if many:
        feeds.append(chain.all_rows(moved))
    cot_b_near = chain.gather_near(out_grad[1])
    *first, feed_in_a, down_in_a = chain.run(
        middle_first,
        (feed_a, feed_a_near, feed_a_far), (out_grad[0], cot_a_near, cot_a_far), feeds[0],
    )
    middle_a = [first]
    far_b = chain.scatter_far(branch_b, near_b)
    cot_b_far = chain.gather_far(cot_b_near)
    begun_back = None
    if many:
        (begun_back,) = chain.run(
            lambda m, w: feed_back([m], [w], None, True), middle_a[0][1], feeds[0]
        )
    chain.wait(*far_b)
    hidden_b, feed_b = chain.run(feed_norm, tokens[1], branch_b, near_b, far_b, gain_two)
    feed_b_near = chain.gather_near(feed_b)
    if many:
        middle_a.append(chain.run(middle_last, feed_in_a, down_in_a, feeds[1]))
    feed_b_far = chain.gather_far(feed_b_near)
    ends_a = slice(1 if many else 0, None)
    back_a = chain.run(feed_back, [m[1] for m in middle_a[ends_a]], feeds[ends_a], begun_back)
    near_a = chain.scatter_near(back_a)
    chain.wait(*cot_b_far)
    chain.wait(*feed_b_far)
    *first, feed_in_b, down_in_b = chain.run(
        middle_first,
        (feed_b, feed_b_near, feed_b_far), (out_grad[1], cot_b_near, cot_b_far), feeds[0],
    )
    middle_b = [first]
    far_a = chain.scatter_far(back_a, near_a)
    grads_first = chain.run(
        lambda f, d, m: feed_grads_of(f, d, m, 0),
        [feed_in_a, feed_in_b], [down_in_a, down_in_b], [middle_a[0], middle_b[0]],
    )
    chain.wait(*far_a)
    sums = [sum_over_dp(*chain.run(only, grads_first))]
    grad_hidden_a, merge_a, gain_two_a = chain.run(
        feed_norm_back, hidden_a, back_a, near_a, far_a, out_grad[0], gain_two
    )
    merge_a_near = chain.gather_near(merge_a)
    if many:
        middle_b.append(chain.run(middle_last, feed_in_b, down_in_b, feeds[1]))
    merge_a_far = chain.gather_far(merge_a_near)
    back_b = chain.run(feed_back, [m[1] for m in middle_b], feeds)
    near_b = chain.scatter_near(back_b)
    chain.wait(*merge_a_far)
    merge_in_a, grad_qkv_a = chain.run(
        attend_back, merge_a, merge_a_near, merge_a_far, merge, kept_a, slots[0]
    )
    far_b = chain.scatter_far(back_b, near_b)
    lower_a = chain.run(project_back, grad_qkv_a, projections)
    lower_a_near = chain.scatter_near(lower_a)
    out_a = chain.run(feed_out, [m[0] for m in middle_a], feeds)
    chain.wait(*far_b)
    grad_hidden_b, merge_b, gain_two_b = chain.run(
        feed_norm_back, hidden_b, back_b, near_b, far_b, out_grad[1], gain_two
    )
    merge_b_near = chain.gather_near(merge_b)
    lower_a_far = chain.scatter_far(lower_a, lower_a_near)
    if many:
        grads_last = chain.run(
            lambda f, d, m: feed_grads_of(f, d, m, 1),
            [feed_in_a, feed_in_b], [down_in_a, down_in_b], [middle_a[1], middle_b[1]],
        )
    merge_b_far = chain.gather_far(merge_b_near)
    chain.wait(*lower_a_far)
    input_grad_a = chain.run(
        project_norm_back, tokens[0], lower_a, lower_a_near, lower_a_far, grad_hidden_a, gain_one
    )
    chain.wait(*merge_b_far)
    out_a_near = chain.scatter_near(out_a)
    merge_in_b, grad_qkv_b = chain.run(
        attend_back, merge_b, merge_b_near, merge_b_far, merge, kept_b, slots[1]
    )
    chain.wait(*out_a_near)
    chain.wait(sums[0])
    if many:
        sums.append(sum_over_dp(*chain.run(only, grads_last)))
    out_a_far = chain.scatter_far(out_a, out_a_near)
    lower_b = chain.run(project_back, grad_qkv_b, projections)
    lower_b_near = chain.scatter_near(lower_b)
    chain.wait(*out_a_far)
    block_a = chain.run(block_of, hidden_a, out_a, out_a_near, out_a_far)
    moved_feed = [chain.own_rows(sums[0])]
    attention_grads = chain.run(
        attention_grads_of,
        [attn_in_a, attn_in_b],
        [grad_qkv_a, grad_qkv_b],
        [merge_in_a, merge_in_b],
        [attn_out_a, attn_out_b],
        [rows_a, rows_b],
        [lower_a, lower_b],
        [gain_two_a, gain_two_b],
    )
    chain.wait(*lower_b_near)
    chain.wait(*moved_feed[0][1:])
    chain.wait(sums[-1])
    attention_sums = sum_over_dp(*chain.run(only, attention_grads))
    lower_b_far = chain.scatter_far(lower_b, lower_b_near)
    out_b = chain.run(feed_out, [m[0] for m in middle_b], feeds)
    out_b_near = chain.scatter_near(out_b)
    chain.wait(*lower_b_far)
    input_grad_b = chain.run(
        project_norm_back, tokens[1], lower_b, lower_b_near, lower_b_far, grad_hidden_b, gain_one
    )
    moved_feed += [chain.own_rows(part) for part in sums[1:]]
    out_b_far = chain.scatter_far(out_b, out_b_near)
    chain.wait(*moved_feed[-1][1:])
    chain.wait(*out_b_far)
    block_b = chain.run(block_of, hidden_b, out_b, out_b_near, out_b_far)
    blocks = [block_a, block_b]
    input_grad = [input_grad_a, input_grad_b]

    key_at, value_at = query_width, query_width + key_width
    merge_at, gain_at = qkv_width, qkv_width + query_width
    feed_pieces = [
        (part, 2 * width + at * tile if kind == 2 else (2 * at + kind) * tile, tile, kind,
         starts[part] + at * tile)
        for part, width in enumerate(chunks)
        for at in range(width // tile)
        for kind in range(3)
    ]
    attention_pieces = [
        (0, 0, query_width, 0, 0),
        (0, key_at, own_key_width, 1, 0),
        (0, value_at, own_key_width, 2, 0),
        (0, merge_at, query_width, 3, 0),
    ]

    def results(received, pieces, widths):
        if square():
            return lay_out(received, pieces, widths)
        columns_of = [[] for _ in widths]
        for group, start, width, target, at in sorted(pieces, key=lambda piece: piece[4]):
            columns_of[target].append(received[group][0][:, :, start : start + width])
        return [
            jnp.concatenate(parts, axis=2)
            .astype(F32)
            .transpose(1, 0, 2)
            .reshape(weight_rows, -1)
            for parts in columns_of
        ]

    gate_total, up_total, down_total = chain.run(
        lambda *received: results(received, feed_pieces, [feed_width] * 3),
        *moved_feed,
    )
    moved = chain.own_rows(attention_sums)
    chain.wait(*moved[1:])
    query_total, key_total, value_total, merge_total = chain.run(
        lambda received: results(
            [received], attention_pieces, [query_width, own_key_width, own_key_width, query_width]
        ),
        moved,
    )
    gain_totals = sum(block[..., gain_at : gain_at + 2].astype(F32) for block in moved)
    if not square():
        gain_totals = jnp.sum(gain_totals, axis=0)
    return (
        jnp.stack(blocks),
        jnp.stack(input_grad),
        gain_totals[:, 0],
        query_total,
        key_total,
        value_total,
        merge_total,
        gain_totals[:, 1],
        gate_total,
        up_total,
        down_total,
    )


def solution(mesh):
    rows = P(("dp", "ctx"), None)
    vector = P(("dp", "ctx"))
    acts = P("dp", "ctx", None)
    in_specs = (
        acts, P("dp", None), acts, vector, rows, rows, rows, rows, vector, rows, rows, rows,
    )
    out_specs = (acts, acts, vector, rows, rows, rows, rows, vector, rows, rows, rows)
    return jax.shard_map(body, mesh=mesh, in_specs=in_specs, out_specs=out_specs, check_vma=False)
```

```python
import functools
import math

import jax
import jax.numpy as jnp
from jax import lax
from jax.experimental import pallas as pl
from jax.experimental.pallas import tpu as pltpu
from jax.sharding import PartitionSpec as P

HEAD_SIZE = 64
LANES = 128
EPS = 1e-05
THETA = 500000.0
QUERY_BLOCK = 256
F32 = jnp.float32
BF16 = jnp.bfloat16

NN = (((1,), (0,)), ((), ()))
NT = (((1,), (1,)), ((), ()))
TN = (((0,), (0,)), ((), ()))


def dot(left, right, dims=NN, out=F32):
    return lax.dot_general(left, right, dims, preferred_element_type=F32).astype(out)


class Chain:
    def __init__(self):
        self.last = ()

    def after(self, values):
        values = tuple(values)
        if not self.last:
            return values
        return lax.optimization_barrier(values + self.last)[: len(values)]

    def run(self, function, *args):
        leaves, tree = jax.tree.flatten(args)
        out = function(*jax.tree.unflatten(tree, self.after(leaves)))
        self.last = tuple(jax.tree.leaves(out))
        return out

    def wait(self, *arrays):
        self.last = self.last + arrays


    def send(self, *sends):
        blocks = self.after(block for block, _ in sends)
        return [
            lax.ppermute(block, "ctx", [(i, i ^ bits) for i in range(4)])
            for block, (_, bits) in zip(blocks, sends)
        ]

    def gather_near(self, own):
        return self.send((own, 1), (own, 2)) if square() else []

    def gather_far(self, near):
        if not square():
            return []
        self.wait(*near)
        half = near[0].shape[0] // 2
        one, two = self.after(near)
        return self.send((one[:half], 2), (two[half:], 1))

    def scatter_near(self, parts):
        return self.send((parts[1], 1), (parts[2], 2)) if square() else []

    def scatter_far(self, parts, near):
        if not square():
            return []

        def add(own, one, two):
            half = one.shape[0] // 2
            for_one = own[2 * half : 3 * half].astype(F32) + two[half:].astype(F32)
            for_two = own[3 * half :].astype(F32) + one[half:].astype(F32)
            return for_one.astype(BF16), for_two.astype(BF16)

        self.wait(*near)
        for_one, for_two = self.run(add, parts[0], *near)
        return self.send((for_one, 1), (for_two, 2))

    def exchange(self, block_for):
        size = lax.axis_size("ctx")
        rank = lax.axis_index("ctx")
        if not square():
            stacked = jnp.stack([block_for(t) for t in range(size)])
            return [lax.all_to_all(stacked, "ctx", 0, 0)]
        return [block_for(rank)] + self.send(*[(block_for(rank ^ m), m) for m in (1, 2, 3)])

    def exchanged(self, received):
        if not square():
            return received[0]
        rank = lax.axis_index("ctx")
        self.wait(*received[1:])

        def lay(*received):
            out = jnp.zeros((4,) + received[0].shape, received[0].dtype)
            for member, value in enumerate(received):
                out = lax.dynamic_update_index_in_dim(out, value, rank ^ member, 0)
            return out

        return self.run(lay, *received)

    def all_rows(self, received):
        mine = self.exchanged(received)
        return lax.all_gather(
            mine.reshape(-1, mine.shape[-1]), "dp", axis=0, tiled=True
        )

    def own_rows(self, summed):
        rows = summed.shape[0] // lax.axis_size("ctx")
        self.wait(summed)
        return self.exchange(lambda t: lax.dynamic_slice_in_dim(summed, t * rows, rows, axis=0))


def square():
    return lax.axis_size("ctx") == 4


HALVES = ((0, 0), (0, 1), (1, 1), (2, 0), (1, 0), (3, 0), (2, 1), (3, 1))


def pieces_of(own, near, far):
    rows = own.shape[0]
    if not square():
        whole = gathered(own, near, far)
        return [whole], [(0, 0, whole.shape[0], 0)]
    half = rows // 2
    sources = [own, *near, *far]
    plan = []
    for at, (member, part) in enumerate(HALVES):
        if member == 3:
            plan.append((3 + part, 0, half, at * half))
        else:
            plan.append((member, part * half, half, at * half))
    return sources, plan


def gathered(own, near, far):
    if not square():
        return lax.all_gather(own, "ctx", axis=0, tiled=True)
    half = own.shape[0] // 2
    one, two = near
    low, high = far
    return jnp.concatenate(
        [own, one[half:], two[:half], one[:half], low, two[half:], high], axis=0
    )


def scattered(parts, near, far):
    if not square():
        return lax.psum_scatter(parts[0], "ctx", scatter_dimension=0, tiled=True).astype(F32)
    half = near[0].shape[0] // 2
    low = parts[0][:half].astype(F32) + near[0][:half].astype(F32) + far[1].astype(F32)
    high = parts[0][half : 2 * half].astype(F32) + near[1][:half].astype(F32) + far[0].astype(F32)
    return jnp.concatenate([low, high], axis=0)


def sum_over_dp(grads):
    return lax.psum_scatter(grads, "dp", scatter_dimension=0, tiled=True)


def swap_halves(rows):
    lane = lax.broadcasted_iota(jnp.int32, rows.shape, 1)
    return jnp.where(
        lane % HEAD_SIZE < HEAD_SIZE // 2,
        pltpu.roll(rows, LANES - HEAD_SIZE // 2, 1),
        pltpu.roll(rows, HEAD_SIZE // 2, 1),
    )


def both_halves(rows, half):
    lane = lax.broadcasted_iota(jnp.int32, rows.shape, 1)
    kept = jnp.where(lane // HEAD_SIZE == half, rows.astype(F32), 0.0)
    return (kept + pltpu.roll(kept, HEAD_SIZE, 1)).astype(BF16)


def two_heads(rows):
    lane = lax.broadcasted_iota(jnp.int32, rows.shape, 1)
    wide = rows.astype(F32)
    first = jnp.where(lane < HEAD_SIZE, wide, 0.0)
    second = jnp.where(lane < HEAD_SIZE, 0.0, wide)
    return jnp.concatenate([first, second], axis=0).astype(BF16)


def visible(size):
    key = lax.broadcasted_iota(jnp.int32, (size, 2 * size), 0)
    query = lax.broadcasted_iota(jnp.int32, (size, 2 * size), 1) % size
    return key <= query


def hide_later(scores, mask, low):
    diagonal = jnp.where(mask, scores[low:], -1e30)
    return jnp.concatenate([scores[:low], diagonal], axis=0) if low else diagonal


def attention_forward_kernel(
    slot_ref, q_ref, k_ref, v_ref, cos_ref, sin_ref,
    out_ref, queries_ref, keys_ref, values_ref, total_ref, key_both, value_turned,
    *, span, pairs_of_head, pairs_of_block
):
    pair = pl.program_id(0)
    length = q_ref.shape[0]
    spans = length // span
    block = QUERY_BLOCK

    def place(index):
        return pl.ds(pl.multiple_of(slot_ref[index] * span, span), span)

    def turned(source, index):
        here = slice(index * span, (index + 1) * span)
        rows = source[place(index), :]
        return rows * cos_ref[here, :] + swap_halves(rows) * sin_ref[here, :]

    for index in range(spans):
        here = slice(index * span, (index + 1) * span)
        queries_ref[here, :] = turned(q_ref, index).astype(BF16)

    @pl.when(pair % pairs_of_block == 0)
    def _():
        for index in range(spans):
            here = slice(index * span, (index + 1) * span)
            keys_ref[here, :] = turned(k_ref, index).astype(BF16)
            values_ref[here, :] = v_ref[place(index), :].astype(BF16)

    @pl.when(pair % pairs_of_head == 0)
    def _():
        half = (pair // pairs_of_head) % 2
        key_both[...] = both_halves(keys_ref[...], half)
        value_both = both_halves(values_ref[...], half)
        value_turned[...] = value_both.astype(F32).T[:HEAD_SIZE].astype(BF16)

    mask = visible(block)
    for index in range(length // block):
        low, high = index * block, (index + 1) * block
        wide = two_heads(queries_ref[low:high, :] * jnp.asarray(HEAD_SIZE**-0.5, BF16))
        scores = hide_later(dot(key_both[:high, :], wide, NT), mask, low)
        top = jnp.max(scores, axis=0, keepdims=True)
        prob = jnp.exp(scores - top)
        total = jnp.sum(prob, axis=0, keepdims=True)
        attended = dot(value_turned[:, :high], prob.astype(BF16))
        total_ref[0, index : index + 1, :] = top + jnp.log(total)
        attended = attended / total
        rows = jnp.concatenate([attended[:, :block], attended[:, block:]], axis=0).T.astype(BF16)
        for part in range(block // span):
            out_ref[place(index * (block // span) + part), :] = rows[
                part * span : (part + 1) * span
            ]


def attention_backward_kernel(
    slot_ref, queries_ref, keys_ref, values_ref, total_ref, out_ref, grad_ref, cos_ref, sin_ref,
    grad_q_ref, grad_k_ref, grad_v_ref, key_both, value_both, key_turned, key_sum, value_sum,
    *, span, pairs_of_head
):
    pair = pl.program_id(0)
    length = queries_ref.shape[0]
    spans = length // span
    block = QUERY_BLOCK
    each = block // span
    half = (pair // pairs_of_head) % 2

    def place(index):
        return pl.ds(pl.multiple_of(slot_ref[index] * span, span), span)

    def turned_back(rows, index):
        here = slice(index * span, (index + 1) * span)
        return rows * cos_ref[here, :] - swap_halves(rows) * sin_ref[here, :]

    @pl.when(pair % pairs_of_head == 0)
    def _():
        key_both[...] = both_halves(keys_ref[...], half)
        value_both[...] = both_halves(values_ref[...], half)
        key_turned[...] = key_both[...].astype(F32).T[:HEAD_SIZE].astype(BF16)
        key_sum[...] = jnp.zeros_like(key_sum)
        value_sum[...] = jnp.zeros_like(value_sum)

    mask = visible(block)
    for index in range(length // block):
        low, high = index * block, (index + 1) * block
        wide = two_heads(queries_ref[low:high, :] * jnp.asarray(HEAD_SIZE**-0.5, BF16))
        here = [place(index * each + part) for part in range(each)]
        grad = jnp.concatenate([grad_ref[rows, :] for rows in here], axis=0)
        out = jnp.concatenate([out_ref[rows, :] for rows in here], axis=0)
        both = (grad.astype(F32) * out.astype(F32)).T
        row_dot = jnp.concatenate(
            [
                jnp.sum(both[:HEAD_SIZE], axis=0, keepdims=True),
                jnp.sum(both[HEAD_SIZE:], axis=0, keepdims=True),
            ],
            axis=1,
        )
        grad = two_heads(grad)
        total = total_ref[0, index : index + 1, :]
        scores = hide_later(dot(key_both[:high, :], wide, NT), mask, low)
        prob = jnp.exp(scores - total)
        grad_prob = dot(value_both[:high, :], grad, NT)
        grad_score = (prob * (grad_prob - row_dot)).astype(BF16)
        value_sum[:high, :] += dot(prob.astype(BF16), grad)
        key_sum[:high, :] += dot(grad_score, wide)
        turned = dot(key_turned[:, :high], grad_score)
        turned = turned * HEAD_SIZE**-0.5
        rows = jnp.concatenate([turned[:, :block], turned[:, block:]], axis=0).T
        for part in range(each):
            at = index * each + part
            grad_q_ref[place(at), :] = turned_back(
                rows[part * span : (part + 1) * span], at
            ).astype(BF16)

    @pl.when(pair % pairs_of_head == pairs_of_head - 1)
    def _():
        for index in range(spans):
            here = slice(index * span, (index + 1) * span)
            key_rows, value_rows = key_sum[here, :], value_sum[here, :]
            key_rows = turned_back(key_rows + pltpu.roll(key_rows, HEAD_SIZE, 1), index)
            value_rows = value_rows + pltpu.roll(value_rows, HEAD_SIZE, 1)
            lane = lax.broadcasted_iota(jnp.int32, key_rows.shape, 1)
            for target, rows in ((grad_k_ref, key_rows), (grad_v_ref, value_rows)):
                old = target[place(index), :].astype(F32)
                keep = (lane < HEAD_SIZE) & (half == 1)
                target[place(index), :] = jnp.where(keep, old, rows).astype(BF16)


def attention_sizes(query_width, group_size):
    pairs = query_width // LANES
    pairs_of_head = group_size // 2
    return pairs, pairs_of_head, 2 * pairs_of_head


def attention_forward(qkv, slots, cos_lanes, sin_lanes, query_width, key_width, group_size):
    length = qkv.shape[0]
    pairs, pairs_of_head, pairs_of_block = attention_sizes(query_width, group_size)
    key_at, value_at = query_width // LANES, (query_width + key_width) // LANES
    tile = (length, LANES)
    by_pair = pl.BlockSpec(tile, lambda p, s: (0, p))
    by_block = pl.BlockSpec(tile, lambda p, s: (0, p // pairs_of_block))
    whole = pl.BlockSpec(tile, lambda p, s: (0, 0))
    blocks = length // QUERY_BLOCK
    work = 2 * query_width * length * length
    return pl.pallas_call(
        functools.partial(
            attention_forward_kernel,
            span=length // slots.shape[0],
            pairs_of_head=pairs_of_head,
            pairs_of_block=pairs_of_block,
        ),
        grid_spec=pltpu.PrefetchScalarGridSpec(
            num_scalar_prefetch=1,
            grid=(pairs,),
            in_specs=[
                by_pair,
                pl.BlockSpec(tile, lambda p, s: (0, key_at + p // pairs_of_block)),
                pl.BlockSpec(tile, lambda p, s: (0, value_at + p // pairs_of_block)),
                whole,
                whole,
            ],
            out_specs=[
                by_pair,
                by_pair,
                by_block,
                by_block,
                pl.BlockSpec((1, blocks, 2 * QUERY_BLOCK), lambda p, s: (p, 0, 0)),
            ],
            scratch_shapes=[pltpu.VMEM(tile, BF16), pltpu.VMEM((HEAD_SIZE, length), BF16)],
        ),
        out_shape=[
            jax.ShapeDtypeStruct((length, query_width), BF16),
            jax.ShapeDtypeStruct((length, query_width), BF16),
            jax.ShapeDtypeStruct((length, key_width), BF16),
            jax.ShapeDtypeStruct((length, key_width), BF16),
            jax.ShapeDtypeStruct((pairs, blocks, 2 * QUERY_BLOCK), F32),
        ],
        compiler_params=pltpu.CompilerParams(
            dimension_semantics=("arbitrary",), vmem_limit_bytes=48 << 20
        ),
        cost_estimate=pl.CostEstimate(
            flops=24 * work, bytes_accessed=8 << 20, transcendentals=work // 128
        ),
        name="attention_forward",
    )(slots, qkv, qkv, qkv, cos_lanes, sin_lanes)


def attention_backward(kept, out, grad, slots, cos_lanes, sin_lanes, group_size):
    queries, keys, values, totals = kept
    length, query_width = queries.shape
    key_width = keys.shape[1]
    pairs, pairs_of_head, pairs_of_block = attention_sizes(query_width, group_size)
    tile = (length, LANES)
    by_pair = pl.BlockSpec(tile, lambda p, s: (0, p))
    by_block = pl.BlockSpec(tile, lambda p, s: (0, p // pairs_of_block))
    whole = pl.BlockSpec(tile, lambda p, s: (0, 0))
    blocks = length // QUERY_BLOCK
    work = 2 * query_width * length * length
    return pl.pallas_call(
        functools.partial(
            attention_backward_kernel, span=length // slots.shape[0], pairs_of_head=pairs_of_head
        ),
        grid_spec=pltpu.PrefetchScalarGridSpec(
            num_scalar_prefetch=1,
            grid=(pairs,),
            in_specs=[
                by_pair,
                by_block,
                by_block,
                pl.BlockSpec((1, blocks, 2 * QUERY_BLOCK), lambda p, s: (p, 0, 0)),
                by_pair,
                by_pair,
                whole,
                whole,
            ],
            out_specs=[by_pair, by_block, by_block],
            scratch_shapes=[
                pltpu.VMEM(tile, BF16),
                pltpu.VMEM(tile, BF16),
                pltpu.VMEM((HEAD_SIZE, length), BF16),
                pltpu.VMEM(tile, F32),
                pltpu.VMEM(tile, F32),
            ],
        ),
        out_shape=[
            jax.ShapeDtypeStruct((length, query_width), BF16),
            jax.ShapeDtypeStruct((length, key_width), BF16),
            jax.ShapeDtypeStruct((length, key_width), BF16),
        ],
        compiler_params=pltpu.CompilerParams(
            dimension_semantics=("arbitrary",), vmem_limit_bytes=48 << 20
        ),
        cost_estimate=pl.CostEstimate(
            flops=60 * work, bytes_accessed=8 << 20, transcendentals=work // 128
        ),
        name="attention_backward",
    )(slots, queries, keys, values, totals, out, grad, cos_lanes, sin_lanes)


def put_together(sources, plan, target, whole_ref, sems):
    copies = [
        pltpu.make_async_copy(
            sources[source].at[pl.ds(row, rows)], target.at[pl.ds(to, rows)], sems.at[at]
        )
        for at, (source, row, rows, to) in enumerate(plan)
    ]
    return copies, pltpu.make_async_copy(target, whole_ref, sems.at[len(plan)])


def gather_in(calls):
    for copies, _ in calls:
        for copy in copies:
            copy.start()
    for copies, out in calls:
        for copy in copies:
            copy.wait()
        out.start()


def feed_tile(feed_ref, down_in_ref, pair_ref, down_ref, activated_ref, grads_ref):
    tile = down_ref.shape[1]
    both = dot(feed_ref[...], pair_ref[...])
    grad_act = dot(down_in_ref[...], down_ref[...])
    gate, up = both[:, :tile], both[:, tile:]
    sig = jax.nn.sigmoid(gate)
    silu = gate * sig
    activated_ref[...] = (silu * up).astype(BF16)
    grads_ref[:, :tile] = (grad_act * up * (sig + silu * (1.0 - sig))).astype(BF16)
    grads_ref[:, tile:] = (grad_act * silu).astype(BF16)


def feed_kernel(*refs, plan, count):
    step = pl.program_id(0)
    feeds, downs, refs = refs[:count], refs[count : 2 * count], refs[2 * count :]
    pair_ref, down_ref, activated_ref, grads_ref, feed_out, down_out = refs[:6]
    feed_all, down_all, feed_sems, down_sems = refs[6:]
    calls = [
        put_together(feeds, plan, feed_all, feed_out, feed_sems),
        put_together(downs, plan, down_all, down_out, down_sems),
    ]

    @pl.when(step == 0)
    def _():
        gather_in(calls)

    feed_tile(feed_all, down_all, pair_ref, down_ref, activated_ref, grads_ref)

    @pl.when(step == pl.num_programs(0) - 1)
    def _():
        for _, out in calls:
            out.wait()


def feed_specs(rows, depth, width, tile):
    tiles = width // tile
    weights = [
        pl.BlockSpec((depth, 2 * tile), lambda j: (0, j)),
        pl.BlockSpec((depth, tile), lambda j: (0, 2 * tiles + j)),
    ]
    outs = [
        pl.BlockSpec((rows, tile), lambda j: (0, j)),
        pl.BlockSpec((rows, 2 * tile), lambda j: (0, j)),
    ]
    shapes = [
        jax.ShapeDtypeStruct((rows, width), BF16),
        jax.ShapeDtypeStruct((rows, 2 * width), BF16),
    ]
    work = rows * depth * width
    settings = {
        "compiler_params": pltpu.CompilerParams(
            dimension_semantics=("arbitrary",), vmem_limit_bytes=56 << 20
        ),
        "cost_estimate": pl.CostEstimate(
            flops=(6 * work) * 3,
            bytes_accessed=(2 * (2 * rows * depth + 3 * depth * width + 3 * rows * width)) * 3,
            transcendentals=rows * width,
        ),
    }
    return weights, outs, shapes, settings


def feed_first(feed, down, weights, width, tile):
    feeds, plan = pieces_of(*feed)
    downs, _ = pieces_of(*down)
    rows, depth = sum(entry[2] for entry in plan), weights.shape[0]
    weight_specs, outs, shapes, settings = feed_specs(rows, depth, width, tile)
    anywhere = pl.BlockSpec(memory_space=pl.ANY)
    whole = jax.ShapeDtypeStruct((rows, depth), BF16)
    return pl.pallas_call(
        functools.partial(feed_kernel, plan=plan, count=len(feeds)),
        grid=(width // tile,),
        in_specs=[anywhere] * (2 * len(feeds)) + weight_specs,
        out_specs=outs + [anywhere] * 2,
        out_shape=shapes + [whole] * 2,
        scratch_shapes=[
            pltpu.VMEM((rows, depth), BF16),
            pltpu.VMEM((rows, depth), BF16),
            pltpu.SemaphoreType.DMA((len(plan) + 1,)),
            pltpu.SemaphoreType.DMA((len(plan) + 1,)),
        ],
        name="feed_first",
        **settings,
    )(*feeds, *downs, weights, weights)


def feed_middle(feed_in, down_in, weights, width, tile):
    rows, depth = feed_in.shape
    weight_specs, outs, shapes, settings = feed_specs(rows, depth, width, tile)
    resident = pl.BlockSpec((rows, depth), lambda j: (0, 0), pipeline_mode=pl.Buffered(1))
    return pl.pallas_call(
        feed_tile,
        grid=(width // tile,),
        in_specs=[resident] * 2 + weight_specs,
        out_specs=outs,
        out_shape=shapes,
        name="feed_middle",
        **settings,
    )(feed_in, down_in, weights, weights)


def rows_kernel(*refs, plan, count):
    sources, (weight_ref, out_ref, whole_ref, target, sems) = refs[:count], refs[count:]
    call = put_together(sources, plan, target, whole_ref, sems)
    gather_in([call])
    out_ref[...] = dot(target[...], weight_ref[...]).astype(BF16)
    call[1].wait()


def rows_times(own, near, far, weight):
    sources, plan = pieces_of(own, near, far)
    rows, depth = sum(entry[2] for entry in plan), weight.shape[0]
    anywhere = pl.BlockSpec(memory_space=pl.ANY)
    return pl.pallas_call(
        functools.partial(rows_kernel, plan=plan, count=len(sources)),
        in_specs=[anywhere] * len(sources) + [pl.BlockSpec(memory_space=pltpu.VMEM)],
        out_specs=[pl.BlockSpec(memory_space=pltpu.VMEM), anywhere],
        out_shape=[
            jax.ShapeDtypeStruct((rows, weight.shape[1]), BF16),
            jax.ShapeDtypeStruct((rows, depth), BF16),
        ],
        scratch_shapes=[
            pltpu.VMEM((rows, depth), BF16),
            pltpu.SemaphoreType.DMA((len(plan) + 1,)),
        ],
        compiler_params=pltpu.CompilerParams(vmem_limit_bytes=48 << 20),
        cost_estimate=pl.CostEstimate(
            flops=(2 * rows * depth * weight.shape[1]) * 3,
            bytes_accessed=(2 * (2 * rows * depth + (rows + depth) * weight.shape[1])) * 3,
            transcendentals=0,
        ),
        name="rows_times",
    )(*sources, weight)


def spread_kernel(*refs, count, begun):
    total = sum(dot(refs[i][...], refs[count + i][...], NT) for i in range(count))
    if begun:
        total = total + refs[2 * count][...]
    start = 0
    for out in refs[2 * count + begun :]:
        out[...] = total[start : start + out.shape[0]].astype(out.dtype)
        start += out.shape[0]


def spread_rows(lefts, weights, places, tile, begun=None, whole=False):
    rows = lefts[0].shape[0]
    depth = weights[0].shape[0]
    widths = [left.shape[1] for left in lefts]
    work = rows * depth * sum(widths)
    outs = [rows // 2, rows // 4, rows // 4] if square() and not whole else [rows]
    begun = [] if begun is None else [begun]

    def weight_spec(width, place):
        return pl.BlockSpec((tile, width), lambda j: (j, place))

    return pl.pallas_call(
        functools.partial(spread_kernel, count=len(lefts), begun=len(begun)),
        grid=(depth // tile,),
        in_specs=[
            pl.BlockSpec((rows, width), lambda j: (0, 0), pipeline_mode=pl.Buffered(1))
            for width in widths
        ]
        + [weight_spec(width, place) for width, place in zip(widths, places)]
        + [pl.BlockSpec((rows, tile), lambda j: (0, j)) for _ in begun],
        out_specs=[pl.BlockSpec((each, tile), lambda j: (0, j)) for each in outs],
        out_shape=[jax.ShapeDtypeStruct((each, depth), F32 if whole else BF16) for each in outs],
        compiler_params=pltpu.CompilerParams(
            dimension_semantics=("arbitrary",), vmem_limit_bytes=56 << 20
        ),
        cost_estimate=pl.CostEstimate(
            flops=(2 * work) * 3,
            bytes_accessed=(2 * ((rows + depth) * sum(widths) + rows * depth)) * 3,
            transcendentals=0,
        ),
        name="spread_rows",
    )(*lefts, *weights, *begun)


def token_kernel(*refs, seqs, pair_tiles):
    feeds, downs, pairs, acts = (refs[at * seqs : (at + 1) * seqs] for at in range(4))
    column = pl.program_id(0)

    @pl.when(column < pair_tiles)
    def _():
        total = sum(dot(left[...], right[...], TN) for left, right in zip(feeds, pairs))
        refs[-1][...] = total.astype(BF16)

    @pl.when(column >= pair_tiles)
    def _():
        total = sum(dot(left[...], right[...], TN) for left, right in zip(downs, acts))
        refs[-1][...] = total.astype(BF16)


def feed_grads(feeds, downs, pairs, acts, tile):
    seqs = len(feeds)
    rows, depth = feeds[0].shape
    pair_tiles, act_tiles = pairs[0].shape[1] // tile, acts[0].shape[1] // tile
    step = min(512, depth)
    columns = (pair_tiles + act_tiles) * tile
    left_pair = pl.BlockSpec((rows, step), lambda j, i: (0, jnp.where(j < pair_tiles, i, 0)))
    left_act = pl.BlockSpec((rows, step), lambda j, i: (0, jnp.where(j < pair_tiles, 0, i)))
    pair = pl.BlockSpec((rows, tile), lambda j, i: (0, jnp.minimum(j, pair_tiles - 1)))
    act = pl.BlockSpec((rows, tile), lambda j, i: (0, jnp.maximum(j - pair_tiles, 0)))
    work = seqs * rows * depth * columns
    return pl.pallas_call(
        functools.partial(token_kernel, seqs=seqs, pair_tiles=pair_tiles),
        grid=(pair_tiles + act_tiles, depth // step),
        in_specs=[left_pair] * seqs + [left_act] * seqs + [pair] * seqs + [act] * seqs,
        out_specs=pl.BlockSpec((step, tile), lambda j, i: (i, j)),
        out_shape=jax.ShapeDtypeStruct((depth, columns), BF16),
        compiler_params=pltpu.CompilerParams(
            dimension_semantics=("arbitrary", "arbitrary"), vmem_limit_bytes=56 << 20
        ),
        cost_estimate=pl.CostEstimate(
            flops=(2 * work) * 3,
            bytes_accessed=(2 * (2 * seqs * rows * depth + (seqs * rows + depth) * columns)) * 3,
            transcendentals=0,
        ),
        name="feed_grads",
    )(*feeds, *downs, *pairs, *acts)


def two_grads_kernel(*refs, seqs):
    lefts, rights, others, more = (refs[at * seqs : (at + 1) * seqs] for at in range(4))
    gains_ref, out_ref = refs[4 * seqs :]
    width = rights[0].shape[1]
    end = width + more[0].shape[1]
    first = sum(dot(left[...], right[...], TN) for left, right in zip(lefts, rights))
    out_ref[:, :width] = first.astype(BF16)
    second = sum(dot(left[...], right[...], TN) for left, right in zip(others, more))
    out_ref[:, width:end] = second.astype(BF16)
    out_ref[:, end:] = gains_ref[...]


def two_grads(lefts, rights, others, more, gains):
    seqs = len(lefts)
    rows, depth = lefts[0].shape
    widths = [rights[0].shape[1], more[0].shape[1], gains.shape[1]]
    step = min(512, depth)
    work = seqs * rows * depth * (widths[0] + widths[1])

    def resident(array):
        return pl.BlockSpec(array.shape, lambda i: (0, 0), pipeline_mode=pl.Buffered(1))

    left = pl.BlockSpec((rows, step), lambda i: (0, i))
    return pl.pallas_call(
        functools.partial(two_grads_kernel, seqs=seqs),
        grid=(depth // step,),
        in_specs=[left] * seqs
        + [resident(array) for array in rights]
        + [left] * seqs
        + [resident(array) for array in more]
        + [pl.BlockSpec((step, widths[2]), lambda i: (i, 0))],
        out_specs=pl.BlockSpec((step, sum(widths)), lambda i: (i, 0)),
        out_shape=jax.ShapeDtypeStruct((depth, sum(widths)), BF16),
        compiler_params=pltpu.CompilerParams(
            dimension_semantics=("arbitrary",), vmem_limit_bytes=56 << 20
        ),
        cost_estimate=pl.CostEstimate(
            flops=(2 * work) * 3,
            bytes_accessed=(2 * (2 * seqs * rows * depth + (seqs * rows + depth) * sum(widths))) * 3,
            transcendentals=0,
        ),
        name="two_grads",
    )(*lefts, *rights, *others, *more, gains)


def lay_kernel(place_ref, *refs, plan, inputs):
    outs = refs[inputs:]
    for source, member, start, width, target, at in plan:
        each = outs[target].shape[1] // 4
        where = pl.ds(pl.multiple_of(place_ref[member] * each + at, LANES), width)
        outs[target][:, where] = refs[source][:, start : start + width].astype(F32)


def lay_out(received, pieces, widths):
    blocks = [block for group in received for block in group]
    rows = blocks[0].shape[0]
    plan = [
        (4 * group + member, member, start, width, target, at)
        for group, start, width, target, at in pieces
        for member in range(4)
    ]
    return pl.pallas_call(
        functools.partial(lay_kernel, plan=plan, inputs=len(blocks)),
        grid_spec=pltpu.PrefetchScalarGridSpec(
            num_scalar_prefetch=1,
            grid=(1,),
            in_specs=[pl.BlockSpec(block.shape, lambda i, p: (0, 0)) for block in blocks],
            out_specs=[pl.BlockSpec((rows, 4 * width), lambda i, p: (0, 0)) for width in widths],
        ),
        out_shape=[jax.ShapeDtypeStruct((rows, 4 * width), F32) for width in widths],
        compiler_params=pltpu.CompilerParams(vmem_limit_bytes=48 << 20),
        name="lay_out",
    )(lax.axis_index("ctx") ^ jnp.arange(4, dtype=jnp.int32), *blocks)


def norm_forward(values):
    inverse_rms = lax.rsqrt(jnp.mean(values * values, axis=-1, keepdims=True) + EPS)
    return (values * inverse_rms, inverse_rms)


def norm_backward(grad_normed, normed, inverse_rms, gain):
    grad_hat = grad_normed * gain
    grad_input = inverse_rms * (
        grad_hat - normed * jnp.mean(grad_hat * normed, axis=-1, keepdims=True)
    )
    return (grad_input, jnp.sum(grad_normed * normed, axis=0))


def rope_lanes(length):
    half = HEAD_SIZE // 2
    frequency = jnp.exp(
        jnp.arange(half, dtype=F32) * (-2.0 * math.log(THETA) / HEAD_SIZE)
    )
    angles = jnp.arange(length, dtype=jnp.int32).astype(F32)[:, None] * frequency[None, :]
    cosine, sine = jnp.cos(angles), jnp.sin(angles)
    return (
        jnp.concatenate([cosine] * 4, axis=1),
        jnp.concatenate([-sine, sine, -sine, sine], axis=1),
    )


def pad_columns(array, width):
    return jnp.pad(array, ((0, 0), (0, width - array.shape[1])))


def body(
    tokens, span_order, out_grad, first_gain, query_weight, key_matrix, value_matrix,
    merge_weight, second_gain, gate_weight, up_weight, down_weight,
):
    seqs, own_rows, depth = tokens.shape
    ctx = lax.axis_size("ctx")
    rank = lax.axis_index("ctx")
    length = own_rows * ctx
    spans = span_order.shape[1]
    weight_rows = gate_weight.shape[0]
    group_size = query_weight.shape[1] // key_matrix.shape[1]
    query_width = query_weight.shape[1] // ctx
    own_key_width = key_matrix.shape[1] // ctx
    key_width = -(-own_key_width // LANES) * LANES
    feed_width = gate_weight.shape[1] // ctx
    tile = min(512, feed_width)
    tiles = feed_width // tile
    first = max(1, 3 * tiles // 4)
    chunks = [first * tile] + ([(tiles - first) * tile] if tiles > first else [])
    starts = [0, chunks[0]][: len(chunks)]
    chain = Chain()

    def columns(weight, t, width, at=0):
        return lax.dynamic_slice_in_dim(weight, t * (weight.shape[1] // ctx) + at, width, axis=1)

    gain_columns = pad_columns(jnp.stack([first_gain, second_gain], axis=1), LANES)

    def projections_for(t):
        return jnp.concatenate(
            [
                columns(query_weight, t, query_width),
                pad_columns(columns(key_matrix, t, own_key_width), key_width),
                pad_columns(columns(value_matrix, t, own_key_width), key_width),
                gain_columns,
            ],
            axis=1,
        )

    def feed_for(part):
        def of(t):
            pieces = []
            for start in range(starts[part], starts[part] + chunks[part], tile):
                pieces += [
                    columns(gate_weight, t, tile, start),
                    columns(up_weight, t, tile, start),
                ]
            pieces.append(columns(down_weight, t, chunks[part], starts[part]))
            return jnp.concatenate(pieces, axis=1)

        return of

    assert seqs == 2 and len(chunks) <= 2
    many = len(chunks) > 1
    qkv_width = query_width + 2 * key_width

    slots = jnp.argsort(span_order, axis=1).astype(jnp.int32)
    if square():
        places = [HALVES.index((member, half)) for member in range(4) for half in range(2)]
        slots = jnp.array(places, jnp.int32)[((slots // 2) ^ rank) * 2 + slots % 2]
    cos_lanes, sin_lanes = rope_lanes(length)

    def project(own, near, far, weight, gain):
        rows = gathered(own, near, far)
        normed, _ = norm_forward(rows.astype(F32))
        attn_in = (normed * gain).astype(BF16)
        return rows, attn_in, dot(attn_in, weight)

    def attend(qkv, slots):
        return attention_forward(
            qkv, slots, cos_lanes, sin_lanes, query_width, key_width, group_size
        )

    def merge_back(rows, weight):
        return spread_rows([rows], [weight], [0], tile)

    def feed_norm(rows, branch, near, far, gain):
        hidden = rows.astype(F32) + scattered(branch, near, far)
        normed, _ = norm_forward(hidden)
        return hidden, (normed * gain).astype(BF16)

    def middle_first(feed, down, weights):
        return feed_first(feed, down, weights, chunks[0], tile)

    def middle_last(feed_in, down_in, weights):
        return feed_middle(feed_in, down_in, weights, chunks[1], tile)

    def feed_back(grads, weights, begun=None, whole=False):
        return spread_rows(grads, weights, [0] * len(grads), tile, begun, whole)

    def feed_out(activated, weights, begun=None, whole=False):
        return spread_rows(activated, weights, [2] * len(activated), tile, begun, whole)

    def feed_grads_of(feed_in, down_in, middle, part):
        return feed_grads(
            feed_in, down_in, [m[1] for m in middle], [m[0] for m in middle], chunks[part]
        )

    def feed_norm_back(hidden, parts, near, far, cot, gain):
        normed, inverse = norm_forward(hidden)
        grad_middle, gain_part = norm_backward(
            scattered(parts, near, far), normed, inverse, gain
        )
        grad_hidden = cot.astype(F32) + grad_middle
        return grad_hidden, grad_hidden.astype(BF16), gain_part

    def attend_back(own, near, far, weight, kept, out, slots):
        grad_attn, merge_in = rows_times(own, near, far, weight)
        parts = attention_backward(kept, out, grad_attn, slots, cos_lanes, sin_lanes, group_size)
        return merge_in, jnp.concatenate(parts, axis=1)

    def project_back(grads, weight):
        return spread_rows([grads], [weight], [0], tile)

    def gain_part_of(rows, lower):
        normed, _ = norm_forward(rows.astype(F32))
        total, start = 0.0, 0
        for part in lower:
            here = slice(start, start + part.shape[0])
            total = total + jnp.sum(normed[here] * part.astype(F32), axis=0)
            start += part.shape[0]
        return total

    def attention_grads_of(attn_in, grad_qkv, merge_in, attn_out, gain_one_parts, gain_two_parts):
        gains = jnp.stack([sum(gain_one_parts), sum(gain_two_parts)], axis=1)
        gains = pad_columns(gains.astype(BF16), LANES)
        return two_grads(attn_in, grad_qkv, merge_in, attn_out, gains)

    def project_norm_back(rows, parts, near, far, grad_hidden, gain):
        normed, inverse = norm_forward(rows.astype(F32))
        grad_lower, _ = norm_backward(scattered(parts, near, far), normed, inverse, gain)
        return grad_hidden + grad_lower

    def block_of(hidden, parts, near, far):
        return (hidden + scattered(parts, near, far)).astype(BF16)

    def only(*values):
        return values

    moved = chain.exchange(projections_for)
    a_near = chain.gather_near(tokens[0])
    projections = chain.all_rows(moved)
    moved = chain.exchange(lambda t: columns(merge_weight, t, query_width))
    merge = chain.all_rows(moved)
    a_far = chain.gather_far(a_near)
    moved = chain.exchange(feed_for(0))
    chain.wait(*a_far)
    b_near = chain.gather_near(tokens[1])
    gains = projections[:, qkv_width : qkv_width + 2].astype(F32)
    gain_one, gain_two = gains[:, 0], gains[:, 1]
    rows_a, attn_in_a, qkv = chain.run(
        project, tokens[0], a_near, a_far, projections[:, :qkv_width], gain_one
    )
    feeds = [chain.all_rows(moved)]
    attn_out_a, *kept_a = chain.run(attend, qkv, slots[0])
    b_far = chain.gather_far(b_near)
    branch_a = chain.run(merge_back, attn_out_a, merge)
    near_a = chain.scatter_near(branch_a)
    chain.wait(*b_far)
    rows_b, attn_in_b, qkv = chain.run(
        project, tokens[1], b_near, b_far, projections[:, :qkv_width], gain_one
    )
    far_a = chain.scatter_far(branch_a, near_a)
    cot_a_near = chain.gather_near(out_grad[0])
    attn_out_b, *kept_b = chain.run(attend, qkv, slots[1])
    chain.wait(*far_a)
    hidden_a, feed_a = chain.run(feed_norm, tokens[0], branch_a, near_a, far_a, gain_two)
    feed_a_near = chain.gather_near(feed_a)
    branch_b = chain.run(merge_back, attn_out_b, merge)
    cot_a_far = chain.gather_far(cot_a_near)
    feed_a_far = chain.gather_far(feed_a_near)
    if many:
        moved = chain.exchange(feed_for(1))
    chain.wait(*cot_a_far)
    chain.wait(*feed_a_far)
    near_b = chain.scatter_near(branch_b)
    if many:
        feeds.append(chain.all_rows(moved))
    cot_b_near = chain.gather_near(out_grad[1])
    *first, feed_in_a, down_in_a = chain.run(
        middle_first,
        (feed_a, feed_a_near, feed_a_far), (out_grad[0], cot_a_near, cot_a_far), feeds[0],
    )
    middle_a = [first]
    far_b = chain.scatter_far(branch_b, near_b)
    cot_b_far = chain.gather_far(cot_b_near)
    begun_back = None
    if many:
        (begun_back,) = chain.run(
            lambda m, w: feed_back([m], [w], None, True), middle_a[0][1], feeds[0]
        )
    chain.wait(*far_b)
    hidden_b, feed_b = chain.run(feed_norm, tokens[1], branch_b, near_b, far_b, gain_two)
    feed_b_near = chain.gather_near(feed_b)
    if many:
        middle_a.append(chain.run(middle_last, feed_in_a, down_in_a, feeds[1]))
    feed_b_far = chain.gather_far(feed_b_near)
    ends_a = slice(1 if many else 0, None)
    back_a = chain.run(feed_back, [m[1] for m in middle_a[ends_a]], feeds[ends_a], begun_back)
    near_a = chain.scatter_near(back_a)
    chain.wait(*cot_b_far)
    chain.wait(*feed_b_far)
    *first, feed_in_b, down_in_b = chain.run(
        middle_first,
        (feed_b, feed_b_near, feed_b_far), (out_grad[1], cot_b_near, cot_b_far), feeds[0],
    )
    middle_b = [first]
    far_a = chain.scatter_far(back_a, near_a)
    grads_first = chain.run(
        lambda f, d, m: feed_grads_of(f, d, m, 0),
        [feed_in_a, feed_in_b], [down_in_a, down_in_b], [middle_a[0], middle_b[0]],
    )
    chain.wait(*far_a)
    sums = [sum_over_dp(*chain.run(only, grads_first))]
    grad_hidden_a, merge_a, gain_two_a = chain.run(
        feed_norm_back, hidden_a, back_a, near_a, far_a, out_grad[0], gain_two
    )
    merge_a_near = chain.gather_near(merge_a)
    if many:
        middle_b.append(chain.run(middle_last, feed_in_b, down_in_b, feeds[1]))
    merge_a_far = chain.gather_far(merge_a_near)
    back_b = chain.run(feed_back, [m[1] for m in middle_b], feeds)
    near_b = chain.scatter_near(back_b)
    chain.wait(*merge_a_far)
    merge_in_a, grad_qkv_a = chain.run(
        attend_back, merge_a, merge_a_near, merge_a_far, merge, kept_a, attn_out_a, slots[0]
    )
    far_b = chain.scatter_far(back_b, near_b)
    lower_a = chain.run(project_back, grad_qkv_a, projections)
    lower_a_near = chain.scatter_near(lower_a)
    out_a = chain.run(feed_out, [m[0] for m in middle_a], feeds)
    chain.wait(*far_b)
    grad_hidden_b, merge_b, gain_two_b = chain.run(
        feed_norm_back, hidden_b, back_b, near_b, far_b, out_grad[1], gain_two
    )
    merge_b_near = chain.gather_near(merge_b)
    lower_a_far = chain.scatter_far(lower_a, lower_a_near)
    if many:
        grads_last = chain.run(
            lambda f, d, m: feed_grads_of(f, d, m, 1),
            [feed_in_a, feed_in_b], [down_in_a, down_in_b], [middle_a[1], middle_b[1]],
        )
    merge_b_far = chain.gather_far(merge_b_near)
    chain.wait(*lower_a_far)
    input_grad_a = chain.run(
        project_norm_back, tokens[0], lower_a, lower_a_near, lower_a_far, grad_hidden_a, gain_one
    )
    chain.wait(*merge_b_far)
    out_a_near = chain.scatter_near(out_a)
    gain_one_a = chain.run(gain_part_of, rows_a, lower_a)
    chain.wait(*out_a_near)
    chain.wait(sums[0])
    if many:
        sums.append(sum_over_dp(*chain.run(only, grads_last)))
    out_a_far = chain.scatter_far(out_a, out_a_near)
    moved_feed = [chain.own_rows(sums[0])]
    merge_in_b, grad_qkv_b = chain.run(
        attend_back, merge_b, merge_b_near, merge_b_far, merge, kept_b, attn_out_b, slots[1]
    )
    lower_b = chain.run(project_back, grad_qkv_b, projections)
    chain.wait(*out_a_far)
    lower_b_near = chain.scatter_near(lower_b)
    chain.wait(*moved_feed[0][1:])
    gain_one_b = chain.run(gain_part_of, rows_b, lower_b)
    attention_grads = chain.run(
        attention_grads_of,
        [attn_in_a, attn_in_b],
        [grad_qkv_a, grad_qkv_b],
        [merge_in_a, merge_in_b],
        [attn_out_a, attn_out_b],
        [gain_one_a, gain_one_b],
        [gain_two_a, gain_two_b],
    )
    chain.wait(*lower_b_near)
    chain.wait(sums[-1])
    attention_sums = sum_over_dp(*chain.run(only, attention_grads))
    lower_b_far = chain.scatter_far(lower_b, lower_b_near)
    out_b = chain.run(feed_out, [m[0] for m in middle_b], feeds)
    out_b_near = chain.scatter_near(out_b)
    chain.wait(*lower_b_far)
    input_grad_b = chain.run(
        project_norm_back, tokens[1], lower_b, lower_b_near, lower_b_far, grad_hidden_b, gain_one
    )
    moved_feed += [chain.own_rows(part) for part in sums[1:]]
    out_b_far = chain.scatter_far(out_b, out_b_near)
    block_a = chain.run(block_of, hidden_a, out_a, out_a_near, out_a_far)
    chain.wait(*moved_feed[-1][1:])
    chain.wait(*out_b_far)
    block_b = chain.run(block_of, hidden_b, out_b, out_b_near, out_b_far)
    blocks = [block_a, block_b]
    input_grad = [input_grad_a, input_grad_b]

    key_at, value_at = query_width, query_width + key_width
    merge_at, gain_at = qkv_width, qkv_width + query_width
    feed_pieces = [
        (part, 2 * width + at * tile if kind == 2 else (2 * at + kind) * tile, tile, kind,
         starts[part] + at * tile)
        for part, width in enumerate(chunks)
        for at in range(width // tile)
        for kind in range(3)
    ]
    attention_pieces = [
        (0, 0, query_width, 0, 0),
        (0, key_at, own_key_width, 1, 0),
        (0, value_at, own_key_width, 2, 0),
        (0, merge_at, query_width, 3, 0),
    ]

    def results(received, pieces, widths):
        if square():
            return lay_out(received, pieces, widths)
        columns_of = [[] for _ in widths]
        for group, start, width, target, at in sorted(pieces, key=lambda piece: piece[4]):
            columns_of[target].append(received[group][0][:, :, start : start + width])
        return [
            jnp.concatenate(parts, axis=2)
            .astype(F32)
            .transpose(1, 0, 2)
            .reshape(weight_rows, -1)
            for parts in columns_of
        ]

    gate_total, up_total, down_total = chain.run(
        lambda *received: results(received, feed_pieces, [feed_width] * 3),
        *moved_feed,
    )
    moved = chain.own_rows(attention_sums)
    chain.wait(*moved[1:])
    query_total, key_total, value_total, merge_total = chain.run(
        lambda received: results(
            [received], attention_pieces, [query_width, own_key_width, own_key_width, query_width]
        ),
        moved,
    )
    gain_totals = sum(block[..., gain_at : gain_at + 2].astype(F32) for block in moved)
    if not square():
        gain_totals = jnp.sum(gain_totals, axis=0)
    return (
        jnp.stack(blocks),
        jnp.stack(input_grad),
        gain_totals[:, 0],
        query_total,
        key_total,
        value_total,
        merge_total,
        gain_totals[:, 1],
        gate_total,
        up_total,
        down_total,
    )


def solution(mesh):
    rows = P(("dp", "ctx"), None)
    vector = P(("dp", "ctx"))
    acts = P("dp", "ctx", None)
    in_specs = (
        acts, P("dp", None), acts, vector, rows, rows, rows, rows, vector, rows, rows, rows,
    )
    out_specs = (acts, acts, vector, rows, rows, rows, rows, vector, rows, rows, rows)
    return jax.shard_map(body, mesh=mesh, in_specs=in_specs, out_specs=out_specs, check_vma=False)
```

```python
import functools
import math

import jax
import jax.numpy as jnp
from jax import lax
from jax.experimental import pallas as pl
from jax.experimental.pallas import tpu as pltpu
from jax.sharding import PartitionSpec as P

HEAD_SIZE = 64
LANES = 128
EPS = 1e-05
THETA = 500000.0
QUERY_BLOCK = 256
F32 = jnp.float32
BF16 = jnp.bfloat16

NN = (((1,), (0,)), ((), ()))
NT = (((1,), (1,)), ((), ()))
TN = (((0,), (0,)), ((), ()))


def dot(left, right, dims=NN, out=F32):
    return lax.dot_general(left, right, dims, preferred_element_type=F32).astype(out)


class Chain:
    def __init__(self):
        self.last = ()

    def after(self, values):
        values = tuple(values)
        if not self.last:
            return values
        return lax.optimization_barrier(values + self.last)[: len(values)]

    def run(self, function, *args):
        leaves, tree = jax.tree.flatten(args)
        out = function(*jax.tree.unflatten(tree, self.after(leaves)))
        self.last = tuple(jax.tree.leaves(out))
        return out

    def wait(self, *arrays):
        self.last = self.last + arrays


    def send(self, *sends):
        blocks = self.after(block for block, _ in sends)
        return [
            lax.ppermute(block, "ctx", [(i, i ^ bits) for i in range(4)])
            for block, (_, bits) in zip(blocks, sends)
        ]

    def gather_near(self, own):
        return self.send((own, 1), (own, 2)) if square() else []

    def gather_far(self, near):
        if not square():
            return []
        self.wait(*near)
        half = near[0].shape[0] // 2
        one, two = self.after(near)
        return self.send((one[:half], 2), (two[half:], 1))

    def scatter_near(self, parts):
        return self.send((parts[1], 1), (parts[2], 2)) if square() else []

    def scatter_far(self, parts, near):
        if not square():
            return []

        def add(own, one, two):
            half = one.shape[0] // 2
            for_one = own[2 * half : 3 * half].astype(F32) + two[half:].astype(F32)
            for_two = own[3 * half :].astype(F32) + one[half:].astype(F32)
            return for_one.astype(BF16), for_two.astype(BF16)

        self.wait(*near)
        for_one, for_two = self.run(add, parts[0], *near)
        return self.send((for_one, 1), (for_two, 2))

    def exchange(self, block_for):
        size = lax.axis_size("ctx")
        rank = lax.axis_index("ctx")
        if not square():
            stacked = jnp.stack([block_for(t) for t in range(size)])
            return [lax.all_to_all(stacked, "ctx", 0, 0)]
        return [block_for(rank)] + self.send(*[(block_for(rank ^ m), m) for m in (1, 2, 3)])

    def exchanged(self, received):
        if not square():
            return received[0]
        self.wait(*received[1:])
        return self.run(stack_rows, received)

    def all_rows(self, received):
        mine = self.exchanged(received)
        return lax.all_gather(
            mine.reshape(-1, mine.shape[-1]), "dp", axis=0, tiled=True
        )

    def own_rows(self, summed):
        rows = summed.shape[0] // lax.axis_size("ctx")
        self.wait(summed)
        return self.exchange(lambda t: lax.dynamic_slice_in_dim(summed, t * rows, rows, axis=0))


def square():
    return lax.axis_size("ctx") == 4


HALVES = ((0, 0), (0, 1), (1, 1), (2, 0), (1, 0), (3, 0), (2, 1), (3, 1))


def pieces_of(own, near, far):
    rows = own.shape[0]
    if not square():
        whole = gathered(own, near, far)
        return [whole], [(0, 0, whole.shape[0], 0)]
    half = rows // 2
    sources = [own, *near, *far]
    plan = []
    for at, (member, part) in enumerate(HALVES):
        if member == 3:
            plan.append((3 + part, 0, half, at * half))
        else:
            plan.append((member, part * half, half, at * half))
    return sources, plan


def gathered(own, near, far):
    if not square():
        return lax.all_gather(own, "ctx", axis=0, tiled=True)
    half = own.shape[0] // 2
    one, two = near
    low, high = far
    return jnp.concatenate(
        [own, one[half:], two[:half], one[:half], low, two[half:], high], axis=0
    )


def scattered(parts, near, far):
    if not square():
        return lax.psum_scatter(parts[0], "ctx", scatter_dimension=0, tiled=True).astype(F32)
    half = near[0].shape[0] // 2
    low = parts[0][:half].astype(F32) + near[0][:half].astype(F32) + far[1].astype(F32)
    high = parts[0][half : 2 * half].astype(F32) + near[1][:half].astype(F32) + far[0].astype(F32)
    return jnp.concatenate([low, high], axis=0)


def stack_kernel(place_ref, *refs):
    rows = refs[0].shape[0]
    for member, block in enumerate(refs[:-1]):
        here = pl.ds(pl.multiple_of(place_ref[member] * rows, rows), rows)
        refs[-1][here, :] = block[...]


def stack_rows(blocks):
    rows, width = blocks[0].shape
    return pl.pallas_call(
        stack_kernel,
        grid_spec=pltpu.PrefetchScalarGridSpec(
            num_scalar_prefetch=1,
            grid=(1,),
            in_specs=[pl.BlockSpec((rows, width), lambda i, p: (0, 0))] * 4,
            out_specs=pl.BlockSpec((4 * rows, width), lambda i, p: (0, 0)),
        ),
        out_shape=jax.ShapeDtypeStruct((4 * rows, width), blocks[0].dtype),
        compiler_params=pltpu.CompilerParams(vmem_limit_bytes=48 << 20),
        name="stack_rows",
    )(lax.axis_index("ctx") ^ jnp.arange(4, dtype=jnp.int32), *blocks)


def sum_over_dp(grads):
    return lax.psum_scatter(grads, "dp", scatter_dimension=0, tiled=True)


def swap_halves(rows):
    lane = lax.broadcasted_iota(jnp.int32, rows.shape, 1)
    return jnp.where(
        lane % HEAD_SIZE < HEAD_SIZE // 2,
        pltpu.roll(rows, LANES - HEAD_SIZE // 2, 1),
        pltpu.roll(rows, HEAD_SIZE // 2, 1),
    )


def both_halves(rows, half):
    lane = lax.broadcasted_iota(jnp.int32, rows.shape, 1)
    kept = jnp.where(lane // HEAD_SIZE == half, rows.astype(F32), 0.0)
    return (kept + pltpu.roll(kept, HEAD_SIZE, 1)).astype(BF16)


def two_heads(rows):
    lane = lax.broadcasted_iota(jnp.int32, rows.shape, 1)
    wide = rows.astype(F32)
    first = jnp.where(lane < HEAD_SIZE, wide, 0.0)
    second = jnp.where(lane < HEAD_SIZE, 0.0, wide)
    return jnp.concatenate([first, second], axis=0).astype(BF16)


def visible(size):
    key = lax.broadcasted_iota(jnp.int32, (size, 2 * size), 0)
    query = lax.broadcasted_iota(jnp.int32, (size, 2 * size), 1) % size
    return key <= query


def hide_later(scores, mask, low):
    diagonal = jnp.where(mask, scores[low:], -1e30)
    return jnp.concatenate([scores[:low], diagonal], axis=0) if low else diagonal


def attention_forward_kernel(
    slot_ref, q_ref, k_ref, v_ref, cos_ref, sin_ref,
    out_ref, queries_ref, keys_ref, values_ref, total_ref, key_both, value_turned,
    *, span, pairs_of_head, pairs_of_block
):
    pair = pl.program_id(0)
    length = q_ref.shape[0]
    spans = length // span
    block = QUERY_BLOCK

    def place(index):
        return pl.ds(pl.multiple_of(slot_ref[index] * span, span), span)

    def turned(source, index):
        here = slice(index * span, (index + 1) * span)
        rows = source[place(index), :]
        return rows * cos_ref[here, :] + swap_halves(rows) * sin_ref[here, :]

    for index in range(spans):
        here = slice(index * span, (index + 1) * span)
        queries_ref[here, :] = turned(q_ref, index).astype(BF16)

    @pl.when(pair % pairs_of_block == 0)
    def _():
        for index in range(spans):
            here = slice(index * span, (index + 1) * span)
            keys_ref[here, :] = turned(k_ref, index).astype(BF16)
            values_ref[here, :] = v_ref[place(index), :].astype(BF16)

    @pl.when(pair % pairs_of_head == 0)
    def _():
        half = (pair // pairs_of_head) % 2
        key_both[...] = both_halves(keys_ref[...], half)
        value_both = both_halves(values_ref[...], half)
        value_turned[...] = value_both.astype(F32).T[:HEAD_SIZE].astype(BF16)

    mask = visible(block)
    for index in range(length // block):
        low, high = index * block, (index + 1) * block
        wide = two_heads(queries_ref[low:high, :] * jnp.asarray(HEAD_SIZE**-0.5, BF16))
        scores = hide_later(dot(key_both[:high, :], wide, NT), mask, low)
        top = jnp.max(scores, axis=0, keepdims=True)
        prob = jnp.exp(scores - top)
        total = jnp.sum(prob, axis=0, keepdims=True)
        attended = dot(value_turned[:, :high], prob.astype(BF16))
        total_ref[0, index : index + 1, :] = top + jnp.log(total)
        attended = attended / total
        rows = jnp.concatenate([attended[:, :block], attended[:, block:]], axis=0).T.astype(BF16)
        for part in range(block // span):
            out_ref[place(index * (block // span) + part), :] = rows[
                part * span : (part + 1) * span
            ]


def attention_backward_kernel(
    slot_ref, queries_ref, keys_ref, values_ref, total_ref, out_ref, grad_ref, cos_ref, sin_ref,
    grad_q_ref, grad_k_ref, grad_v_ref, key_both, value_both, key_turned, key_sum, value_sum,
    *, span, pairs_of_head
):
    pair = pl.program_id(0)
    length = queries_ref.shape[0]
    spans = length // span
    block = QUERY_BLOCK
    each = block // span
    half = (pair // pairs_of_head) % 2

    def place(index):
        return pl.ds(pl.multiple_of(slot_ref[index] * span, span), span)

    def turned_back(rows, index):
        here = slice(index * span, (index + 1) * span)
        return rows * cos_ref[here, :] - swap_halves(rows) * sin_ref[here, :]

    @pl.when(pair % pairs_of_head == 0)
    def _():
        key_both[...] = both_halves(keys_ref[...], half)
        value_both[...] = both_halves(values_ref[...], half)
        key_turned[...] = key_both[...].astype(F32).T[:HEAD_SIZE].astype(BF16)
        key_sum[...] = jnp.zeros_like(key_sum)
        value_sum[...] = jnp.zeros_like(value_sum)

    mask = visible(block)
    for index in range(length // block):
        low, high = index * block, (index + 1) * block
        wide = two_heads(queries_ref[low:high, :] * jnp.asarray(HEAD_SIZE**-0.5, BF16))
        here = [place(index * each + part) for part in range(each)]
        grad = jnp.concatenate([grad_ref[rows, :] for rows in here], axis=0)
        out = jnp.concatenate([out_ref[rows, :] for rows in here], axis=0)
        both = (grad.astype(F32) * out.astype(F32)).T
        row_dot = jnp.concatenate(
            [
                jnp.sum(both[:HEAD_SIZE], axis=0, keepdims=True),
                jnp.sum(both[HEAD_SIZE:], axis=0, keepdims=True),
            ],
            axis=1,
        )
        grad = two_heads(grad)
        total = total_ref[0, index : index + 1, :]
        scores = hide_later(dot(key_both[:high, :], wide, NT), mask, low)
        prob = jnp.exp(scores - total)
        grad_prob = dot(value_both[:high, :], grad, NT)
        grad_score = (prob * (grad_prob - row_dot)).astype(BF16)
        value_sum[:high, :] += dot(prob.astype(BF16), grad)
        key_sum[:high, :] += dot(grad_score, wide)
        turned = dot(key_turned[:, :high], grad_score)
        turned = turned * HEAD_SIZE**-0.5
        rows = jnp.concatenate([turned[:, :block], turned[:, block:]], axis=0).T
        for part in range(each):
            at = index * each + part
            grad_q_ref[place(at), :] = turned_back(
                rows[part * span : (part + 1) * span], at
            ).astype(BF16)

    @pl.when(pair % pairs_of_head == pairs_of_head - 1)
    def _():
        for index in range(spans):
            here = slice(index * span, (index + 1) * span)
            key_rows, value_rows = key_sum[here, :], value_sum[here, :]
            key_rows = turned_back(key_rows + pltpu.roll(key_rows, HEAD_SIZE, 1), index)
            value_rows = value_rows + pltpu.roll(value_rows, HEAD_SIZE, 1)
            lane = lax.broadcasted_iota(jnp.int32, key_rows.shape, 1)
            for target, rows in ((grad_k_ref, key_rows), (grad_v_ref, value_rows)):
                old = target[place(index), :].astype(F32)
                keep = (lane < HEAD_SIZE) & (half == 1)
                target[place(index), :] = jnp.where(keep, old, rows).astype(BF16)


def attention_sizes(query_width, group_size):
    pairs = query_width // LANES
    pairs_of_head = group_size // 2
    return pairs, pairs_of_head, 2 * pairs_of_head


def attention_forward(qkv, slots, cos_lanes, sin_lanes, query_width, key_width, group_size):
    length = qkv.shape[0]
    pairs, pairs_of_head, pairs_of_block = attention_sizes(query_width, group_size)
    key_at, value_at = query_width // LANES, (query_width + key_width) // LANES
    tile = (length, LANES)
    by_pair = pl.BlockSpec(tile, lambda p, s: (0, p))
    by_block = pl.BlockSpec(tile, lambda p, s: (0, p // pairs_of_block))
    whole = pl.BlockSpec(tile, lambda p, s: (0, 0))
    blocks = length // QUERY_BLOCK
    work = 2 * query_width * length * length
    return pl.pallas_call(
        functools.partial(
            attention_forward_kernel,
            span=length // slots.shape[0],
            pairs_of_head=pairs_of_head,
            pairs_of_block=pairs_of_block,
        ),
        grid_spec=pltpu.PrefetchScalarGridSpec(
            num_scalar_prefetch=1,
            grid=(pairs,),
            in_specs=[
                by_pair,
                pl.BlockSpec(tile, lambda p, s: (0, key_at + p // pairs_of_block)),
                pl.BlockSpec(tile, lambda p, s: (0, value_at + p // pairs_of_block)),
                whole,
                whole,
            ],
            out_specs=[
                by_pair,
                by_pair,
                by_block,
                by_block,
                pl.BlockSpec((1, blocks, 2 * QUERY_BLOCK), lambda p, s: (p, 0, 0)),
            ],
            scratch_shapes=[pltpu.VMEM(tile, BF16), pltpu.VMEM((HEAD_SIZE, length), BF16)],
        ),
        out_shape=[
            jax.ShapeDtypeStruct((length, query_width), BF16),
            jax.ShapeDtypeStruct((length, query_width), BF16),
            jax.ShapeDtypeStruct((length, key_width), BF16),
            jax.ShapeDtypeStruct((length, key_width), BF16),
            jax.ShapeDtypeStruct((pairs, blocks, 2 * QUERY_BLOCK), F32),
        ],
        compiler_params=pltpu.CompilerParams(
            dimension_semantics=("arbitrary",), vmem_limit_bytes=48 << 20
        ),
        cost_estimate=pl.CostEstimate(
            flops=24 * work, bytes_accessed=8 << 20, transcendentals=work // 128
        ),
        name="attention_forward",
    )(slots, qkv, qkv, qkv, cos_lanes, sin_lanes)


def attention_backward(kept, out, grad, slots, cos_lanes, sin_lanes, group_size):
    queries, keys, values, totals = kept
    length, query_width = queries.shape
    key_width = keys.shape[1]
    pairs, pairs_of_head, pairs_of_block = attention_sizes(query_width, group_size)
    tile = (length, LANES)
    by_pair = pl.BlockSpec(tile, lambda p, s: (0, p))
    by_block = pl.BlockSpec(tile, lambda p, s: (0, p // pairs_of_block))
    whole = pl.BlockSpec(tile, lambda p, s: (0, 0))
    blocks = length // QUERY_BLOCK
    work = 2 * query_width * length * length
    return pl.pallas_call(
        functools.partial(
            attention_backward_kernel, span=length // slots.shape[0], pairs_of_head=pairs_of_head
        ),
        grid_spec=pltpu.PrefetchScalarGridSpec(
            num_scalar_prefetch=1,
            grid=(pairs,),
            in_specs=[
                by_pair,
                by_block,
                by_block,
                pl.BlockSpec((1, blocks, 2 * QUERY_BLOCK), lambda p, s: (p, 0, 0)),
                by_pair,
                by_pair,
                whole,
                whole,
            ],
            out_specs=[by_pair, by_block, by_block],
            scratch_shapes=[
                pltpu.VMEM(tile, BF16),
                pltpu.VMEM(tile, BF16),
                pltpu.VMEM((HEAD_SIZE, length), BF16),
                pltpu.VMEM(tile, F32),
                pltpu.VMEM(tile, F32),
            ],
        ),
        out_shape=[
            jax.ShapeDtypeStruct((length, query_width), BF16),
            jax.ShapeDtypeStruct((length, key_width), BF16),
            jax.ShapeDtypeStruct((length, key_width), BF16),
        ],
        compiler_params=pltpu.CompilerParams(
            dimension_semantics=("arbitrary",), vmem_limit_bytes=48 << 20
        ),
        cost_estimate=pl.CostEstimate(
            flops=60 * work, bytes_accessed=8 << 20, transcendentals=work // 128
        ),
        name="attention_backward",
    )(slots, queries, keys, values, totals, out, grad, cos_lanes, sin_lanes)


def put_together(sources, plan, target, whole_ref, sems):
    copies = [
        pltpu.make_async_copy(
            sources[source].at[pl.ds(row, rows)], target.at[pl.ds(to, rows)], sems.at[at]
        )
        for at, (source, row, rows, to) in enumerate(plan)
    ]
    return copies, pltpu.make_async_copy(target, whole_ref, sems.at[len(plan)])


def gather_in(calls):
    for copies, _ in calls:
        for copy in copies:
            copy.start()
    for copies, out in calls:
        for copy in copies:
            copy.wait()
        out.start()


def feed_tile(feed_ref, down_in_ref, pair_ref, down_ref, activated_ref, grads_ref):
    tile = down_ref.shape[1]
    both = dot(feed_ref[...], pair_ref[...])
    grad_act = dot(down_in_ref[...], down_ref[...])
    gate, up = both[:, :tile], both[:, tile:]
    sig = jax.nn.sigmoid(gate)
    silu = gate * sig
    activated_ref[...] = (silu * up).astype(BF16)
    grads_ref[:, :tile] = (grad_act * up * (sig + silu * (1.0 - sig))).astype(BF16)
    grads_ref[:, tile:] = (grad_act * silu).astype(BF16)


def feed_kernel(*refs, plan, count):
    step = pl.program_id(0)
    feeds, downs, refs = refs[:count], refs[count : 2 * count], refs[2 * count :]
    pair_ref, down_ref, activated_ref, grads_ref, feed_out, down_out = refs[:6]
    feed_all, down_all, feed_sems, down_sems = refs[6:]
    calls = [
        put_together(feeds, plan, feed_all, feed_out, feed_sems),
        put_together(downs, plan, down_all, down_out, down_sems),
    ]

    @pl.when(step == 0)
    def _():
        gather_in(calls)

    feed_tile(feed_all, down_all, pair_ref, down_ref, activated_ref, grads_ref)

    @pl.when(step == pl.num_programs(0) - 1)
    def _():
        for _, out in calls:
            out.wait()


def feed_specs(rows, depth, width, tile):
    tiles = width // tile
    weights = [
        pl.BlockSpec((depth, 2 * tile), lambda j: (0, j)),
        pl.BlockSpec((depth, tile), lambda j: (0, 2 * tiles + j)),
    ]
    outs = [
        pl.BlockSpec((rows, tile), lambda j: (0, j)),
        pl.BlockSpec((rows, 2 * tile), lambda j: (0, j)),
    ]
    shapes = [
        jax.ShapeDtypeStruct((rows, width), BF16),
        jax.ShapeDtypeStruct((rows, 2 * width), BF16),
    ]
    work = rows * depth * width
    settings = {
        "compiler_params": pltpu.CompilerParams(
            dimension_semantics=("arbitrary",), vmem_limit_bytes=56 << 20
        ),
        "cost_estimate": pl.CostEstimate(
            flops=(6 * work) * 3,
            bytes_accessed=(2 * (2 * rows * depth + 3 * depth * width + 3 * rows * width)) * 3,
            transcendentals=rows * width,
        ),
    }
    return weights, outs, shapes, settings


def feed_first(feed, down, weights, width, tile):
    feeds, plan = pieces_of(*feed)
    downs, _ = pieces_of(*down)
    rows, depth = sum(entry[2] for entry in plan), weights.shape[0]
    weight_specs, outs, shapes, settings = feed_specs(rows, depth, width, tile)
    anywhere = pl.BlockSpec(memory_space=pl.ANY)
    whole = jax.ShapeDtypeStruct((rows, depth), BF16)
    return pl.pallas_call(
        functools.partial(feed_kernel, plan=plan, count=len(feeds)),
        grid=(width // tile,),
        in_specs=[anywhere] * (2 * len(feeds)) + weight_specs,
        out_specs=outs + [anywhere] * 2,
        out_shape=shapes + [whole] * 2,
        scratch_shapes=[
            pltpu.VMEM((rows, depth), BF16),
            pltpu.VMEM((rows, depth), BF16),
            pltpu.SemaphoreType.DMA((len(plan) + 1,)),
            pltpu.SemaphoreType.DMA((len(plan) + 1,)),
        ],
        name="feed_first",
        **settings,
    )(*feeds, *downs, weights, weights)


def feed_middle(feed_in, down_in, weights, width, tile):
    rows, depth = feed_in.shape
    weight_specs, outs, shapes, settings = feed_specs(rows, depth, width, tile)
    resident = pl.BlockSpec((rows, depth), lambda j: (0, 0), pipeline_mode=pl.Buffered(1))
    return pl.pallas_call(
        feed_tile,
        grid=(width // tile,),
        in_specs=[resident] * 2 + weight_specs,
        out_specs=outs,
        out_shape=shapes,
        name="feed_middle",
        **settings,
    )(feed_in, down_in, weights, weights)


def rows_kernel(*refs, plan, count):
    sources, (weight_ref, out_ref, whole_ref, target, sems) = refs[:count], refs[count:]
    call = put_together(sources, plan, target, whole_ref, sems)
    gather_in([call])
    out_ref[...] = dot(target[...], weight_ref[...]).astype(BF16)
    call[1].wait()


def rows_times(own, near, far, weight):
    sources, plan = pieces_of(own, near, far)
    rows, depth = sum(entry[2] for entry in plan), weight.shape[0]
    anywhere = pl.BlockSpec(memory_space=pl.ANY)
    return pl.pallas_call(
        functools.partial(rows_kernel, plan=plan, count=len(sources)),
        in_specs=[anywhere] * len(sources) + [pl.BlockSpec(memory_space=pltpu.VMEM)],
        out_specs=[pl.BlockSpec(memory_space=pltpu.VMEM), anywhere],
        out_shape=[
            jax.ShapeDtypeStruct((rows, weight.shape[1]), BF16),
            jax.ShapeDtypeStruct((rows, depth), BF16),
        ],
        scratch_shapes=[
            pltpu.VMEM((rows, depth), BF16),
            pltpu.SemaphoreType.DMA((len(plan) + 1,)),
        ],
        compiler_params=pltpu.CompilerParams(vmem_limit_bytes=48 << 20),
        cost_estimate=pl.CostEstimate(
            flops=(2 * rows * depth * weight.shape[1]) * 3,
            bytes_accessed=(2 * (2 * rows * depth + (rows + depth) * weight.shape[1])) * 3,
            transcendentals=0,
        ),
        name="rows_times",
    )(*sources, weight)


def spread_kernel(*refs, count, begun):
    total = sum(dot(refs[i][...], refs[count + i][...], NT) for i in range(count))
    if begun:
        total = total + refs[2 * count][...]
    start = 0
    for out in refs[2 * count + begun :]:
        out[...] = total[start : start + out.shape[0]].astype(out.dtype)
        start += out.shape[0]


def spread_rows(lefts, weights, places, tile, begun=None, whole=False):
    rows = lefts[0].shape[0]
    depth = weights[0].shape[0]
    widths = [left.shape[1] for left in lefts]
    work = rows * depth * sum(widths)
    outs = [rows // 2, rows // 4, rows // 4] if square() and not whole else [rows]
    begun = [] if begun is None else [begun]

    def weight_spec(width, place):
        return pl.BlockSpec((tile, width), lambda j: (j, place))

    return pl.pallas_call(
        functools.partial(spread_kernel, count=len(lefts), begun=len(begun)),
        grid=(depth // tile,),
        in_specs=[
            pl.BlockSpec((rows, width), lambda j: (0, 0), pipeline_mode=pl.Buffered(1))
            for width in widths
        ]
        + [weight_spec(width, place) for width, place in zip(widths, places)]
        + [pl.BlockSpec((rows, tile), lambda j: (0, j)) for _ in begun],
        out_specs=[pl.BlockSpec((each, tile), lambda j: (0, j)) for each in outs],
        out_shape=[jax.ShapeDtypeStruct((each, depth), F32 if whole else BF16) for each in outs],
        compiler_params=pltpu.CompilerParams(
            dimension_semantics=("arbitrary",), vmem_limit_bytes=56 << 20
        ),
        cost_estimate=pl.CostEstimate(
            flops=(2 * work) * 3,
            bytes_accessed=(2 * ((rows + depth) * sum(widths) + rows * depth)) * 3,
            transcendentals=0,
        ),
        name="spread_rows",
    )(*lefts, *weights, *begun)


def token_kernel(*refs, seqs, pair_tiles):
    feeds, downs, pairs, acts = (refs[at * seqs : (at + 1) * seqs] for at in range(4))
    column = pl.program_id(0)

    @pl.when(column < pair_tiles)
    def _():
        total = sum(dot(left[...], right[...], TN) for left, right in zip(feeds, pairs))
        refs[-1][...] = total.astype(BF16)

    @pl.when(column >= pair_tiles)
    def _():
        total = sum(dot(left[...], right[...], TN) for left, right in zip(downs, acts))
        refs[-1][...] = total.astype(BF16)


def feed_grads(feeds, downs, pairs, acts, tile):
    seqs = len(feeds)
    rows, depth = feeds[0].shape
    pair_tiles, act_tiles = pairs[0].shape[1] // tile, acts[0].shape[1] // tile
    step = min(512, depth)
    columns = (pair_tiles + act_tiles) * tile
    left_pair = pl.BlockSpec((rows, step), lambda j, i: (0, jnp.where(j < pair_tiles, i, 0)))
    left_act = pl.BlockSpec((rows, step), lambda j, i: (0, jnp.where(j < pair_tiles, 0, i)))
    pair = pl.BlockSpec((rows, tile), lambda j, i: (0, jnp.minimum(j, pair_tiles - 1)))
    act = pl.BlockSpec((rows, tile), lambda j, i: (0, jnp.maximum(j - pair_tiles, 0)))
    work = seqs * rows * depth * columns
    return pl.pallas_call(
        functools.partial(token_kernel, seqs=seqs, pair_tiles=pair_tiles),
        grid=(pair_tiles + act_tiles, depth // step),
        in_specs=[left_pair] * seqs + [left_act] * seqs + [pair] * seqs + [act] * seqs,
        out_specs=pl.BlockSpec((step, tile), lambda j, i: (i, j)),
        out_shape=jax.ShapeDtypeStruct((depth, columns), BF16),
        compiler_params=pltpu.CompilerParams(
            dimension_semantics=("arbitrary", "arbitrary"), vmem_limit_bytes=56 << 20
        ),
        cost_estimate=pl.CostEstimate(
            flops=(2 * work) * 3,
            bytes_accessed=(2 * (2 * seqs * rows * depth + (seqs * rows + depth) * columns)) * 3,
            transcendentals=0,
        ),
        name="feed_grads",
    )(*feeds, *downs, *pairs, *acts)


def two_grads_kernel(*refs, seqs):
    lefts, rights, others, more = (refs[at * seqs : (at + 1) * seqs] for at in range(4))
    gains_ref, out_ref = refs[4 * seqs :]
    width = rights[0].shape[1]
    end = width + more[0].shape[1]
    first = sum(dot(left[...], right[...], TN) for left, right in zip(lefts, rights))
    out_ref[:, :width] = first.astype(BF16)
    second = sum(dot(left[...], right[...], TN) for left, right in zip(others, more))
    out_ref[:, width:end] = second.astype(BF16)
    out_ref[:, end:] = gains_ref[...]


def two_grads(lefts, rights, others, more, gains):
    seqs = len(lefts)
    rows, depth = lefts[0].shape
    widths = [rights[0].shape[1], more[0].shape[1], gains.shape[1]]
    step = min(512, depth)
    work = seqs * rows * depth * (widths[0] + widths[1])

    def resident(array):
        return pl.BlockSpec(array.shape, lambda i: (0, 0), pipeline_mode=pl.Buffered(1))

    left = pl.BlockSpec((rows, step), lambda i: (0, i))
    return pl.pallas_call(
        functools.partial(two_grads_kernel, seqs=seqs),
        grid=(depth // step,),
        in_specs=[left] * seqs
        + [resident(array) for array in rights]
        + [left] * seqs
        + [resident(array) for array in more]
        + [pl.BlockSpec((step, widths[2]), lambda i: (i, 0))],
        out_specs=pl.BlockSpec((step, sum(widths)), lambda i: (i, 0)),
        out_shape=jax.ShapeDtypeStruct((depth, sum(widths)), BF16),
        compiler_params=pltpu.CompilerParams(
            dimension_semantics=("arbitrary",), vmem_limit_bytes=56 << 20
        ),
        cost_estimate=pl.CostEstimate(
            flops=(2 * work) * 3,
            bytes_accessed=(2 * (2 * seqs * rows * depth + (seqs * rows + depth) * sum(widths))) * 3,
            transcendentals=0,
        ),
        name="two_grads",
    )(*lefts, *rights, *others, *more, gains)


def lay_kernel(place_ref, *refs, plan, inputs):
    outs = refs[inputs:]
    for source, member, start, width, target, at in plan:
        each = outs[target].shape[1] // 4
        where = pl.ds(pl.multiple_of(place_ref[member] * each + at, LANES), width)
        outs[target][:, where] = refs[source][:, start : start + width].astype(F32)


def lay_out(received, pieces, widths):
    blocks = [block for group in received for block in group]
    rows = blocks[0].shape[0]
    plan = [
        (4 * group + member, member, start, width, target, at)
        for group, start, width, target, at in pieces
        for member in range(4)
    ]
    return pl.pallas_call(
        functools.partial(lay_kernel, plan=plan, inputs=len(blocks)),
        grid_spec=pltpu.PrefetchScalarGridSpec(
            num_scalar_prefetch=1,
            grid=(1,),
            in_specs=[pl.BlockSpec(block.shape, lambda i, p: (0, 0)) for block in blocks],
            out_specs=[pl.BlockSpec((rows, 4 * width), lambda i, p: (0, 0)) for width in widths],
        ),
        out_shape=[jax.ShapeDtypeStruct((rows, 4 * width), F32) for width in widths],
        compiler_params=pltpu.CompilerParams(vmem_limit_bytes=48 << 20),
        name="lay_out",
    )(lax.axis_index("ctx") ^ jnp.arange(4, dtype=jnp.int32), *blocks)


def norm_forward(values):
    inverse_rms = lax.rsqrt(jnp.mean(values * values, axis=-1, keepdims=True) + EPS)
    return (values * inverse_rms, inverse_rms)


def norm_backward(grad_normed, normed, inverse_rms, gain):
    grad_hat = grad_normed * gain
    grad_input = inverse_rms * (
        grad_hat - normed * jnp.mean(grad_hat * normed, axis=-1, keepdims=True)
    )
    return (grad_input, jnp.sum(grad_normed * normed, axis=0))


def rope_lanes(length):
    half = HEAD_SIZE // 2
    frequency = jnp.exp(
        jnp.arange(half, dtype=F32) * (-2.0 * math.log(THETA) / HEAD_SIZE)
    )
    angles = jnp.arange(length, dtype=jnp.int32).astype(F32)[:, None] * frequency[None, :]
    cosine, sine = jnp.cos(angles), jnp.sin(angles)
    return (
        jnp.concatenate([cosine] * 4, axis=1),
        jnp.concatenate([-sine, sine, -sine, sine], axis=1),
    )


def pad_columns(array, width):
    return jnp.pad(array, ((0, 0), (0, width - array.shape[1])))


def body(
    tokens, span_order, out_grad, first_gain, query_weight, key_matrix, value_matrix,
    merge_weight, second_gain, gate_weight, up_weight, down_weight,
):
    seqs, own_rows, depth = tokens.shape
    ctx = lax.axis_size("ctx")
    rank = lax.axis_index("ctx")
    length = own_rows * ctx
    spans = span_order.shape[1]
    weight_rows = gate_weight.shape[0]
    group_size = query_weight.shape[1] // key_matrix.shape[1]
    query_width = query_weight.shape[1] // ctx
    own_key_width = key_matrix.shape[1] // ctx
    key_width = -(-own_key_width // LANES) * LANES
    feed_width = gate_weight.shape[1] // ctx
    tile = min(512, feed_width)
    tiles = feed_width // tile
    first = max(1, 3 * tiles // 4)
    chunks = [first * tile] + ([(tiles - first) * tile] if tiles > first else [])
    starts = [0, chunks[0]][: len(chunks)]
    chain = Chain()

    def columns(weight, t, width, at=0):
        return lax.dynamic_slice_in_dim(weight, t * (weight.shape[1] // ctx) + at, width, axis=1)

    gain_columns = pad_columns(jnp.stack([first_gain, second_gain], axis=1), LANES)

    def projections_for(t):
        return jnp.concatenate(
            [
                columns(query_weight, t, query_width),
                pad_columns(columns(key_matrix, t, own_key_width), key_width),
                pad_columns(columns(value_matrix, t, own_key_width), key_width),
                gain_columns,
            ],
            axis=1,
        )

    def feed_for(part):
        def of(t):
            pieces = []
            for start in range(starts[part], starts[part] + chunks[part], tile):
                pieces += [
                    columns(gate_weight, t, tile, start),
                    columns(up_weight, t, tile, start),
                ]
            pieces.append(columns(down_weight, t, chunks[part], starts[part]))
            return jnp.concatenate(pieces, axis=1)

        return of

    assert seqs == 2 and len(chunks) <= 2
    many = len(chunks) > 1
    qkv_width = query_width + 2 * key_width

    slots = jnp.argsort(span_order, axis=1).astype(jnp.int32)
    if square():
        places = [HALVES.index((member, half)) for member in range(4) for half in range(2)]
        slots = jnp.array(places, jnp.int32)[((slots // 2) ^ rank) * 2 + slots % 2]
    cos_lanes, sin_lanes = rope_lanes(length)

    def project(own, near, far, weight, gain):
        rows = gathered(own, near, far)
        normed, _ = norm_forward(rows.astype(F32))
        attn_in = (normed * gain).astype(BF16)
        return rows, attn_in, dot(attn_in, weight)

    def attend(qkv, slots):
        return attention_forward(
            qkv, slots, cos_lanes, sin_lanes, query_width, key_width, group_size
        )

    def merge_back(rows, weight):
        return spread_rows([rows], [weight], [0], tile)

    def feed_norm(rows, branch, near, far, gain):
        hidden = rows.astype(F32) + scattered(branch, near, far)
        normed, _ = norm_forward(hidden)
        return hidden, (normed * gain).astype(BF16)

    def middle_first(feed, down, weights):
        return feed_first(feed, down, weights, chunks[0], tile)

    def middle_last(feed_in, down_in, weights):
        return feed_middle(feed_in, down_in, weights, chunks[1], tile)

    def feed_back(grads, weights, begun=None, whole=False):
        return spread_rows(grads, weights, [0] * len(grads), tile, begun, whole)

    def feed_out(activated, weights, begun=None, whole=False):
        return spread_rows(activated, weights, [2] * len(activated), tile, begun, whole)

    def feed_grads_of(feed_in, down_in, middle, part):
        return feed_grads(
            feed_in, down_in, [m[1] for m in middle], [m[0] for m in middle], chunks[part]
        )

    def feed_norm_back(hidden, parts, near, far, cot, gain):
        normed, inverse = norm_forward(hidden)
        grad_middle, gain_part = norm_backward(
            scattered(parts, near, far), normed, inverse, gain
        )
        grad_hidden = cot.astype(F32) + grad_middle
        return grad_hidden, grad_hidden.astype(BF16), gain_part

    def attend_back(own, near, far, weight, kept, out, slots):
        grad_attn, merge_in = rows_times(own, near, far, weight)
        parts = attention_backward(kept, out, grad_attn, slots, cos_lanes, sin_lanes, group_size)
        return merge_in, jnp.concatenate(parts, axis=1)

    def project_back(grads, weight):
        return spread_rows([grads], [weight], [0], tile)

    def gain_part_of(rows, lower):
        normed, _ = norm_forward(rows.astype(F32))
        total, start = 0.0, 0
        for part in lower:
            here = slice(start, start + part.shape[0])
            total = total + jnp.sum(normed[here] * part.astype(F32), axis=0)
            start += part.shape[0]
        return total

    def attention_grads_of(attn_in, grad_qkv, merge_in, attn_out, gain_one_parts, gain_two_parts):
        gains = jnp.stack([sum(gain_one_parts), sum(gain_two_parts)], axis=1)
        gains = pad_columns(gains.astype(BF16), LANES)
        return two_grads(attn_in, grad_qkv, merge_in, attn_out, gains)

    def project_norm_back(rows, parts, near, far, grad_hidden, gain):
        normed, inverse = norm_forward(rows.astype(F32))
        grad_lower, _ = norm_backward(scattered(parts, near, far), normed, inverse, gain)
        return grad_hidden + grad_lower

    def block_of(hidden, parts, near, far):
        return (hidden + scattered(parts, near, far)).astype(BF16)

    def only(*values):
        return values

    moved = chain.exchange(projections_for)
    a_near = chain.gather_near(tokens[0])
    projections = chain.all_rows(moved)
    moved = chain.exchange(lambda t: columns(merge_weight, t, query_width))
    merge = chain.all_rows(moved)
    a_far = chain.gather_far(a_near)
    moved = chain.exchange(feed_for(0))
    chain.wait(*a_far)
    b_near = chain.gather_near(tokens[1])
    gains = projections[:, qkv_width : qkv_width + 2].astype(F32)
    gain_one, gain_two = gains[:, 0], gains[:, 1]
    rows_a, attn_in_a, qkv = chain.run(
        project, tokens[0], a_near, a_far, projections[:, :qkv_width], gain_one
    )
    feeds = [chain.all_rows(moved)]
    attn_out_a, *kept_a = chain.run(attend, qkv, slots[0])
    b_far = chain.gather_far(b_near)
    branch_a = chain.run(merge_back, attn_out_a, merge)
    near_a = chain.scatter_near(branch_a)
    chain.wait(*b_far)
    rows_b, attn_in_b, qkv = chain.run(
        project, tokens[1], b_near, b_far, projections[:, :qkv_width], gain_one
    )
    far_a = chain.scatter_far(branch_a, near_a)
    cot_a_near = chain.gather_near(out_grad[0])
    attn_out_b, *kept_b = chain.run(attend, qkv, slots[1])
    chain.wait(*far_a)
    hidden_a, feed_a = chain.run(feed_norm, tokens[0], branch_a, near_a, far_a, gain_two)
    feed_a_near = chain.gather_near(feed_a)
    branch_b = chain.run(merge_back, attn_out_b, merge)
    cot_a_far = chain.gather_far(cot_a_near)
    feed_a_far = chain.gather_far(feed_a_near)
    if many:
        moved = chain.exchange(feed_for(1))
    chain.wait(*cot_a_far)
    chain.wait(*feed_a_far)
    near_b = chain.scatter_near(branch_b)
    if many:
        feeds.append(chain.all_rows(moved))
    cot_b_near = chain.gather_near(out_grad[1])
    *first, feed_in_a, down_in_a = chain.run(
        middle_first,
        (feed_a, feed_a_near, feed_a_far), (out_grad[0], cot_a_near, cot_a_far), feeds[0],
    )
    middle_a = [first]
    far_b = chain.scatter_far(branch_b, near_b)
    cot_b_far = chain.gather_far(cot_b_near)
    begun_back = None
    if many:
        (begun_back,) = chain.run(
            lambda m, w: feed_back([m], [w], None, True), middle_a[0][1], feeds[0]
        )
    chain.wait(*far_b)
    hidden_b, feed_b = chain.run(feed_norm, tokens[1], branch_b, near_b, far_b, gain_two)
    feed_b_near = chain.gather_near(feed_b)
    if many:
        middle_a.append(chain.run(middle_last, feed_in_a, down_in_a, feeds[1]))
    feed_b_far = chain.gather_far(feed_b_near)
    ends_a = slice(1 if many else 0, None)
    back_a = chain.run(feed_back, [m[1] for m in middle_a[ends_a]], feeds[ends_a], begun_back)
    near_a = chain.scatter_near(back_a)
    chain.wait(*cot_b_far)
    chain.wait(*feed_b_far)
    *first, feed_in_b, down_in_b = chain.run(
        middle_first,
        (feed_b, feed_b_near, feed_b_far), (out_grad[1], cot_b_near, cot_b_far), feeds[0],
    )
    middle_b = [first]
    far_a = chain.scatter_far(back_a, near_a)
    grads_first = chain.run(
        lambda f, d, m: feed_grads_of(f, d, m, 0),
        [feed_in_a, feed_in_b], [down_in_a, down_in_b], [middle_a[0], middle_b[0]],
    )
    chain.wait(*far_a)
    sums = [sum_over_dp(*chain.run(only, grads_first))]
    grad_hidden_a, merge_a, gain_two_a = chain.run(
        feed_norm_back, hidden_a, back_a, near_a, far_a, out_grad[0], gain_two
    )
    merge_a_near = chain.gather_near(merge_a)
    if many:
        middle_b.append(chain.run(middle_last, feed_in_b, down_in_b, feeds[1]))
    merge_a_far = chain.gather_far(merge_a_near)
    back_b = chain.run(feed_back, [m[1] for m in middle_b], feeds)
    near_b = chain.scatter_near(back_b)
    chain.wait(*merge_a_far)
    merge_in_a, grad_qkv_a = chain.run(
        attend_back, merge_a, merge_a_near, merge_a_far, merge, kept_a, attn_out_a, slots[0]
    )
    far_b = chain.scatter_far(back_b, near_b)
    lower_a = chain.run(project_back, grad_qkv_a, projections)
    lower_a_near = chain.scatter_near(lower_a)
    out_a = chain.run(feed_out, [m[0] for m in middle_a], feeds)
    chain.wait(*far_b)
    grad_hidden_b, merge_b, gain_two_b = chain.run(
        feed_norm_back, hidden_b, back_b, near_b, far_b, out_grad[1], gain_two
    )
    merge_b_near = chain.gather_near(merge_b)
    lower_a_far = chain.scatter_far(lower_a, lower_a_near)
    if many:
        grads_last = chain.run(
            lambda f, d, m: feed_grads_of(f, d, m, 1),
            [feed_in_a, feed_in_b], [down_in_a, down_in_b], [middle_a[1], middle_b[1]],
        )
    merge_b_far = chain.gather_far(merge_b_near)
    chain.wait(*lower_a_far)
    input_grad_a = chain.run(
        project_norm_back, tokens[0], lower_a, lower_a_near, lower_a_far, grad_hidden_a, gain_one
    )
    chain.wait(*merge_b_far)
    out_a_near = chain.scatter_near(out_a)
    gain_one_a = chain.run(gain_part_of, rows_a, lower_a)
    chain.wait(*out_a_near)
    chain.wait(sums[0])
    if many:
        sums.append(sum_over_dp(*chain.run(only, grads_last)))
    out_a_far = chain.scatter_far(out_a, out_a_near)
    moved_feed = [chain.own_rows(sums[0])]
    merge_in_b, grad_qkv_b = chain.run(
        attend_back, merge_b, merge_b_near, merge_b_far, merge, kept_b, attn_out_b, slots[1]
    )
    lower_b = chain.run(project_back, grad_qkv_b, projections)
    chain.wait(*out_a_far)
    lower_b_near = chain.scatter_near(lower_b)
    chain.wait(*moved_feed[0][1:])
    gain_one_b = chain.run(gain_part_of, rows_b, lower_b)
    attention_grads = chain.run(
        attention_grads_of,
        [attn_in_a, attn_in_b],
        [grad_qkv_a, grad_qkv_b],
        [merge_in_a, merge_in_b],
        [attn_out_a, attn_out_b],
        [gain_one_a, gain_one_b],
        [gain_two_a, gain_two_b],
    )
    chain.wait(*lower_b_near)
    chain.wait(sums[-1])
    attention_sums = sum_over_dp(*chain.run(only, attention_grads))
    lower_b_far = chain.scatter_far(lower_b, lower_b_near)
    out_b = chain.run(feed_out, [m[0] for m in middle_b], feeds)
    out_b_near = chain.scatter_near(out_b)
    chain.wait(*lower_b_far)
    input_grad_b = chain.run(
        project_norm_back, tokens[1], lower_b, lower_b_near, lower_b_far, grad_hidden_b, gain_one
    )
    moved_feed += [chain.own_rows(part) for part in sums[1:]]
    out_b_far = chain.scatter_far(out_b, out_b_near)
    block_a = chain.run(block_of, hidden_a, out_a, out_a_near, out_a_far)
    chain.wait(*moved_feed[-1][1:])
    chain.wait(*out_b_far)
    block_b = chain.run(block_of, hidden_b, out_b, out_b_near, out_b_far)
    blocks = [block_a, block_b]
    input_grad = [input_grad_a, input_grad_b]

    key_at, value_at = query_width, query_width + key_width
    merge_at, gain_at = qkv_width, qkv_width + query_width
    feed_pieces = [
        (part, 2 * width + at * tile if kind == 2 else (2 * at + kind) * tile, tile, kind,
         starts[part] + at * tile)
        for part, width in enumerate(chunks)
        for at in range(width // tile)
        for kind in range(3)
    ]
    attention_pieces = [
        (0, 0, query_width, 0, 0),
        (0, key_at, own_key_width, 1, 0),
        (0, value_at, own_key_width, 2, 0),
        (0, merge_at, query_width, 3, 0),
    ]

    def results(received, pieces, widths):
        if square():
            return lay_out(received, pieces, widths)
        columns_of = [[] for _ in widths]
        for group, start, width, target, at in sorted(pieces, key=lambda piece: piece[4]):
            columns_of[target].append(received[group][0][:, :, start : start + width])
        return [
            jnp.concatenate(parts, axis=2)
            .astype(F32)
            .transpose(1, 0, 2)
            .reshape(weight_rows, -1)
            for parts in columns_of
        ]

    gate_total, up_total, down_total = chain.run(
        lambda *received: results(received, feed_pieces, [feed_width] * 3),
        *moved_feed,
    )
    moved = chain.own_rows(attention_sums)
    chain.wait(*moved[1:])
    query_total, key_total, value_total, merge_total = chain.run(
        lambda received: results(
            [received], attention_pieces, [query_width, own_key_width, own_key_width, query_width]
        ),
        moved,
    )
    gain_totals = sum(block[..., gain_at : gain_at + 2].astype(F32) for block in moved)
    if not square():
        gain_totals = jnp.sum(gain_totals, axis=0)
    return (
        jnp.stack(blocks),
        jnp.stack(input_grad),
        gain_totals[:, 0],
        query_total,
        key_total,
        value_total,
        merge_total,
        gain_totals[:, 1],
        gate_total,
        up_total,
        down_total,
    )


def solution(mesh):
    rows = P(("dp", "ctx"), None)
    vector = P(("dp", "ctx"))
    acts = P("dp", "ctx", None)
    in_specs = (
        acts, P("dp", None), acts, vector, rows, rows, rows, rows, vector, rows, rows, rows,
    )
    out_specs = (acts, acts, vector, rows, rows, rows, rows, vector, rows, rows, rows)
    return jax.shard_map(body, mesh=mesh, in_specs=in_specs, out_specs=out_specs, check_vma=False)
```
